32 devices in a mesh: region: 4 (over z), pos: 8 (over y, x, core).
Axes of the slice: x: 2, y: 2, z: 4, core: 2. Of those that a mesh axis runs over, the one named last changes fastest.
Arguments:
- object_tiles: bfloat16 [2, 512, 1024], P(None, 'region', 'pos'), may hold values from -4.1875 to 4.1875
- probe: float32 [2, 4, 128, 128], replicated, may hold values from -3 to 3
- amplitudes: float32 [4, 32, 128, 128], P('region', 'pos'), may hold values from 0.3 to 6
- offsets: int32 [4, 2, 32], P('region', None, 'pos'), may hold values from 0 to 127
- counts: int32 [4, 8], P('region', 'pos'), may hold values from 1 to 4
Outputs:
- object_grad: float32 [2, 512, 1024], P(None, 'region', 'pos')
- probe_grad: float32 [2, 4, 128, 128], replicated
The draws below stay inside these ranges and needn't reach their ends.
All inputs are finite; a program needn't handle non-finite values.
Results may differ from the reference program's by a relative error of at most 0.0003.
Values may be sent and summed in bfloat16 or wider, within the bound.
No kernel may reach another device: no remote copies, remote signals or barrier semaphores. Data moves between devices by JAX's collectives and lax.ppermute only.
A program may use at most 64 MiB of HBM per device.

```python
import math
import jax
import jax.numpy as jnp
from jax import lax

DETECTOR_PIXELS = 128
MODES = 4
P_CAP = 4
OROWS = 512
OCOLS = 1024
STRIP_SLOTS = 32
N_REGION = 4
N_POS = 8


def set_ends(values, own_key, smallest, top_value):
    place = [jax.random.randint(jax.random.fold_in(own_key, axis), (), 0, length) for axis, length in enumerate(values.shape)]
    main_axis = values.shape.index(max(values.shape))
    next_to = place[:main_axis] + [(place[main_axis] + 1) % values.shape[main_axis]] + place[main_axis + 1:]
    return values.at[tuple(place)].set(smallest).at[tuple(next_to)].set(top_value)


def level_of(rng, dims, split, smallest, high):
    factor_of = 1.0
    for dim, shards_of in split:
        draws = jax.random.uniform(jax.random.fold_in(jax.random.fold_in(rng, 6), dim), (shards_of,), jnp.float32, smallest / len(split), high / len(split))
        factor_of = factor_of * jnp.repeat(jnp.exp(draws), dims[dim] // shards_of).reshape((-1,) + (1,) * (len(dims) - 1 - dim))
    return factor_of


def bell_draw(stream_key, shape, deviation, reach, pieces=(), kind=jnp.bfloat16):
    loudness = level_of(stream_key, shape, pieces, -0.22, 0.18) if pieces else 1.0
    entries = jax.random.normal(stream_key, shape, jnp.float32) * deviation * loudness
    return jnp.minimum(jnp.maximum(entries, -reach), reach).astype(kind)


def setup_inputs(seed: int = 0) -> dict:
    key_list = jax.random.split(jax.random.key(seed), 6)
    return {
        "object_tiles": bell_draw(key_list[0], (2, OROWS, OCOLS), 0.7, 4.1875, ((1, 4), (2, 8))),
        "probe": bell_draw(key_list[1], (2, MODES, DETECTOR_PIXELS, DETECTOR_PIXELS), 0.5, 3.0, (), jnp.float32),
        "amplitudes": jnp.clip(jnp.exp(math.log(6.0) - 2.9957322 * jax.random.uniform(key_list[2], (N_REGION, STRIP_SLOTS, DETECTOR_PIXELS, DETECTOR_PIXELS), jnp.float32) ** level_of(key_list[2], (N_REGION, STRIP_SLOTS, DETECTOR_PIXELS, DETECTOR_PIXELS), ((0, 4), (1, 8)), -0.2, 0.2)), 0.3, 6.0),
        "offsets": set_ends(jax.random.randint(key_list[3], (N_REGION, 2, STRIP_SLOTS), 0, DETECTOR_PIXELS), jax.random.fold_in(key_list[3], 1), 0, DETECTOR_PIXELS - 1).astype(jnp.int32),
        "counts": set_ends(jax.random.randint(key_list[4], (N_REGION, N_POS), 1, P_CAP + 1), jax.random.fold_in(key_list[4], 1), 1, P_CAP).astype(jnp.int32),
    }


def dft_tables(order):
    row_index_list = jnp.arange(order, dtype=jnp.int32)
    product = row_index_list[:, None] * row_index_list[None, :] % order
    angle = product.astype(jnp.float32) * (2.0 * math.pi / order)
    norm_factor = 1.0 / math.sqrt(order)
    return (jnp.cos(angle) * norm_factor, jnp.sin(angle) * norm_factor)

def both_sides(real_part, imag_part, cos_table, sin_table):
    high = lax.Precision.HIGHEST
    left_r = jnp.einsum('ab,mbc->mac', cos_table, real_part, precision=high) - jnp.einsum('ab,mbc->mac', sin_table, imag_part, precision=high)
    left_i = jnp.einsum('ab,mbc->mac', cos_table, imag_part, precision=high) + jnp.einsum('ab,mbc->mac', sin_table, real_part, precision=high)
    right_r = jnp.einsum('mab,bc->mac', left_r, cos_table, precision=high) - jnp.einsum('mab,bc->mac', left_i, sin_table, precision=high)
    right_i = jnp.einsum('mab,bc->mac', left_i, cos_table, precision=high) + jnp.einsum('mab,bc->mac', left_r, sin_table, precision=high)
    return (right_r, right_i)

def position_terms(obj_patch, probe, amplitude, cos_table, sin_table):
    exit_r = probe[0] * obj_patch[0][None] - probe[1] * obj_patch[1][None]
    exit_i = probe[0] * obj_patch[1][None] + probe[1] * obj_patch[0][None]
    far_r, far_i = both_sides(exit_r, exit_i, cos_table, -sin_table)
    intensity = lax.optimization_barrier(jnp.sum(far_r * far_r + far_i * far_i, axis=0))
    factor = 1.0 - amplitude / jnp.sqrt(intensity + 1.0)
    back_r, back_i = both_sides(far_r * factor[None], far_i * factor[None], cos_table, sin_table)
    obj_r = lax.optimization_barrier(jnp.sum(probe[0] * back_r + probe[1] * back_i, axis=0))
    obj_i = lax.optimization_barrier(jnp.sum(probe[0] * back_i - probe[1] * back_r, axis=0))
    probe_r = obj_patch[0][None] * back_r + obj_patch[1][None] * back_i
    probe_i = obj_patch[0][None] * back_i - obj_patch[1][None] * back_r
    return (jnp.stack([obj_r, obj_i]), jnp.stack([probe_r, probe_i]))

def reference(object_tiles, probe, amplitudes, offsets, counts):
    cos_table, sin_table = dft_tables(DETECTOR_PIXELS)
    field = jnp.pad(object_tiles.astype(jnp.float32), ((0, 0), (0, DETECTOR_PIXELS), (0, DETECTOR_PIXELS)))
    slot_ids = jnp.arange(N_POS * P_CAP, dtype=jnp.int32)
    region_ids = jnp.arange(N_REGION, dtype=jnp.int32)
    tile_cols = (slot_ids // P_CAP).astype(jnp.int32)
    row_start = (offsets[:, 0, :] + region_ids[:, None] * DETECTOR_PIXELS).astype(jnp.int32).reshape(-1)
    column_begin = (offsets[:, 1, :] + tile_cols[None, :] * DETECTOR_PIXELS).astype(jnp.int32).reshape(-1)
    live_flag = ((slot_ids % P_CAP)[None, :] < counts[:, tile_cols]).astype(jnp.float32).reshape(-1)
    flat_amp = amplitudes.reshape(-1, DETECTOR_PIXELS, DETECTOR_PIXELS)
    zero_index = jnp.zeros((), jnp.int32)

    def visit(carry, item):
        grad_field, probe_sum = carry
        row0, col0, amplitude, weight = item
        obj_patch = lax.dynamic_slice(field, (zero_index, row0, col0), (2, DETECTOR_PIXELS, DETECTOR_PIXELS))
        obj_term, probe_term = position_terms(obj_patch, probe, amplitude, cos_table, sin_table)
        current = lax.dynamic_slice(grad_field, (zero_index, row0, col0), (2, DETECTOR_PIXELS, DETECTOR_PIXELS))
        grad_field = lax.dynamic_update_slice(grad_field, current + weight * obj_term, (zero_index, row0, col0))
        return ((grad_field, probe_sum + weight * probe_term), None)
    start = (jnp.zeros(field.shape, jnp.float32), jnp.zeros(probe.shape, jnp.float32))
    (grad_field, probe_sum), ignored_value = lax.scan(visit, start, (row_start, column_begin, flat_amp, live_flag))
    scale = 1.0 / math.sqrt(N_REGION * N_POS * P_CAP)
    return (grad_field[:, :OROWS, :OCOLS], probe_sum * scale)
```

```python
import functools
import math

import jax
import jax.numpy as jnp
import ml_dtypes
import numpy as np
from jax import lax
from jax.experimental import pallas as pl
from jax.experimental.pallas import tpu as pltpu
from jax.sharding import PartitionSpec as P


def split_table(table):
    high = table.astype(ml_dtypes.bfloat16)
    low = (table - high.astype(np.float64)).astype(ml_dtypes.bfloat16)
    return high, low


def dft_tables(order):
    index = np.arange(order)
    angle = (index[:, None] * index[None, :] % order) * (2.0 * math.pi / order)
    cos_table = np.cos(angle) / math.sqrt(order)
    sin_table = np.sin(angle) / math.sqrt(order)
    spread = np.block([[cos_table, -sin_table], [sin_table, cos_table]])
    return split_table(spread) + split_table(spread.T)


def split(value):
    high = value.astype(jnp.bfloat16)
    low = (value - high.astype(jnp.float32)).astype(jnp.bfloat16)
    return high, low


def dot(a, b):
    return jnp.dot(a, b, preferred_element_type=jnp.float32)


def times_table(value, table_high, table_low):
    high, low = split(value)
    return dot(high, table_high) + (dot(low, table_high) + dot(high, table_low))


def table_times(table_high, table_low, value):
    high, low = split(value)
    return dot(table_high, high) + (dot(table_high, low) + dot(table_low, high))


def slots_kernel(
    chunks, scale, offsets, counts, rank, own, below, right, diag, probe, amplitudes,
    spread_high, spread_low, turn_high, turn_low,
    own_grad, below_grad, right_grad, diag_grad, keep, send,
    field_left, field_right, grad_left, grad_right, probe_sum,
):
    modes, edge = probe.shape[1], probe.shape[2]
    slot_total = amplitudes.shape[1]
    field_left[:, :edge] = own[...].astype(jnp.float32)
    field_left[:, edge:] = below[...].astype(jnp.float32)
    field_right[:, :edge] = right[...].astype(jnp.float32)
    field_right[:, edge:] = diag[...].astype(jnp.float32)
    grad_left[...] = jnp.zeros_like(grad_left)
    grad_right[...] = jnp.zeros_like(grad_right)
    lane = lax.broadcasted_iota(jnp.int32, (edge, edge), 1)
    for slot in range(slot_total):
        row0 = offsets[0, 0, slot]
        col0 = offsets[0, 1, slot]
        rows = pl.ds(row0, edge)
        in_left = lane >= col0
        weight = (slot < counts[0, 0]).astype(jnp.float32)
        back_shift = lax.rem(edge - col0, edge)
        crop_r, crop_i = (
            pltpu.roll(
                jnp.where(in_left, field_left[part, rows, :], field_right[part, rows, :]), back_shift, 1
            )
            for part in range(2)
        )
        exits = jnp.concatenate(
            [
                jnp.concatenate(
                    [
                        probe[0, m] * crop_r - probe[1, m] * crop_i,
                        probe[0, m] * crop_i + probe[1, m] * crop_r,
                    ],
                    axis=1,
                )
                for m in range(modes)
            ],
            axis=0,
        )
        half = times_table(exits, spread_high[...], spread_low[...])
        half = jnp.concatenate(
            [
                jnp.concatenate(
                    [half[m * edge : (m + 1) * edge, part * edge : (part + 1) * edge] for m in range(modes)],
                    axis=1,
                )
                for part in range(2)
            ],
            axis=0,
        )
        far = table_times(turn_high[...], turn_low[...], half)
        squares = far * far
        squares = squares[:edge] + squares[edge:]
        intensity = functools.reduce(
            jnp.add, [squares[:, m * edge : (m + 1) * edge] for m in range(modes)]
        )
        factor = weight * (1.0 - amplitudes[0, slot] * lax.rsqrt(intensity + 1.0))
        factor = jnp.concatenate([factor] * modes, axis=1)
        residual = far * jnp.concatenate([factor, factor], axis=0)
        half = table_times(spread_high[...], spread_low[...], residual)
        half = jnp.concatenate(
            [
                jnp.concatenate(
                    [half[part * edge : (part + 1) * edge, m * edge : (m + 1) * edge] for part in range(2)],
                    axis=1,
                )
                for m in range(modes)
            ],
            axis=0,
        )
        back = times_table(half, turn_high[...], turn_low[...])
        object_r = jnp.zeros((edge, edge), jnp.float32)
        object_i = jnp.zeros((edge, edge), jnp.float32)
        for m in range(modes):
            back_r = back[m * edge : (m + 1) * edge, :edge]
            back_i = back[m * edge : (m + 1) * edge, edge:]
            object_r += probe[0, m] * back_r + probe[1, m] * back_i
            object_i += probe[0, m] * back_i - probe[1, m] * back_r
            term_r = crop_r * back_r + crop_i * back_i
            term_i = crop_r * back_i - crop_i * back_r
            if slot == 0:
                probe_sum[0, m] = term_r
                probe_sum[1, m] = term_i
            else:
                probe_sum[0, m] += term_r
                probe_sum[1, m] += term_i
        for part, term in enumerate((object_r, object_i)):
            term = pltpu.roll(term, col0, 1)
            grad_left[part, rows, :] += jnp.where(in_left, term, 0.0)
            grad_right[part, rows, :] += jnp.where(in_left, 0.0, term)
    own_grad[...] = grad_left[:, :edge]
    below_grad[...] = grad_left[:, edge:]
    right_grad[...] = grad_right[:, :edge]
    diag_grad[...] = grad_right[:, edge:]
    flat = probe_sum.reshape(2 * modes * edge, edge)
    depth = flat.shape[0] // chunks
    for position in range(chunks):
        chunk = jnp.bitwise_xor(rank[0], position)
        target, place = (keep, position) if position < chunks // 2 else (send, position - chunks // 2)
        start = chunk * depth
        if depth % 8 == 0:
            start = pl.multiple_of(start, depth)
        target[pl.ds(place * depth, depth), :] = flat[pl.ds(start, depth), :] * scale


def unpermute_kernel(rank, *refs):
    pieces, out = refs[:-1], refs[-1]
    depth = pieces[0].shape[0]
    position = 0
    for piece in pieces:
        for index in range(piece.shape[0] // depth):
            start = jnp.bitwise_xor(rank[0], position) * depth
            if depth % 8 == 0:
                start = pl.multiple_of(start, depth)
            out[pl.ds(start, depth), :] = piece[pl.ds(index * depth, depth), :]
            position += 1


def on_device(object_tiles, probe, amplitudes, offsets, counts):
    modes, edge = probe.shape[1], probe.shape[2]
    slot_total = amplitudes.shape[1]
    n_region, n_pos = lax.axis_size("region"), lax.axis_size("pos")
    total = n_region * n_pos
    axes = ("region", "pos")
    f32 = jnp.float32

    def shifted(block, down, across):
        route = []
        for i in range(n_region):
            for j in range(n_pos):
                a, b = i + down, j + across
                if 0 <= a < n_region and 0 <= b < n_pos:
                    route.append((i * n_pos + j, a * n_pos + b))
        return lax.ppermute(block, axes, route)

    def exchanged(block, mask):
        return lax.ppermute(block, axes, [(i, i ^ mask) for i in range(total)])

    pos_bits = [1 << k for k in range(n_pos.bit_length() - 1)]
    region_bits = [n_pos << k for k in range(n_region.bit_length() - 1)]
    masks = pos_bits + region_bits
    me = lax.axis_index("region") * n_pos + lax.axis_index("pos")
    rank = jnp.zeros((), jnp.int32)
    for k, mask in enumerate(masks):
        bit = (me & mask) // mask
        rank = rank + bit * (total >> (k + 1))
    rank = rank.reshape(1).astype(jnp.int32)

    below = shifted(object_tiles, -1, 0)
    right = shifted(object_tiles, 0, -1)
    diag = shifted(object_tiles, -1, -1)

    lines = 2 * modes * edge
    smem = pl.BlockSpec(memory_space=pltpu.SMEM)
    vmem = pl.BlockSpec(memory_space=pltpu.VMEM)
    quadrant = jax.ShapeDtypeStruct((2, edge, edge), f32)
    part = jax.ShapeDtypeStruct((lines // 2, edge), f32)
    scale = 1.0 / math.sqrt(total * slot_total)
    own_grad, below_grad, right_grad, diag_grad, keep, send = pl.pallas_call(
        functools.partial(slots_kernel, total, scale),
        out_shape=(quadrant,) * 4 + (part, part),
        in_specs=[smem] * 3 + [vmem] * 10,
        out_specs=(vmem,) * 6,
        scratch_shapes=[pltpu.VMEM((2, 2 * edge, edge), f32)] * 4
        + [pltpu.VMEM((2, modes, edge, edge), f32)],
        compiler_params=pltpu.CompilerParams(vmem_limit_bytes=40 * 1024 * 1024),
    )(
        offsets, counts, rank, object_tiles, below, right, diag, probe, amplitudes,
        *(jnp.asarray(table) for table in dft_tables(edge)),
    )

    object_grad = (
        own_grad
        + shifted(below_grad, 1, 0)
        + shifted(right_grad, 0, 1)
        + shifted(diag_grad, 1, 1)
    )
    for k, mask in enumerate(masks):
        keep = keep + exchanged(send, mask)
        if k < len(masks) - 1:
            middle = keep.shape[0] // 2
            keep, send = keep[:middle], keep[middle:]
    pieces = [keep]
    for mask in reversed(masks):
        held = jnp.concatenate(pieces, axis=0) if len(pieces) > 1 else pieces[0]
        pieces.append(exchanged(held, mask))
    probe_grad = pl.pallas_call(
        unpermute_kernel,
        out_shape=jax.ShapeDtypeStruct((lines, edge), f32),
        in_specs=[smem] + [vmem] * len(pieces),
        out_specs=vmem,
    )(rank, *pieces)
    return (object_grad, probe_grad.reshape(probe.shape))


def solution(mesh):
    return jax.shard_map(
        on_device,
        mesh=mesh,
        in_specs=(
            P(None, "region", "pos"),
            P(),
            P("region", "pos", None, None),
            P("region", None, "pos"),
            P("region", "pos"),
        ),
        out_specs=(P(None, "region", "pos"), P()),
        check_vma=False,
    )
```

```python
import functools
import math

import jax
import jax.numpy as jnp
import ml_dtypes
import numpy as np
from jax import lax
from jax.experimental import pallas as pl
from jax.experimental.pallas import tpu as pltpu
from jax.sharding import PartitionSpec as P


def split_table(table):
    high = table.astype(ml_dtypes.bfloat16)
    low = (table - high.astype(np.float64)).astype(ml_dtypes.bfloat16)
    return high, low


def dft_tables(order):
    index = np.arange(order)
    angle = (index[:, None] * index[None, :] % order) * (2.0 * math.pi / order)
    cos_table = np.cos(angle) / math.sqrt(order)
    sin_table = np.sin(angle) / math.sqrt(order)
    spread = np.block([[cos_table, -sin_table], [sin_table, cos_table]])
    return np.stack(split_table(spread) + split_table(spread.T))


def split(value):
    high = value.astype(jnp.bfloat16)
    low = (value - high.astype(jnp.float32)).astype(jnp.bfloat16)
    return high, low


def dot(a, b):
    return jnp.dot(a, b, preferred_element_type=jnp.float32)


def times_table(value, table_high, table_low):
    high, low = split(value)
    return dot(high, table_high) + (dot(low, table_high) + dot(high, table_low))


def table_times(table_high, table_low, value):
    high, low = split(value)
    return dot(table_high, high) + (dot(table_high, low) + dot(table_low, high))


def load_kernel(*refs):
    count = (len(refs) - 1) // 2
    sources, targets, semaphores = refs[:count], refs[count : 2 * count], refs[-1]
    copies = [
        pltpu.make_async_copy(source, target, semaphores.at[index])
        for index, (source, target) in enumerate(zip(sources, targets))
    ]
    for copy in copies:
        copy.start()
    for copy in copies:
        copy.wait()


def slots_kernel(
    chunks, scale, offsets, counts, place, own, below, right, diag, probe, amplitudes, tables,
    own_grad, below_grad, right_grad, diag_grad, keep, send,
    field_left, field_right, grad_left, grad_right, probe_sum,
):
    spread_high, spread_low, turn_high, turn_low = (tables.at[k] for k in range(4))
    has_below, has_right = place[2] > 0, place[3] > 0
    has_diag = jnp.logical_and(has_below, has_right)

    def present(flag, value):
        return jnp.where(flag, value, jnp.zeros_like(value))

    modes, edge = probe.shape[1], probe.shape[2]
    slot_total = amplitudes.shape[1]
    field_left[:, :edge] = own[...].astype(jnp.float32)
    field_left[:, edge:] = present(has_below, below[...].astype(jnp.float32))
    field_right[:, :edge] = present(has_right, right[...].astype(jnp.float32))
    field_right[:, edge:] = present(has_diag, diag[...].astype(jnp.float32))
    grad_left[...] = jnp.zeros_like(grad_left)
    grad_right[...] = jnp.zeros_like(grad_right)
    lane = lax.broadcasted_iota(jnp.int32, (edge, edge), 1)
    for slot in range(slot_total):
        row0 = offsets[0, 0, slot]
        col0 = offsets[0, 1, slot]
        rows = pl.ds(row0, edge)
        in_left = lane >= col0
        weight = (slot < counts[0, 0]).astype(jnp.float32)
        back_shift = lax.rem(edge - col0, edge)
        crop_r, crop_i = (
            pltpu.roll(
                jnp.where(in_left, field_left[part, rows, :], field_right[part, rows, :]), back_shift, 1
            )
            for part in range(2)
        )
        exits = jnp.concatenate(
            [
                jnp.concatenate(
                    [
                        probe[0, m] * crop_r - probe[1, m] * crop_i,
                        probe[0, m] * crop_i + probe[1, m] * crop_r,
                    ],
                    axis=1,
                )
                for m in range(modes)
            ],
            axis=0,
        )
        half = times_table(exits, spread_high[...], spread_low[...])
        half = jnp.concatenate(
            [
                jnp.concatenate(
                    [half[m * edge : (m + 1) * edge, part * edge : (part + 1) * edge] for m in range(modes)],
                    axis=1,
                )
                for part in range(2)
            ],
            axis=0,
        )
        far = table_times(turn_high[...], turn_low[...], half)
        squares = far * far
        squares = squares[:edge] + squares[edge:]
        intensity = functools.reduce(
            jnp.add, [squares[:, m * edge : (m + 1) * edge] for m in range(modes)]
        )
        factor = weight * (1.0 - amplitudes[0, slot] * lax.rsqrt(intensity + 1.0))
        factor = jnp.concatenate([factor] * modes, axis=1)
        residual = far * jnp.concatenate([factor, factor], axis=0)
        half = table_times(spread_high[...], spread_low[...], residual)
        half = jnp.concatenate(
            [
                jnp.concatenate(
                    [half[part * edge : (part + 1) * edge, m * edge : (m + 1) * edge] for part in range(2)],
                    axis=1,
                )
                for m in range(modes)
            ],
            axis=0,
        )
        back = times_table(half, turn_high[...], turn_low[...])
        object_r = jnp.zeros((edge, edge), jnp.float32)
        object_i = jnp.zeros((edge, edge), jnp.float32)
        for m in range(modes):
            back_r = back[m * edge : (m + 1) * edge, :edge]
            back_i = back[m * edge : (m + 1) * edge, edge:]
            object_r += probe[0, m] * back_r + probe[1, m] * back_i
            object_i += probe[0, m] * back_i - probe[1, m] * back_r
            term_r = crop_r * back_r + crop_i * back_i
            term_i = crop_r * back_i - crop_i * back_r
            if slot == 0:
                probe_sum[0, m] = term_r
                probe_sum[1, m] = term_i
            else:
                probe_sum[0, m] += term_r
                probe_sum[1, m] += term_i
        for part, term in enumerate((object_r, object_i)):
            term = pltpu.roll(term, col0, 1)
            grad_left[part, rows, :] += jnp.where(in_left, term, 0.0)
            grad_right[part, rows, :] += jnp.where(in_left, 0.0, term)
    own_grad[...] = grad_left[:, :edge]
    below_grad[...] = present(has_below, grad_left[:, edge:])
    right_grad[...] = present(has_right, grad_right[:, :edge])
    diag_grad[...] = present(has_diag, grad_right[:, edge:])
    flat = probe_sum.reshape(2 * modes * edge, edge)
    depth = flat.shape[0] // chunks
    for target, owner in ((keep, place[0]), (send, place[1])):
        for row in range(chunks // 2):
            start = pl.multiple_of(jnp.bitwise_xor(owner, row) * depth, depth)
            target[pl.ds(row * depth, depth), :] = flat[pl.ds(start, depth), :] * scale


def on_device(object_tiles, probe, amplitudes, offsets, counts):
    modes, edge = probe.shape[1], probe.shape[2]
    slot_total = amplitudes.shape[1]
    n_region, n_pos = lax.axis_size("region"), lax.axis_size("pos")
    total = n_region * n_pos
    axes = ("region", "pos")
    f32 = jnp.float32

    row_index, column_index = lax.axis_index("region"), lax.axis_index("pos")

    def shifted(block, down, across):
        route = [
            (i * n_pos + j, (i + down) % n_region * n_pos + (j + across) % n_pos)
            for i in range(n_region)
            for j in range(n_pos)
        ]
        return lax.ppermute(block, axes, route)

    def after(first, second):
        return lax.optimization_barrier((first, second))

    bits = [1 << k for k in range(n_pos.bit_length() - 1)]
    other = list(bits)
    if len(bits) > 2:
        other[1], other[2] = bits[2], bits[1]
    steps = len(bits)

    def exchanged(block, step):
        route = [(i, i ^ (other if i % 2 else bits)[step]) for i in range(total)]
        return lax.ppermute(block, axes, route)

    def summed(block, k):
        return block + lax.ppermute(block, axes, [(i, i ^ (n_pos << k)) for i in range(total)])

    def bit_of(step, flip=0):
        index = column_index ^ flip
        return jnp.where(index % 2 == 1, (index & other[step]) != 0, (index & bits[step]) != 0)

    def rank_of(flip):
        return sum(bit_of(step, flip).astype(jnp.int32) << (steps - 1 - step) for step in range(steps))

    place = jnp.stack(
        [
            rank_of(0),
            rank_of(1),
            (row_index < n_region - 1).astype(jnp.int32),
            (column_index < n_pos - 1).astype(jnp.int32),
        ]
    )

    below = shifted(object_tiles, -1, 0)
    right = shifted(object_tiles, 0, -1)
    diag = shifted(object_tiles, -1, -1)

    lines = 2 * modes * edge
    smem = pl.BlockSpec(memory_space=pltpu.SMEM)
    vmem = pl.BlockSpec(memory_space=pltpu.VMEM)
    held = (object_tiles, probe, amplitudes, jnp.asarray(dft_tables(edge)))
    held = pl.pallas_call(
        load_kernel,
        out_shape=tuple(jax.ShapeDtypeStruct(array.shape, array.dtype) for array in held),
        in_specs=[pl.BlockSpec(memory_space=pl.ANY)] * len(held),
        out_specs=(vmem,) * len(held),
        scratch_shapes=[pltpu.SemaphoreType.DMA((len(held),))],
        cost_estimate=pl.CostEstimate(flops=0, bytes_accessed=4 << 20, transcendentals=0),
    )(*held)
    quadrant = jax.ShapeDtypeStruct((2, edge, edge), f32)
    part = jax.ShapeDtypeStruct((lines // 2, edge), f32)
    scale = 1.0 / math.sqrt(total * slot_total)
    own_grad, below_grad, right_grad, diag_grad, keep, send = pl.pallas_call(
        functools.partial(slots_kernel, n_pos, scale),
        out_shape=(quadrant,) * 4 + (part, part),
        in_specs=[smem] * 3 + [vmem] * 7,
        out_specs=(vmem,) * 6,
        scratch_shapes=[pltpu.VMEM((2, 2 * edge, edge), f32)] * 4
        + [pltpu.VMEM((2, modes, edge, edge), f32)],
        compiler_params=pltpu.CompilerParams(vmem_limit_bytes=32 * 1024 * 1024),
    )(offsets, counts, place, held[0], below, right, diag, *held[1:])

    pieces = [(below_grad, 1, 0), (right_grad, 0, 1), (diag_grad, 1, 1)]
    object_grad = own_grad
    for step in range(steps):
        keep = keep + exchanged(send, step)
        if step < steps - 1:
            middle = keep.shape[0] // 2
            keep, send = keep[:middle], keep[middle:]
    for k in range(n_region.bit_length() - 1):
        keep = summed(keep, k)
    for step in reversed(range(steps)):
        got = exchanged(keep, step)
        keep = jnp.where(
            bit_of(step), jnp.concatenate([got, keep], axis=0), jnp.concatenate([keep, got], axis=0)
        )
    for piece, down, across in pieces:
        object_grad = object_grad + shifted(piece, down, across)
    return (object_grad, keep.reshape(probe.shape))


def solution(mesh):
    return jax.shard_map(
        on_device,
        mesh=mesh,
        in_specs=(
            P(None, "region", "pos"),
            P(),
            P("region", "pos", None, None),
            P("region", None, "pos"),
            P("region", "pos"),
        ),
        out_specs=(P(None, "region", "pos"), P()),
        check_vma=False,
    )
```

```python
import functools
import math

import jax
import jax.numpy as jnp
import ml_dtypes
import numpy as np
from jax import lax
from jax.experimental import pallas as pl
from jax.experimental.pallas import tpu as pltpu
from jax.sharding import PartitionSpec as P


def split_table(table):
    high = table.astype(ml_dtypes.bfloat16)
    low = (table - high.astype(np.float64)).astype(ml_dtypes.bfloat16)
    return high, low


def dft_tables(order):
    index = np.arange(order)
    angle = (index[:, None] * index[None, :] % order) * (2.0 * math.pi / order)
    cos_table = np.cos(angle) / math.sqrt(order)
    sin_table = np.sin(angle) / math.sqrt(order)
    spread = np.block([[cos_table, -sin_table], [sin_table, cos_table]])
    return np.stack(split_table(spread) + split_table(spread.T))


def split(value):
    high = value.astype(jnp.bfloat16)
    low = (value - high.astype(jnp.float32)).astype(jnp.bfloat16)
    return high, low


def dot(a, b):
    return jnp.dot(a, b, preferred_element_type=jnp.float32)


def times_table(value, table_high, table_low):
    high, low = split(value)
    return dot(high, table_high) + (dot(low, table_high) + dot(high, table_low))


def table_times(table_high, table_low, value):
    high, low = split(value)
    return dot(table_high, high) + (dot(table_high, low) + dot(table_low, high))


def load_kernel(*refs):
    count = (len(refs) - 1) // 2
    sources, targets, semaphores = refs[:count], refs[count : 2 * count], refs[-1]
    copies = [
        pltpu.make_async_copy(source, target, semaphores.at[index])
        for index, (source, target) in enumerate(zip(sources, targets))
    ]
    for copy in copies:
        copy.start()
    for copy in copies:
        copy.wait()


def slots_kernel(
    chunks, scale, offsets, counts, place, own, below, right, diag, probe, amplitudes, tables,
    own_grad, below_grad, right_grad, diag_grad, keep, send,
    field_left, field_right, grad_left, grad_right, probe_sum,
):
    spread_high, spread_low, turn_high, turn_low = (tables.at[k] for k in range(4))
    has_below, has_right = place[2] > 0, place[3] > 0
    has_diag = jnp.logical_and(has_below, has_right)

    def present(flag, value):
        return jnp.where(flag, value, jnp.zeros_like(value))

    modes, edge = probe.shape[1], probe.shape[2]
    slot_total = amplitudes.shape[1]
    field_left[:, :edge] = own[...].astype(jnp.float32)
    field_left[:, edge:] = present(has_below, below[...].astype(jnp.float32))
    field_right[:, :edge] = present(has_right, right[...].astype(jnp.float32))
    field_right[:, edge:] = present(has_diag, diag[...].astype(jnp.float32))
    grad_left[...] = jnp.zeros_like(grad_left)
    grad_right[...] = jnp.zeros_like(grad_right)
    lane = lax.broadcasted_iota(jnp.int32, (edge, edge), 1)
    for slot in range(slot_total):
        row0 = offsets[0, 0, slot]
        col0 = offsets[0, 1, slot]
        rows = pl.ds(row0, edge)
        in_left = lane >= col0
        weight = (slot < counts[0, 0]).astype(jnp.float32)
        back_shift = lax.rem(edge - col0, edge)
        crop_r, crop_i = (
            pltpu.roll(
                jnp.where(in_left, field_left[part, rows, :], field_right[part, rows, :]), back_shift, 1
            )
            for part in range(2)
        )
        exits = jnp.concatenate(
            [
                jnp.concatenate(
                    [
                        probe[0, m] * crop_r - probe[1, m] * crop_i,
                        probe[0, m] * crop_i + probe[1, m] * crop_r,
                    ],
                    axis=1,
                )
                for m in range(modes)
            ],
            axis=0,
        )
        half = times_table(exits, spread_high[...], spread_low[...])
        half = jnp.concatenate(
            [
                jnp.concatenate(
                    [half[m * edge : (m + 1) * edge, part * edge : (part + 1) * edge] for m in range(modes)],
                    axis=1,
                )
                for part in range(2)
            ],
            axis=0,
        )
        far = table_times(turn_high[...], turn_low[...], half)
        squares = far * far
        squares = squares[:edge] + squares[edge:]
        intensity = functools.reduce(
            jnp.add, [squares[:, m * edge : (m + 1) * edge] for m in range(modes)]
        )
        factor = weight * (1.0 - amplitudes[0, slot] * lax.rsqrt(intensity + 1.0))
        factor = jnp.concatenate([factor] * modes, axis=1)
        residual = far * jnp.concatenate([factor, factor], axis=0)
        half = table_times(spread_high[...], spread_low[...], residual)
        half = jnp.concatenate(
            [
                jnp.concatenate(
                    [half[part * edge : (part + 1) * edge, m * edge : (m + 1) * edge] for part in range(2)],
                    axis=1,
                )
                for m in range(modes)
            ],
            axis=0,
        )
        back = times_table(half, turn_high[...], turn_low[...])
        object_r = jnp.zeros((edge, edge), jnp.float32)
        object_i = jnp.zeros((edge, edge), jnp.float32)
        for m in range(modes):
            back_r = back[m * edge : (m + 1) * edge, :edge]
            back_i = back[m * edge : (m + 1) * edge, edge:]
            object_r += probe[0, m] * back_r + probe[1, m] * back_i
            object_i += probe[0, m] * back_i - probe[1, m] * back_r
            term_r = crop_r * back_r + crop_i * back_i
            term_i = crop_r * back_i - crop_i * back_r
            if slot == 0:
                probe_sum[0, m] = term_r
                probe_sum[1, m] = term_i
            else:
                probe_sum[0, m] += term_r
                probe_sum[1, m] += term_i
        for part, term in enumerate((object_r, object_i)):
            term = pltpu.roll(term, col0, 1)
            grad_left[part, rows, :] += jnp.where(in_left, term, 0.0)
            grad_right[part, rows, :] += jnp.where(in_left, 0.0, term)
    own_grad[...] = grad_left[:, :edge]
    below_grad[...] = present(has_below, grad_left[:, edge:])
    right_grad[...] = present(has_right, grad_right[:, :edge])
    diag_grad[...] = present(has_diag, grad_right[:, edge:])
    flat = probe_sum.reshape(2 * modes * edge, edge)
    depth = flat.shape[0] // chunks
    for target, owner in ((keep, place[0]), (send, place[1])):
        for row in range(chunks // 2):
            start = pl.multiple_of(jnp.bitwise_xor(owner, row) * depth, depth)
            target[pl.ds(row * depth, depth), :] = flat[pl.ds(start, depth), :] * scale


def on_device(object_tiles, probe, amplitudes, offsets, counts):
    modes, edge = probe.shape[1], probe.shape[2]
    slot_total = amplitudes.shape[1]
    n_region, n_pos = lax.axis_size("region"), lax.axis_size("pos")
    total = n_region * n_pos
    axes = ("region", "pos")
    f32 = jnp.float32

    row_index, column_index = lax.axis_index("region"), lax.axis_index("pos")

    def shifted(block, down, across):
        route = [
            (i * n_pos + j, (i + down) % n_region * n_pos + (j + across) % n_pos)
            for i in range(n_region)
            for j in range(n_pos)
        ]
        return lax.ppermute(block, axes, route)

    bits = [1 << k for k in range(n_pos.bit_length() - 1)]
    other = list(bits)
    if len(bits) > 2:
        other[1], other[2] = bits[2], bits[1]
    steps = len(bits)

    def exchanged(block, step):
        route = [(i, i ^ (other if i % 2 else bits)[step]) for i in range(total)]
        return lax.ppermute(block, axes, route)

    def partner(block, k):
        return lax.ppermute(block, axes, [(i, i ^ (n_pos << k)) for i in range(total)])

    def bit_of(step, flip=0):
        index = column_index ^ flip
        return jnp.where(index % 2 == 1, (index & other[step]) != 0, (index & bits[step]) != 0)

    def rank_of(flip):
        return sum(bit_of(step, flip).astype(jnp.int32) << (steps - 1 - step) for step in range(steps))

    place = jnp.stack(
        [
            rank_of(0),
            rank_of(1),
            (row_index < n_region - 1).astype(jnp.int32),
            (column_index < n_pos - 1).astype(jnp.int32),
        ]
    )

    below = shifted(object_tiles, -1, 0)
    right = shifted(object_tiles, 0, -1)
    diag = shifted(object_tiles, -1, -1)

    lines = 2 * modes * edge
    smem = pl.BlockSpec(memory_space=pltpu.SMEM)
    vmem = pl.BlockSpec(memory_space=pltpu.VMEM)
    held = (object_tiles, probe, amplitudes, jnp.asarray(dft_tables(edge)))
    held = pl.pallas_call(
        load_kernel,
        out_shape=tuple(jax.ShapeDtypeStruct(array.shape, array.dtype) for array in held),
        in_specs=[pl.BlockSpec(memory_space=pl.ANY)] * len(held),
        out_specs=(vmem,) * len(held),
        scratch_shapes=[pltpu.SemaphoreType.DMA((len(held),))],
        cost_estimate=pl.CostEstimate(flops=0, bytes_accessed=4 << 20, transcendentals=0),
        compiler_params=pltpu.CompilerParams(vmem_limit_bytes=2 * 1024 * 1024),
    )(*held)
    quadrant = jax.ShapeDtypeStruct((2, edge, edge), f32)
    part = jax.ShapeDtypeStruct((lines // 2, edge), f32)
    scale = 1.0 / math.sqrt(total * slot_total)
    own_grad, below_grad, right_grad, diag_grad, keep, send = pl.pallas_call(
        functools.partial(slots_kernel, n_pos, scale),
        out_shape=(quadrant,) * 4 + (part, part),
        in_specs=[smem] * 3 + [vmem] * 7,
        out_specs=(vmem,) * 6,
        scratch_shapes=[pltpu.VMEM((2, 2 * edge, edge), f32)] * 4
        + [pltpu.VMEM((2, modes, edge, edge), f32)],
        compiler_params=pltpu.CompilerParams(vmem_limit_bytes=16 * 1024 * 1024),
    )(offsets, counts, place, held[0], below, right, diag, *held[1:])

    arrived = []

    def beside(move, block, *pieces):
        blocks = lax.optimization_barrier((block,) + tuple(piece for piece, _, _ in pieces))
        moved = [move(blocks[0])]
        moved += [shifted(block, *piece[1:]) for block, piece in zip(blocks[1:], pieces)]
        got, *rest = lax.optimization_barrier(tuple(moved))
        arrived.extend(rest)
        return got

    for step in range(steps):
        move = functools.partial(exchanged, step=step)
        if step == 1:
            got = beside(move, send, (below_grad, 1, 0), (diag_grad, 1, 1))
        else:
            got = move(send)
        keep = keep + got
        if step < steps - 1:
            middle = keep.shape[0] // 2
            keep, send = keep[:middle], keep[middle:]
    for k in range(n_region.bit_length() - 1):
        keep = keep + partner(keep, k)
    for step in reversed(range(steps)):
        move = functools.partial(exchanged, step=step)
        got = beside(move, keep, (right_grad, 0, 1)) if step == 1 else move(keep)
        keep = jnp.where(
            bit_of(step), jnp.concatenate([got, keep], axis=0), jnp.concatenate([keep, got], axis=0)
        )
    object_grad = own_grad
    for piece in arrived:
        object_grad = object_grad + piece
    return (object_grad, keep.reshape(probe.shape))


def solution(mesh):
    return jax.shard_map(
        on_device,
        mesh=mesh,
        in_specs=(
            P(None, "region", "pos"),
            P(),
            P("region", "pos", None, None),
            P("region", None, "pos"),
            P("region", "pos"),
        ),
        out_specs=(P(None, "region", "pos"), P()),
        check_vma=False,
    )
```

```python
import functools
import math

import jax
import jax.numpy as jnp
import numpy as np
from jax import lax
from jax.experimental import pallas as pl
from jax.experimental.pallas import tpu as pltpu
from jax.sharding import PartitionSpec as P


def dft_tables(order):
    index = np.arange(order)
    angle = (index[:, None] * index[None, :] % order) * (2.0 * math.pi / order)
    tables = np.concatenate([np.cos(angle), np.sin(angle)]) / math.sqrt(order)
    return tables.astype(np.float32)


def split(value):
    high = value.astype(jnp.bfloat16)
    low = (value - high.astype(jnp.float32)).astype(jnp.bfloat16)
    return high, low


def dot(a, b):
    return jnp.dot(a, b, preferred_element_type=jnp.float32)


def times_table(value, table_high, table_low):
    high, low = split(value)
    return dot(high, table_high) + (dot(low, table_high) + dot(high, table_low))


def table_times(table_high, table_low, value):
    high, low = split(value)
    return dot(table_high, high) + (dot(table_high, low) + dot(table_low, high))


def held_parts(held, modes, slot_total, edge):
    parts, row = [], 0
    for shape in ((2,), (2, modes), (slot_total,), (), ()):
        depth = math.prod(shape) * edge
        parts.append(held.at[pl.ds(row, depth), :].reshape(*shape, edge, edge))
        row += depth
    return parts


def slots_kernel(
    chunks, scale, modes, slot_total, edge, place, held, below, right, diag,
    own_grad, right_grad, lower_grad, keep, send,
    tables, field_left, field_right, grad_left, grad_right, probe_sum,
):
    own, probe, amplitudes, cos_table, sin_table = held_parts(held, modes, slot_total, edge)
    cos_high, cos_low = split(cos_table[...])
    sin_high, sin_low = split(sin_table[...])
    spread_high, spread_low, turn_high, turn_low = (tables.at[k] for k in range(4))
    for spread, turn, cos_part, sin_part in (
        (spread_high, turn_high, cos_high, sin_high),
        (spread_low, turn_low, cos_low, sin_low),
    ):
        for target, upper, lower in ((spread, -sin_part, sin_part), (turn, sin_part, -sin_part)):
            target[:edge, :edge] = cos_part
            target[:edge, edge:] = upper
            target[edge:, :edge] = lower
            target[edge:, edge:] = cos_part
    has_below, has_right = place[2] > 0, place[3] > 0
    has_diag = jnp.logical_and(has_below, has_right)

    def present(flag, value):
        return jnp.where(flag, value, jnp.zeros_like(value))

    field_left[:, :edge] = own[...]
    field_left[:, edge:] = present(has_below, below[...].astype(jnp.float32))
    field_right[:, :edge] = present(has_right, right[...].astype(jnp.float32))
    field_right[:, edge:] = present(has_diag, diag[...].astype(jnp.float32))
    grad_left[...] = jnp.zeros_like(grad_left)
    grad_right[...] = jnp.zeros_like(grad_right)
    lane = lax.broadcasted_iota(jnp.int32, (edge, edge), 1)
    for slot in range(slot_total):
        row0 = place[5 + slot]
        col0 = place[5 + slot_total + slot]
        rows = pl.ds(row0, edge)
        in_left = lane >= col0
        weight = (slot < place[4]).astype(jnp.float32)
        back_shift = lax.rem(edge - col0, edge)
        crop_r, crop_i = (
            pltpu.roll(
                jnp.where(in_left, field_left[part, rows, :], field_right[part, rows, :]), back_shift, 1
            )
            for part in range(2)
        )
        exits = jnp.concatenate(
            [
                jnp.concatenate(
                    [
                        probe[0, m] * crop_r - probe[1, m] * crop_i,
                        probe[0, m] * crop_i + probe[1, m] * crop_r,
                    ],
                    axis=1,
                )
                for m in range(modes)
            ],
            axis=0,
        )
        half = times_table(exits, spread_high[...], spread_low[...])
        half = jnp.concatenate(
            [
                jnp.concatenate(
                    [half[m * edge : (m + 1) * edge, part * edge : (part + 1) * edge] for m in range(modes)],
                    axis=1,
                )
                for part in range(2)
            ],
            axis=0,
        )
        far = table_times(turn_high[...], turn_low[...], half)
        squares = far * far
        squares = squares[:edge] + squares[edge:]
        intensity = functools.reduce(
            jnp.add, [squares[:, m * edge : (m + 1) * edge] for m in range(modes)]
        )
        factor = weight * (1.0 - amplitudes[slot] * lax.rsqrt(intensity + 1.0))
        factor = jnp.concatenate([factor] * modes, axis=1)
        residual = far * jnp.concatenate([factor, factor], axis=0)
        half = table_times(spread_high[...], spread_low[...], residual)
        half = jnp.concatenate(
            [
                jnp.concatenate(
                    [half[part * edge : (part + 1) * edge, m * edge : (m + 1) * edge] for part in range(2)],
                    axis=1,
                )
                for m in range(modes)
            ],
            axis=0,
        )
        back = times_table(half, turn_high[...], turn_low[...])
        object_r = jnp.zeros((edge, edge), jnp.float32)
        object_i = jnp.zeros((edge, edge), jnp.float32)
        for m in range(modes):
            back_r = back[m * edge : (m + 1) * edge, :edge]
            back_i = back[m * edge : (m + 1) * edge, edge:]
            object_r += probe[0, m] * back_r + probe[1, m] * back_i
            object_i += probe[0, m] * back_i - probe[1, m] * back_r
            term_r = crop_r * back_r + crop_i * back_i
            term_i = crop_r * back_i - crop_i * back_r
            if slot == 0:
                probe_sum[0, m] = term_r
                probe_sum[1, m] = term_i
            else:
                probe_sum[0, m] += term_r
                probe_sum[1, m] += term_i
        for part, term in enumerate((object_r, object_i)):
            term = pltpu.roll(term, col0, 1)
            grad_left[part, rows, :] += jnp.where(in_left, term, 0.0)
            grad_right[part, rows, :] += jnp.where(in_left, 0.0, term)
    own_grad[...] = grad_left[:, :edge]
    right_grad[...] = present(has_right, grad_right[:, :edge])
    lower_grad[0] = present(has_below, grad_left[:, edge:])
    lower_grad[1] = present(has_diag, grad_right[:, edge:])
    flat = probe_sum.reshape(2 * modes * edge, edge)
    depth = flat.shape[0] // chunks
    for target, owner in ((keep, place[0]), (send, place[1])):
        for row in range(chunks // 2):
            start = pl.multiple_of(jnp.bitwise_xor(owner, row) * depth, depth)
            target[pl.ds(row * depth, depth), :] = flat[pl.ds(start, depth), :] * scale


def on_device(object_tiles, probe, amplitudes, offsets, counts):
    modes, edge = probe.shape[1], probe.shape[2]
    slot_total = amplitudes.shape[1]
    n_region, n_pos = lax.axis_size("region"), lax.axis_size("pos")
    total = n_region * n_pos
    axes = ("region", "pos")
    f32 = jnp.float32

    row_index, column_index = lax.axis_index("region"), lax.axis_index("pos")

    def shifted(block, down, across):
        route = [
            (i * n_pos + j, (i + down) % n_region * n_pos + (j + across) % n_pos)
            for i in range(n_region)
            for j in range(n_pos)
        ]
        return lax.ppermute(block, axes, route)

    bits = [1 << k for k in range(n_pos.bit_length() - 1)]
    other = list(bits)
    if len(bits) > 2:
        other[1], other[2] = bits[2], bits[1]
    steps = len(bits)

    def exchanged(block, step):
        route = [(i, i ^ (other if i % 2 else bits)[step]) for i in range(total)]
        return lax.ppermute(block, axes, route)

    def partner(block, k):
        return lax.ppermute(block, axes, [(i, i ^ (n_pos << k)) for i in range(total)])

    def bit_of(step, flip=0):
        index = column_index ^ flip
        return jnp.where(index % 2 == 1, (index & other[step]) != 0, (index & bits[step]) != 0)

    def rank_of(flip):
        return sum(bit_of(step, flip).astype(jnp.int32) << (steps - 1 - step) for step in range(steps))

    place = jnp.stack(
        [
            rank_of(0),
            rank_of(1),
            (row_index < n_region - 1).astype(jnp.int32),
            (column_index < n_pos - 1).astype(jnp.int32),
        ]
    )
    place = jnp.concatenate([place, counts.reshape(-1), offsets.reshape(-1)])

    below = shifted(object_tiles, -1, 0)
    right = shifted(object_tiles, 0, -1)
    diag = shifted(object_tiles, -1, -1)

    lines = 2 * modes * edge
    smem = pl.BlockSpec(memory_space=pltpu.SMEM)
    vmem = pl.BlockSpec(memory_space=pltpu.VMEM)
    held = jnp.concatenate(
        [
            object_tiles.astype(f32).reshape(-1, edge),
            probe.reshape(-1, edge),
            amplitudes.reshape(-1, edge),
            jnp.asarray(dft_tables(edge)),
        ],
        axis=0,
    )
    quadrant = jax.ShapeDtypeStruct((2, edge, edge), f32)
    part = jax.ShapeDtypeStruct((lines // 2, edge), f32)
    scale = 1.0 / math.sqrt(total * slot_total)
    own_grad, right_grad, lower_grad, keep, send = pl.pallas_call(
        functools.partial(slots_kernel, n_pos, scale, modes, slot_total, edge),
        out_shape=(quadrant, quadrant, jax.ShapeDtypeStruct((2, 2, edge, edge), f32), part, part),
        in_specs=[smem] + [vmem] * 4,
        out_specs=(vmem,) * 5,
        scratch_shapes=[pltpu.VMEM((4, 2 * edge, 2 * edge), jnp.bfloat16)]
        + [pltpu.VMEM((2, 2 * edge, edge), f32)] * 4
        + [pltpu.VMEM((2, modes, edge, edge), f32)],
        compiler_params=pltpu.CompilerParams(vmem_limit_bytes=16 * 1024 * 1024),
    )(place, held, below, right, diag)

    for step in range(steps):
        if step == 1:
            send, lower_grad = lax.optimization_barrier((send, lower_grad))
        keep = keep + exchanged(send, step)
        if step < steps - 1:
            middle = keep.shape[0] // 2
            keep, send = keep[:middle], keep[middle:]
    keep, upper = lax.optimization_barrier((keep, shifted(lower_grad, 1, 0)))
    own_grad, right_grad = own_grad + upper[0], right_grad + upper[1]
    for k in range(n_region.bit_length() - 1):
        keep = keep + partner(keep, k)
    keep, left = lax.optimization_barrier((keep, shifted(right_grad, 0, 1)))
    object_grad = own_grad + left
    for step in reversed(range(steps)):
        got = exchanged(keep, step)
        keep = jnp.where(
            bit_of(step), jnp.concatenate([got, keep], axis=0), jnp.concatenate([keep, got], axis=0)
        )
    return (object_grad, keep.reshape(probe.shape))


def solution(mesh):
    return jax.shard_map(
        on_device,
        mesh=mesh,
        in_specs=(
            P(None, "region", "pos"),
            P(),
            P("region", "pos", None, None),
            P("region", None, "pos"),
            P("region", "pos"),
        ),
        out_specs=(P(None, "region", "pos"), P()),
        check_vma=False,
    )
```

```python
import functools
import math

import jax
import jax.numpy as jnp
import numpy as np
from jax import lax
from jax.experimental import pallas as pl
from jax.experimental.pallas import tpu as pltpu
from jax.sharding import PartitionSpec as P


def dft_tables(order):
    index = np.arange(order)
    angle = (index[:, None] * index[None, :] % order) * (2.0 * math.pi / order)
    tables = np.concatenate([np.cos(angle), np.sin(angle)]) / math.sqrt(order)
    return tables.astype(np.float32)


def split(value):
    high = value.astype(jnp.bfloat16)
    low = (value - high.astype(jnp.float32)).astype(jnp.bfloat16)
    return high, low


def dot(a, b):
    return jnp.dot(a, b, preferred_element_type=jnp.float32)


def times_table(value, table_high, table_low):
    high, low = split(value)
    return dot(high, table_high) + (dot(low, table_high) + dot(high, table_low))


def table_times(table_high, table_low, value):
    high, low = split(value)
    return dot(table_high, high) + (dot(table_high, low) + dot(table_low, high))


def held_parts(held, modes, slot_total, edge):
    parts, row = [], 0
    for shape in ((2,), (2, modes), (slot_total,), (), ()):
        depth = math.prod(shape) * edge
        parts.append(held.at[pl.ds(row, depth), :].reshape(*shape, edge, edge))
        row += depth
    return parts


def slots_kernel(
    chunks, scale, modes, slot_total, edge, place, held, below, right, diag,
    own_grad, below_grad, right_grads, keep, send,
    tables, field_left, field_right, grad_left, grad_right, probe_sum,
):
    own, probe, amplitudes, cos_table, sin_table = held_parts(held, modes, slot_total, edge)
    cos_high, cos_low = split(cos_table[...])
    sin_high, sin_low = split(sin_table[...])
    spread_high, spread_low, turn_high, turn_low = (tables.at[k] for k in range(4))
    for spread, turn, cos_part, sin_part in (
        (spread_high, turn_high, cos_high, sin_high),
        (spread_low, turn_low, cos_low, sin_low),
    ):
        for target, upper, lower in ((spread, -sin_part, sin_part), (turn, sin_part, -sin_part)):
            target[:edge, :edge] = cos_part
            target[:edge, edge:] = upper
            target[edge:, :edge] = lower
            target[edge:, edge:] = cos_part
    has_below, has_right = place[2] > 0, place[3] > 0
    has_diag = jnp.logical_and(has_below, has_right)

    def present(flag, value):
        return jnp.where(flag, value, jnp.zeros_like(value))

    field_left[:, :edge] = own[...]
    field_left[:, edge:] = present(has_below, below[...].astype(jnp.float32))
    field_right[:, :edge] = present(has_right, right[...].astype(jnp.float32))
    field_right[:, edge:] = present(has_diag, diag[...].astype(jnp.float32))
    grad_left[...] = jnp.zeros_like(grad_left)
    grad_right[...] = jnp.zeros_like(grad_right)
    lane = lax.broadcasted_iota(jnp.int32, (edge, edge), 1)
    for slot in range(slot_total):
        row0 = place[5 + slot]
        col0 = place[5 + slot_total + slot]
        rows = pl.ds(row0, edge)
        in_left = lane >= col0
        weight = (slot < place[4]).astype(jnp.float32)
        back_shift = lax.rem(edge - col0, edge)
        crop_r, crop_i = (
            pltpu.roll(
                jnp.where(in_left, field_left[part, rows, :], field_right[part, rows, :]), back_shift, 1
            )
            for part in range(2)
        )
        exits = jnp.concatenate(
            [
                jnp.concatenate(
                    [
                        probe[0, m] * crop_r - probe[1, m] * crop_i,
                        probe[0, m] * crop_i + probe[1, m] * crop_r,
                    ],
                    axis=1,
                )
                for m in range(modes)
            ],
            axis=0,
        )
        half = times_table(exits, spread_high[...], spread_low[...])
        half = jnp.concatenate(
            [
                jnp.concatenate(
                    [half[m * edge : (m + 1) * edge, part * edge : (part + 1) * edge] for m in range(modes)],
                    axis=1,
                )
                for part in range(2)
            ],
            axis=0,
        )
        far = table_times(turn_high[...], turn_low[...], half)
        squares = far * far
        squares = squares[:edge] + squares[edge:]
        intensity = functools.reduce(
            jnp.add, [squares[:, m * edge : (m + 1) * edge] for m in range(modes)]
        )
        factor = weight * (1.0 - amplitudes[slot] * lax.rsqrt(intensity + 1.0))
        factor = jnp.concatenate([factor] * modes, axis=1)
        residual = far * jnp.concatenate([factor, factor], axis=0)
        half = table_times(spread_high[...], spread_low[...], residual)
        half = jnp.concatenate(
            [
                jnp.concatenate(
                    [half[part * edge : (part + 1) * edge, m * edge : (m + 1) * edge] for part in range(2)],
                    axis=1,
                )
                for m in range(modes)
            ],
            axis=0,
        )
        back = times_table(half, turn_high[...], turn_low[...])
        object_r = jnp.zeros((edge, edge), jnp.float32)
        object_i = jnp.zeros((edge, edge), jnp.float32)
        for m in range(modes):
            back_r = back[m * edge : (m + 1) * edge, :edge]
            back_i = back[m * edge : (m + 1) * edge, edge:]
            object_r += probe[0, m] * back_r + probe[1, m] * back_i
            object_i += probe[0, m] * back_i - probe[1, m] * back_r
            term_r = crop_r * back_r + crop_i * back_i
            term_i = crop_r * back_i - crop_i * back_r
            if slot == 0:
                probe_sum[0, m] = term_r
                probe_sum[1, m] = term_i
            else:
                probe_sum[0, m] += term_r
                probe_sum[1, m] += term_i
        for part, term in enumerate((object_r, object_i)):
            term = pltpu.roll(term, col0, 1)
            grad_left[part, rows, :] += jnp.where(in_left, term, 0.0)
            grad_right[part, rows, :] += jnp.where(in_left, 0.0, term)
    own_grad[...] = grad_left[:, :edge]
    below_grad[...] = present(has_below, grad_left[:, edge:])
    right_grads[0] = present(has_right, grad_right[:, :edge])
    right_grads[1] = present(has_diag, grad_right[:, edge:])
    flat = probe_sum.reshape(2 * modes * edge, edge)
    depth = flat.shape[0] // chunks
    for target, owner in ((keep, place[0]), (send, place[1])):
        for row in range(chunks // 2):
            start = pl.multiple_of(jnp.bitwise_xor(owner, row) * depth, depth)
            target[pl.ds(row * depth, depth), :] = flat[pl.ds(start, depth), :] * scale


def on_device(object_tiles, probe, amplitudes, offsets, counts):
    modes, edge = probe.shape[1], probe.shape[2]
    slot_total = amplitudes.shape[1]
    n_region, n_pos = lax.axis_size("region"), lax.axis_size("pos")
    total = n_region * n_pos
    axes = ("region", "pos")
    f32 = jnp.float32

    row_index, column_index = lax.axis_index("region"), lax.axis_index("pos")

    def shifted(block, down, across):
        route = [
            (i * n_pos + j, (i + down) % n_region * n_pos + (j + across) % n_pos)
            for i in range(n_region)
            for j in range(n_pos)
        ]
        return lax.ppermute(block, axes, route)

    bits = [1 << k for k in range(n_pos.bit_length() - 1)]
    other = list(bits)
    if len(bits) > 2:
        other[1], other[2] = bits[2], bits[1]
    steps = len(bits)

    def exchanged(block, step):
        route = [(i, i ^ (other if i % 2 else bits)[step]) for i in range(total)]
        return lax.ppermute(block, axes, route)

    def partner(block, k):
        return lax.ppermute(block, axes, [(i, i ^ (n_pos << k)) for i in range(total)])

    def bit_of(step, flip=0):
        index = column_index ^ flip
        return jnp.where(index % 2 == 1, (index & other[step]) != 0, (index & bits[step]) != 0)

    def rank_of(flip):
        return sum(bit_of(step, flip).astype(jnp.int32) << (steps - 1 - step) for step in range(steps))

    place = jnp.stack(
        [
            rank_of(0),
            rank_of(1),
            (row_index < n_region - 1).astype(jnp.int32),
            (column_index < n_pos - 1).astype(jnp.int32),
        ]
    )
    place = jnp.concatenate([place, counts.reshape(-1), offsets.reshape(-1)])

    below = shifted(object_tiles, -1, 0)
    right = shifted(object_tiles, 0, -1)
    diag = shifted(object_tiles, -1, -1)

    lines = 2 * modes * edge
    smem = pl.BlockSpec(memory_space=pltpu.SMEM)
    vmem = pl.BlockSpec(memory_space=pltpu.VMEM)
    held = jnp.concatenate(
        [
            object_tiles.astype(f32).reshape(-1, edge),
            probe.reshape(-1, edge),
            amplitudes.reshape(-1, edge),
            jnp.asarray(dft_tables(edge)),
        ],
        axis=0,
    )
    quadrant = jax.ShapeDtypeStruct((2, edge, edge), f32)
    part = jax.ShapeDtypeStruct((lines // 2, edge), f32)
    scale = 1.0 / math.sqrt(total * slot_total)
    own_grad, below_grad, right_grads, keep, send = pl.pallas_call(
        functools.partial(slots_kernel, n_pos, scale, modes, slot_total, edge),
        out_shape=(quadrant, quadrant, jax.ShapeDtypeStruct((2, 2, edge, edge), f32), part, part),
        in_specs=[smem] + [vmem] * 4,
        out_specs=(vmem,) * 5,
        scratch_shapes=[pltpu.VMEM((4, 2 * edge, 2 * edge), jnp.bfloat16)]
        + [pltpu.VMEM((2, 2 * edge, edge), f32)] * 4
        + [pltpu.VMEM((2, modes, edge, edge), f32)],
        compiler_params=pltpu.CompilerParams(vmem_limit_bytes=16 * 1024 * 1024),
    )(place, held, below, right, diag)

    for step in range(steps):
        keep = keep + exchanged(send, step)
        if step < steps - 1:
            middle = keep.shape[0] // 2
            keep, send = keep[:middle], keep[middle:]
    keep, right_grads = lax.optimization_barrier((keep, right_grads))
    left = shifted(right_grads, 0, 1)
    for k in range(n_region.bit_length() - 1):
        keep = keep + partner(keep, k)
    keep, left = lax.optimization_barrier((keep, left))
    above = shifted(below_grad + left[1], 1, 0)
    for step in reversed(range(steps)):
        got = exchanged(keep, step)
        keep = jnp.where(
            bit_of(step), jnp.concatenate([got, keep], axis=0), jnp.concatenate([keep, got], axis=0)
        )
    object_grad = own_grad + left[0] + above
    return (object_grad, keep.reshape(probe.shape))


def solution(mesh):
    return jax.shard_map(
        on_device,
        mesh=mesh,
        in_specs=(
            P(None, "region", "pos"),
            P(),
            P("region", "pos", None, None),
            P("region", None, "pos"),
            P("region", "pos"),
        ),
        out_specs=(P(None, "region", "pos"), P()),
        check_vma=False,
    )
```

```python
import functools
import math

import jax
import jax.numpy as jnp
import numpy as np
from jax import lax
from jax.experimental import pallas as pl
from jax.experimental.pallas import tpu as pltpu
from jax.sharding import PartitionSpec as P


def dft_tables(order):
    index = np.arange(order)
    angle = (index[:, None] * index[None, :] % order) * (2.0 * math.pi / order)
    tables = np.concatenate([np.cos(angle), np.sin(angle)]) / math.sqrt(order)
    return tables.astype(np.float32)


def split(value):
    high = value.astype(jnp.bfloat16)
    low = (value - high.astype(jnp.float32)).astype(jnp.bfloat16)
    return high, low


def dot(a, b):
    return jnp.dot(a, b, preferred_element_type=jnp.float32)


def times_table(value, table_high, table_low):
    high, low = split(value)
    return dot(high, table_high) + (dot(low, table_high) + dot(high, table_low))


def table_times(table_high, table_low, value):
    high, low = split(value)
    return dot(table_high, high) + (dot(table_high, low) + dot(table_low, high))


def held_parts(held, modes, slot_total, edge):
    parts, row = [], 0
    for shape in ((2,), (2, modes), (slot_total,), (), ()):
        depth = math.prod(shape) * edge
        parts.append(held.at[pl.ds(row, depth), :].reshape(*shape, edge, edge))
        row += depth
    return parts


def slots_kernel(
    scale, modes, slot_total, edge, place, held, below, right, diag,
    own_grad, below_grad, right_grads, keep, send,
    tables, field_left, field_right, grad_left, grad_right, probe_sum,
):
    own, probe, amplitudes, cos_table, sin_table = held_parts(held, modes, slot_total, edge)
    cos_high, cos_low = split(cos_table[...])
    sin_high, sin_low = split(sin_table[...])
    spread_high, spread_low, turn_high, turn_low = (tables.at[k] for k in range(4))
    for spread, turn, cos_part, sin_part in (
        (spread_high, turn_high, cos_high, sin_high),
        (spread_low, turn_low, cos_low, sin_low),
    ):
        for target, upper, lower in ((spread, -sin_part, sin_part), (turn, sin_part, -sin_part)):
            target[:edge, :edge] = cos_part
            target[:edge, edge:] = upper
            target[edge:, :edge] = lower
            target[edge:, edge:] = cos_part
    has_below, has_right = place[1] > 0, place[2] > 0
    has_diag = jnp.logical_and(has_below, has_right)

    def present(flag, value):
        return jnp.where(flag, value, jnp.zeros_like(value))

    field_left[:, :edge] = own[...]
    field_left[:, edge:] = present(has_below, below[...].astype(jnp.float32))
    field_right[:, :edge] = present(has_right, right[...].astype(jnp.float32))
    field_right[:, edge:] = present(has_diag, diag[...].astype(jnp.float32))
    grad_left[...] = jnp.zeros_like(grad_left)
    grad_right[...] = jnp.zeros_like(grad_right)
    lane = lax.broadcasted_iota(jnp.int32, (edge, edge), 1)
    for slot in range(slot_total):
        row0 = place[4 + slot]
        col0 = place[4 + slot_total + slot]
        rows = pl.ds(row0, edge)
        in_left = lane >= col0
        weight = (slot < place[3]).astype(jnp.float32)
        back_shift = lax.rem(edge - col0, edge)
        crop_r, crop_i = (
            pltpu.roll(
                jnp.where(in_left, field_left[part, rows, :], field_right[part, rows, :]), back_shift, 1
            )
            for part in range(2)
        )
        exits = jnp.concatenate(
            [
                jnp.concatenate(
                    [
                        probe[0, m] * crop_r - probe[1, m] * crop_i,
                        probe[0, m] * crop_i + probe[1, m] * crop_r,
                    ],
                    axis=1,
                )
                for m in range(modes)
            ],
            axis=0,
        )
        half = times_table(exits, spread_high[...], spread_low[...])
        half = jnp.concatenate(
            [
                jnp.concatenate(
                    [half[m * edge : (m + 1) * edge, part * edge : (part + 1) * edge] for m in range(modes)],
                    axis=1,
                )
                for part in range(2)
            ],
            axis=0,
        )
        far = table_times(turn_high[...], turn_low[...], half)
        squares = far * far
        squares = squares[:edge] + squares[edge:]
        intensity = functools.reduce(
            jnp.add, [squares[:, m * edge : (m + 1) * edge] for m in range(modes)]
        )
        factor = weight * (1.0 - amplitudes[slot] * lax.rsqrt(intensity + 1.0))
        factor = jnp.concatenate([factor] * modes, axis=1)
        residual = far * jnp.concatenate([factor, factor], axis=0)
        half = table_times(spread_high[...], spread_low[...], residual)
        half = jnp.concatenate(
            [
                jnp.concatenate(
                    [half[part * edge : (part + 1) * edge, m * edge : (m + 1) * edge] for part in range(2)],
                    axis=1,
                )
                for m in range(modes)
            ],
            axis=0,
        )
        back = times_table(half, turn_high[...], turn_low[...])
        object_r = jnp.zeros((edge, edge), jnp.float32)
        object_i = jnp.zeros((edge, edge), jnp.float32)
        for m in range(modes):
            back_r = back[m * edge : (m + 1) * edge, :edge]
            back_i = back[m * edge : (m + 1) * edge, edge:]
            object_r += probe[0, m] * back_r + probe[1, m] * back_i
            object_i += probe[0, m] * back_i - probe[1, m] * back_r
            term_r = crop_r * back_r + crop_i * back_i
            term_i = crop_r * back_i - crop_i * back_r
            if slot == 0:
                probe_sum[0, m] = term_r
                probe_sum[1, m] = term_i
            else:
                probe_sum[0, m] += term_r
                probe_sum[1, m] += term_i
        for part, term in enumerate((object_r, object_i)):
            term = pltpu.roll(term, col0, 1)
            grad_left[part, rows, :] += jnp.where(in_left, term, 0.0)
            grad_right[part, rows, :] += jnp.where(in_left, 0.0, term)
    own_grad[...] = grad_left[:, :edge]
    below_grad[...] = present(has_below, grad_left[:, edge:])
    right_grads[0] = present(has_right, grad_right[:, :edge])
    right_grads[1] = present(has_diag, grad_right[:, edge:])
    flat = probe_sum.reshape(2 * modes * edge, edge)
    depth = flat.shape[0] // 2
    for target, half in ((keep, place[0]), (send, 1 - place[0])):
        target[...] = flat[pl.ds(pl.multiple_of(half * depth, depth), depth), :] * scale


def on_device(object_tiles, probe, amplitudes, offsets, counts):
    modes, edge = probe.shape[1], probe.shape[2]
    slot_total = amplitudes.shape[1]
    n_region, n_pos = lax.axis_size("region"), lax.axis_size("pos")
    total = n_region * n_pos
    axes = ("region", "pos")
    f32 = jnp.float32

    row_index, column_index = lax.axis_index("region"), lax.axis_index("pos")

    def shifted(block, down, across):
        route = [
            (i * n_pos + j, (i + down) % n_region * n_pos + (j + across) % n_pos)
            for i in range(n_region)
            for j in range(n_pos)
        ]
        return lax.ppermute(block, axes, route)

    other = [(i, i ^ 1) for i in range(total)]
    others = [
        [i * n_pos + j for j in range(parity, n_pos, 2)] for i in range(n_region) for parity in range(2)
    ]
    parity = column_index % 2

    def swapped(block):
        return lax.all_to_all(block, axes, 0, 0, axis_index_groups=others, tiled=True)

    def partner(block, k):
        return lax.ppermute(block, axes, [(i, i ^ (n_pos << k)) for i in range(total)])

    place = jnp.stack(
        [
            parity.astype(jnp.int32),
            (row_index < n_region - 1).astype(jnp.int32),
            (column_index < n_pos - 1).astype(jnp.int32),
        ]
    )
    place = jnp.concatenate([place, counts.reshape(-1), offsets.reshape(-1)])

    below = shifted(object_tiles, -1, 0)
    right = shifted(object_tiles, 0, -1)
    diag = shifted(object_tiles, -1, -1)

    lines = 2 * modes * edge
    smem = pl.BlockSpec(memory_space=pltpu.SMEM)
    vmem = pl.BlockSpec(memory_space=pltpu.VMEM)
    held = jnp.concatenate(
        [
            object_tiles.astype(f32).reshape(-1, edge),
            probe.reshape(-1, edge),
            amplitudes.reshape(-1, edge),
            jnp.asarray(dft_tables(edge)),
        ],
        axis=0,
    )
    quadrant = jax.ShapeDtypeStruct((2, edge, edge), f32)
    part = jax.ShapeDtypeStruct((lines // 2, edge), f32)
    scale = 1.0 / math.sqrt(total * slot_total)
    own_grad, below_grad, right_grads, keep, send = pl.pallas_call(
        functools.partial(slots_kernel, scale, modes, slot_total, edge),
        out_shape=(quadrant, quadrant, jax.ShapeDtypeStruct((2, 2, edge, edge), f32), part, part),
        in_specs=[smem] + [vmem] * 4,
        out_specs=(vmem,) * 5,
        scratch_shapes=[pltpu.VMEM((4, 2 * edge, 2 * edge), jnp.bfloat16)]
        + [pltpu.VMEM((2, 2 * edge, edge), f32)] * 4
        + [pltpu.VMEM((2, modes, edge, edge), f32)],
        compiler_params=pltpu.CompilerParams(vmem_limit_bytes=16 * 1024 * 1024),
    )(place, held, below, right, diag)

    keep = keep + lax.ppermute(send, axes, other)
    keep = jnp.sum(swapped(keep).reshape(n_pos // 2, -1, edge), axis=0)
    keep, right_grads = lax.optimization_barrier((keep, right_grads))
    left = shifted(right_grads, 0, 1)
    for k in range(n_region.bit_length() - 1):
        keep = keep + partner(keep, k)
    keep, left = lax.optimization_barrier((keep, left))
    above = shifted(below_grad + left[1], 1, 0)
    keep = swapped(jnp.concatenate([keep] * (n_pos // 2), axis=0))
    got = lax.ppermute(keep, axes, other)
    keep = jnp.where(
        parity == 1, jnp.concatenate([got, keep], axis=0), jnp.concatenate([keep, got], axis=0)
    )
    object_grad = own_grad + left[0] + above
    return (object_grad, keep.reshape(probe.shape))


def solution(mesh):
    return jax.shard_map(
        on_device,
        mesh=mesh,
        in_specs=(
            P(None, "region", "pos"),
            P(),
            P("region", "pos", None, None),
            P("region", None, "pos"),
            P("region", "pos"),
        ),
        out_specs=(P(None, "region", "pos"), P()),
        check_vma=False,
    )
```

```python
import functools
import math

import jax
import jax.numpy as jnp
import numpy as np
from jax import lax
from jax.experimental import pallas as pl
from jax.experimental.pallas import tpu as pltpu
from jax.sharding import PartitionSpec as P


def dft_tables(order):
    index = np.arange(order)
    angle = (index[:, None] * index[None, :] % order) * (2.0 * math.pi / order)
    tables = np.stack([np.cos(angle), np.sin(angle)]) / math.sqrt(order)
    return tables.astype(np.float32)


def split(value):
    high = value.astype(jnp.bfloat16)
    low = (value - high.astype(jnp.float32)).astype(jnp.bfloat16)
    return high, low


def dot(a, b):
    return jnp.dot(a, b, preferred_element_type=jnp.float32)


def times_table(value, tables):
    high, low = split(value)
    return dot(jnp.concatenate([high, low, high], axis=1), tables)


def table_times(tables, value):
    high, low = split(value)
    return dot(tables, jnp.concatenate([high, low, high], axis=0))


def slots_kernel(
    scale, modes, slot_total, edge, place, held, below, right, diag,
    own_grad, below_grad, right_grads, keep, send,
    tables, field_left, field_right, grad_left, grad_right, probe_sum,
):

    def probe(part, mode):
        return held[part, pl.ds((1 + mode) * edge, edge), :]

    amplitude_rows = (1 + modes) * edge
    table_rows = amplitude_rows + slot_total * edge // 2
    cos_high, cos_low = split(held[0, pl.ds(table_rows, edge), :])
    sin_high, sin_low = split(held[1, pl.ds(table_rows, edge), :])
    spread_down, turn_down, spread_along, turn_along = tables
    for place_in, cos_part, sin_part in ((0, cos_high, sin_high), (1, cos_high, sin_high), (2, cos_low, sin_low)):
        start = 2 * edge * place_in
        for upper, lower, down, along in (
            (-sin_part, sin_part, spread_down, spread_along),
            (sin_part, -sin_part, turn_down, turn_along),
        ):
            for row, column, part in (
                (0, 0, cos_part), (0, edge, upper), (edge, 0, lower), (edge, edge, cos_part),
            ):
                down[pl.ds(start + row, edge), pl.ds(column, edge)] = part
                along[pl.ds(row, edge), pl.ds(start + column, edge)] = part
    has_below, has_right = place[4, 0] > 0, place[5, 0] > 0
    has_diag = jnp.logical_and(has_below, has_right)

    def present(flag, value):
        return jnp.where(flag, value, jnp.zeros_like(value))

    field_left[:, :edge] = held[:, :edge]
    field_left[:, edge:] = present(has_below, below[...].astype(jnp.float32))
    field_right[:, :edge] = present(has_right, right[...].astype(jnp.float32))
    field_right[:, edge:] = present(has_diag, diag[...].astype(jnp.float32))
    grad_left[...] = jnp.zeros_like(grad_left)
    grad_right[...] = jnp.zeros_like(grad_right)
    lane = lax.broadcasted_iota(jnp.int32, (edge, edge), 1)
    for slot in range(slot_total):
        row0 = place[0, slot]
        col0 = place[1, slot]
        rows = pl.ds(row0, edge)
        in_left = lane >= col0
        weight = (slot < place[6, 0]).astype(jnp.float32)
        back_shift = lax.rem(edge - col0, edge)
        crop_r, crop_i = (
            pltpu.roll(
                jnp.where(in_left, field_left[part, rows, :], field_right[part, rows, :]), back_shift, 1
            )
            for part in range(2)
        )
        exits = jnp.concatenate(
            [
                jnp.concatenate(
                    [
                        probe(0, m) * crop_r - probe(1, m) * crop_i,
                        probe(0, m) * crop_i + probe(1, m) * crop_r,
                    ],
                    axis=1,
                )
                for m in range(modes)
            ],
            axis=0,
        )
        half = times_table(exits, spread_down[...])
        half = jnp.concatenate(
            [
                jnp.concatenate(
                    [half[m * edge : (m + 1) * edge, part * edge : (part + 1) * edge] for m in range(modes)],
                    axis=1,
                )
                for part in range(2)
            ],
            axis=0,
        )
        far = table_times(turn_along[...], half)
        squares = far * far
        squares = squares[:edge] + squares[edge:]
        intensity = functools.reduce(
            jnp.add, [squares[:, m * edge : (m + 1) * edge] for m in range(modes)]
        )
        half_slots = slot_total // 2
        amplitude = held[slot // half_slots, pl.ds(amplitude_rows + slot % half_slots * edge, edge), :]
        factor = weight * (1.0 - amplitude * lax.rsqrt(intensity + 1.0))
        factor = jnp.concatenate([factor] * modes, axis=1)
        residual = far * jnp.concatenate([factor, factor], axis=0)
        half = table_times(spread_along[...], residual)
        half = jnp.concatenate(
            [
                jnp.concatenate(
                    [half[part * edge : (part + 1) * edge, m * edge : (m + 1) * edge] for part in range(2)],
                    axis=1,
                )
                for m in range(modes)
            ],
            axis=0,
        )
        back = times_table(half, turn_down[...])
        object_r = jnp.zeros((edge, edge), jnp.float32)
        object_i = jnp.zeros((edge, edge), jnp.float32)
        for m in range(modes):
            back_r = back[m * edge : (m + 1) * edge, :edge]
            back_i = back[m * edge : (m + 1) * edge, edge:]
            object_r += probe(0, m) * back_r + probe(1, m) * back_i
            object_i += probe(0, m) * back_i - probe(1, m) * back_r
            term_r = crop_r * back_r + crop_i * back_i
            term_i = crop_r * back_i - crop_i * back_r
            if slot == 0:
                probe_sum[0, m] = term_r
                probe_sum[1, m] = term_i
            else:
                probe_sum[0, m] += term_r
                probe_sum[1, m] += term_i
        for part, term in enumerate((object_r, object_i)):
            term = pltpu.roll(term, col0, 1)
            grad_left[part, rows, :] += jnp.where(in_left, term, 0.0)
            grad_right[part, rows, :] += jnp.where(in_left, 0.0, term)
    own_grad[...] = grad_left[:, :edge]
    below_grad[...] = present(has_below, grad_left[:, edge:])
    right_grads[0] = present(has_right, grad_right[:, :edge])
    right_grads[1] = present(has_diag, grad_right[:, edge:])
    flat = probe_sum.reshape(2 * modes * edge, edge)
    pieces, depth = keep.shape[0], keep.shape[1]
    for target, half in ((keep, place[2, 0]), (send, 1 - place[2, 0])):
        for position in range(pieces):
            chunk = half * pieces + jnp.bitwise_xor(place[3, 0], position)
            rows = pl.ds(pl.multiple_of(chunk * depth, depth), depth)
            target[position] = flat[rows, :] * scale


def join_kernel(place, own_grad, left, above, *refs):
    pieces, (out, object_grad, total, semaphores) = refs[:-4], refs[-4:]
    count, depth = len(pieces) // 2, pieces[0].shape[0]
    copies = []
    for index, piece in enumerate(pieces):
        half = place[2, 0] if index < count else 1 - place[2, 0]
        chunk = half * count + jnp.bitwise_xor(place[3, 0], index % count)
        rows = pl.ds(pl.multiple_of(chunk * depth, depth), depth)
        copies.append(pltpu.make_async_copy(piece, out.at[rows, :], semaphores.at[index]))
    total[...] = own_grad[...] + left[0] + above[...]
    copies.insert(0, pltpu.make_async_copy(total, object_grad, semaphores.at[len(pieces)]))
    for copy in copies:
        copy.start()
    for copy in copies:
        copy.wait()


def on_device(object_tiles, probe, amplitudes, offsets, counts):
    modes, edge = probe.shape[1], probe.shape[2]
    slot_total = amplitudes.shape[1]
    n_region, n_pos = lax.axis_size("region"), lax.axis_size("pos")
    total = n_region * n_pos
    axes = ("region", "pos")
    f32 = jnp.float32

    row_index, column_index = lax.axis_index("region"), lax.axis_index("pos")

    def shifted(block, down, across):
        route = [
            (i * n_pos + j, (i + down) % n_region * n_pos + (j + across) % n_pos)
            for i in range(n_region)
            for j in range(n_pos)
        ]
        return lax.ppermute(block, axes, route)

    pieces = n_pos // 2

    def partner(block, mask):
        return lax.ppermute(block, axes, [(i, i ^ mask) for i in range(total)])

    place = jnp.concatenate(
        [offsets.reshape(2, slot_total)]
        + [
            jnp.broadcast_to(value.astype(jnp.int32).reshape(1, 1), (1, slot_total))
            for value in (
                column_index % 2,
                column_index // 2,
                row_index < n_region - 1,
                column_index < n_pos - 1,
                counts,
            )
        ],
        axis=0,
    )

    below = shifted(object_tiles, -1, 0)
    right = shifted(object_tiles, 0, -1)
    diag = shifted(object_tiles, -1, -1)

    lines = 2 * modes * edge
    smem = pl.BlockSpec(memory_space=pltpu.SMEM)
    vmem = pl.BlockSpec(memory_space=pltpu.VMEM)
    held = jnp.concatenate(
        [
            object_tiles.astype(f32),
            probe.reshape(2, -1, edge),
            amplitudes.reshape(2, -1, edge),
            jnp.asarray(dft_tables(edge)),
        ],
        axis=1,
    )
    quadrant = jax.ShapeDtypeStruct((2, edge, edge), f32)
    part = jax.ShapeDtypeStruct((pieces, lines // n_pos, edge), f32)
    scale = 1.0 / math.sqrt(total * slot_total)
    own_grad, below_grad, right_grads, keep, send = pl.pallas_call(
        functools.partial(slots_kernel, scale, modes, slot_total, edge),
        out_shape=(quadrant, quadrant, jax.ShapeDtypeStruct((2, 2, edge, edge), f32), part, part),
        in_specs=[smem] + [vmem] * 4,
        out_specs=(vmem,) * 5,
        scratch_shapes=[
            [pltpu.VMEM((6 * edge, 2 * edge), jnp.bfloat16)] * 2
            + [pltpu.VMEM((2 * edge, 6 * edge), jnp.bfloat16)] * 2
        ]
        + [pltpu.VMEM((2, 2 * edge, edge), f32)] * 4
        + [pltpu.VMEM((2, modes, edge, edge), f32)],
        compiler_params=pltpu.CompilerParams(vmem_limit_bytes=16 * 1024 * 1024),
    )(place, held, below, right, diag)

    half = keep + partner(send, 1)
    got = [partner(half[k], 2 * k) for k in range(1, pieces)]
    got[0], right_grads = lax.optimization_barrier((got[0], right_grads))
    left = shifted(right_grads, 0, 1)
    chunk = functools.reduce(jnp.add, got, half[0])
    terms = [chunk] + [partner(chunk, n_pos * k) for k in range(1, n_region)]
    while len(terms) > 1:
        terms = [terms[k] + terms[k + 1] for k in range(0, len(terms), 2)]
    chunk = terms[0]
    chunk, left = lax.optimization_barrier((chunk, left))
    above = shifted(below_grad + left[1], 1, 0)
    gathered = [chunk] + [partner(chunk, 2 * k) for k in range(1, pieces)]
    gathered += [partner(piece, 1) for piece in gathered]
    probe_grad, object_grad = pl.pallas_call(
        join_kernel,
        out_shape=(jax.ShapeDtypeStruct((lines, edge), f32), quadrant),
        in_specs=[smem] + [vmem] * (3 + n_pos),
        out_specs=(pl.BlockSpec(memory_space=pl.ANY),) * 2,
        scratch_shapes=[pltpu.VMEM((2, edge, edge), f32), pltpu.SemaphoreType.DMA((n_pos + 1,))],
        compiler_params=pltpu.CompilerParams(vmem_limit_bytes=4 * 1024 * 1024),
    )(place, own_grad, left, above, *gathered)
    return (object_grad, probe_grad.reshape(probe.shape))


def solution(mesh):
    return jax.shard_map(
        on_device,
        mesh=mesh,
        in_specs=(
            P(None, "region", "pos"),
            P(),
            P("region", "pos", None, None),
            P("region", None, "pos"),
            P("region", "pos"),
        ),
        out_specs=(P(None, "region", "pos"), P()),
        check_vma=False,
    )
```

```python
import functools
import math

import jax
import jax.numpy as jnp
import numpy as np
from jax import lax
from jax.experimental import pallas as pl
from jax.experimental.pallas import tpu as pltpu
from jax.sharding import PartitionSpec as P


def dft_tables(order):
    index = np.arange(order)
    angle = (index[:, None] * index[None, :] % order) * (2.0 * math.pi / order)
    tables = np.stack([np.cos(angle), np.sin(angle)]) / math.sqrt(order)
    return tables.astype(np.float32)


def split(value):
    high = value.astype(jnp.bfloat16)
    low = (value - high.astype(jnp.float32)).astype(jnp.bfloat16)
    return high, low


def dot(a, b):
    return jnp.dot(a, b, preferred_element_type=jnp.float32)


def times_table(value, table_high, table_low):
    high, low = split(value)
    return dot(high, table_high) + (dot(low, table_high) + dot(high, table_low))


def table_times(table_high, table_low, value):
    high, low = split(value)
    return dot(table_high, high) + (dot(table_high, low) + dot(table_low, high))


def slots_kernel(
    scale, modes, slot_total, edge, offsets, counts, place, held, own, below, right, diag,
    own_grad, below_grad, right_grads, keep, send,
    tables, field_left, field_right, grad_left, grad_right, probe_sum, corners, live, semaphores,
):
    scalars = (
        pltpu.make_async_copy(offsets, corners, semaphores.at[0]),
        pltpu.make_async_copy(counts, live, semaphores.at[1]),
    )
    for copy in scalars:
        copy.start()

    def probe(part, mode):
        return held[part, pl.ds(mode * edge, edge), :]

    amplitude_rows = modes * edge
    table_rows = amplitude_rows + slot_total * edge // 2
    cos_high, cos_low = split(held[0, pl.ds(table_rows, edge), :])
    sin_high, sin_low = split(held[1, pl.ds(table_rows, edge), :])
    spread_high, spread_low, turn_high, turn_low = (tables.at[k] for k in range(4))
    for spread, turn, cos_part, sin_part in (
        (spread_high, turn_high, cos_high, sin_high),
        (spread_low, turn_low, cos_low, sin_low),
    ):
        for target, upper, lower in ((spread, -sin_part, sin_part), (turn, sin_part, -sin_part)):
            target[:edge, :edge] = cos_part
            target[:edge, edge:] = upper
            target[edge:, :edge] = lower
            target[edge:, edge:] = cos_part
    has_below, has_right = place[2] > 0, place[3] > 0
    has_diag = jnp.logical_and(has_below, has_right)

    def present(flag, value):
        return jnp.where(flag, value, jnp.zeros_like(value))

    field_left[:, :edge] = own[...].astype(jnp.float32)
    field_left[:, edge:] = present(has_below, below[...].astype(jnp.float32))
    field_right[:, :edge] = present(has_right, right[...].astype(jnp.float32))
    field_right[:, edge:] = present(has_diag, diag[...].astype(jnp.float32))
    grad_left[...] = jnp.zeros_like(grad_left)
    grad_right[...] = jnp.zeros_like(grad_right)
    lane = lax.broadcasted_iota(jnp.int32, (edge, edge), 1)
    for copy in scalars:
        copy.wait()
    slots = range(slot_total)
    corner = [(corners[0, 0, slot], corners[0, 1, slot]) for slot in slots]
    in_left = [lane >= col0 for _, col0 in corner]
    crops, halves = [], []
    for slot in slots:
        row0, col0 = corner[slot]
        rows, shift = pl.ds(row0, edge), lax.rem(edge - col0, edge)
        crop_r, crop_i = (
            pltpu.roll(
                jnp.where(in_left[slot], field_left[part, rows, :], field_right[part, rows, :]), shift, 1
            )
            for part in range(2)
        )
        exits = [
            jnp.concatenate(
                [
                    probe(0, m) * crop_r - probe(1, m) * crop_i,
                    probe(0, m) * crop_i + probe(1, m) * crop_r,
                ],
                axis=1,
            )
            for m in range(modes)
        ]
        crops.append((crop_r, crop_i))
        halves.append(times_table(jnp.concatenate(exits, axis=0), spread_high[...], spread_low[...]))
    fars = []
    for half in halves:
        parts = [
            [half[m * edge : (m + 1) * edge, part * edge : (part + 1) * edge] for m in range(modes)]
            for part in range(2)
        ]
        half = jnp.concatenate([jnp.concatenate(part, axis=1) for part in parts], axis=0)
        fars.append(table_times(turn_high[...], turn_low[...], half))
    halves = []
    for slot in slots:
        far = fars[slot]
        squares = far * far
        squares = squares[:edge] + squares[edge:]
        intensity = functools.reduce(
            jnp.add, [squares[:, m * edge : (m + 1) * edge] for m in range(modes)]
        )
        weight = (slot < live[0, 0]).astype(jnp.float32)
        half_slots = slot_total // 2
        amplitude = held[slot // half_slots, pl.ds(amplitude_rows + slot % half_slots * edge, edge), :]
        factor = weight * (1.0 - amplitude * lax.rsqrt(intensity + 1.0))
        factor = jnp.concatenate([factor] * modes, axis=1)
        residual = far * jnp.concatenate([factor, factor], axis=0)
        halves.append(table_times(spread_high[...], spread_low[...], residual))
    backs = []
    for half in halves:
        parts = [
            [half[part * edge : (part + 1) * edge, m * edge : (m + 1) * edge] for part in range(2)]
            for m in range(modes)
        ]
        half = jnp.concatenate([jnp.concatenate(part, axis=1) for part in parts], axis=0)
        backs.append(times_table(half, turn_high[...], turn_low[...]))
    for slot in slots:
        crop_r, crop_i = crops[slot]
        row0, col0 = corner[slot]
        rows = pl.ds(row0, edge)
        object_r = jnp.zeros((edge, edge), jnp.float32)
        object_i = jnp.zeros((edge, edge), jnp.float32)
        for m in range(modes):
            back_r = backs[slot][m * edge : (m + 1) * edge, :edge]
            back_i = backs[slot][m * edge : (m + 1) * edge, edge:]
            object_r += probe(0, m) * back_r + probe(1, m) * back_i
            object_i += probe(0, m) * back_i - probe(1, m) * back_r
            term_r = crop_r * back_r + crop_i * back_i
            term_i = crop_r * back_i - crop_i * back_r
            if slot == 0:
                probe_sum[0, m] = term_r
                probe_sum[1, m] = term_i
            else:
                probe_sum[0, m] += term_r
                probe_sum[1, m] += term_i
        for part, term in enumerate((object_r, object_i)):
            term = pltpu.roll(term, col0, 1)
            grad_left[part, rows, :] += jnp.where(in_left[slot], term, 0.0)
            grad_right[part, rows, :] += jnp.where(in_left[slot], 0.0, term)
    own_grad[...] = grad_left[:, :edge]
    below_grad[...] = present(has_below, grad_left[:, edge:])
    right_grads[0] = present(has_right, grad_right[:, :edge])
    right_grads[1] = present(has_diag, grad_right[:, edge:])
    flat = probe_sum.reshape(2 * modes * edge, edge)
    pieces, depth = keep.shape[0], keep.shape[1]
    for target, half in ((keep, place[0]), (send, 1 - place[0])):
        for position in range(pieces):
            chunk = half * pieces + jnp.bitwise_xor(place[1], position)
            rows = pl.ds(pl.multiple_of(chunk * depth, depth), depth)
            target[position] = flat[rows, :] * scale


def join_kernel(place, own_grad, left, above, *refs):
    pieces, (out, object_grad, total, semaphores) = refs[:-4], refs[-4:]
    count, depth = len(pieces) // 2, pieces[0].shape[0]
    copies = []
    for index, piece in enumerate(pieces):
        half = place[0] if index < count else 1 - place[0]
        chunk = half * count + jnp.bitwise_xor(place[1], index % count)
        rows = pl.ds(pl.multiple_of(chunk * depth, depth), depth)
        copies.append(pltpu.make_async_copy(piece, out.at[rows, :], semaphores.at[index]))
    total[...] = own_grad[...] + left[0] + above[...]
    copies.insert(0, pltpu.make_async_copy(total, object_grad, semaphores.at[len(pieces)]))
    for copy in copies:
        copy.start()
    for copy in copies:
        copy.wait()


def on_device(object_tiles, probe, amplitudes, offsets, counts):
    modes, edge = probe.shape[1], probe.shape[2]
    slot_total = amplitudes.shape[1]
    n_region, n_pos = lax.axis_size("region"), lax.axis_size("pos")
    total = n_region * n_pos
    axes = ("region", "pos")
    f32 = jnp.float32

    row_index, column_index = lax.axis_index("region"), lax.axis_index("pos")

    def shifted(block, down, across):
        route = [
            (i * n_pos + j, (i + down) % n_region * n_pos + (j + across) % n_pos)
            for i in range(n_region)
            for j in range(n_pos)
        ]
        return lax.ppermute(block, axes, route)

    pieces = n_pos // 2

    def partner(block, mask):
        return lax.ppermute(block, axes, [(i, i ^ mask) for i in range(total)])

    place = jnp.stack(
        [
            column_index & 1,
            column_index >> 1,
            (row_index < n_region - 1).astype(jnp.int32),
            (column_index < n_pos - 1).astype(jnp.int32),
        ]
    )

    below = shifted(object_tiles, -1, 0)
    right = shifted(object_tiles, 0, -1)
    diag = shifted(object_tiles, -1, -1)

    lines = 2 * modes * edge
    smem = pl.BlockSpec(memory_space=pltpu.SMEM)
    vmem = pl.BlockSpec(memory_space=pltpu.VMEM)
    held = jnp.concatenate(
        [
            probe.reshape(2, -1, edge),
            amplitudes.reshape(2, -1, edge),
            jnp.asarray(dft_tables(edge)),
        ],
        axis=1,
    )
    quadrant = jax.ShapeDtypeStruct((2, edge, edge), f32)
    part = jax.ShapeDtypeStruct((pieces, lines // n_pos, edge), f32)
    scale = 1.0 / math.sqrt(total * slot_total)
    own_grad, below_grad, right_grads, keep, send = pl.pallas_call(
        functools.partial(slots_kernel, scale, modes, slot_total, edge),
        out_shape=(quadrant, quadrant, jax.ShapeDtypeStruct((2, 2, edge, edge), f32), part, part),
        in_specs=[pl.BlockSpec(memory_space=pl.ANY)] * 2 + [smem] + [vmem] * 5,
        out_specs=(vmem,) * 5,
        scratch_shapes=[pltpu.VMEM((4, 2 * edge, 2 * edge), jnp.bfloat16)]
        + [pltpu.VMEM((2, 2 * edge, edge), f32)] * 4
        + [
            pltpu.VMEM((2, modes, edge, edge), f32),
            pltpu.SMEM(offsets.shape, jnp.int32),
            pltpu.SMEM(counts.shape, jnp.int32),
            pltpu.SemaphoreType.DMA((2,)),
        ],
        compiler_params=pltpu.CompilerParams(vmem_limit_bytes=16 * 1024 * 1024),
    )(offsets, counts, place, held, object_tiles, below, right, diag)

    half = keep + partner(send, 1)
    got = [partner(half[k], 2 * k) for k in range(1, pieces)]
    got[0], right_grads = lax.optimization_barrier((got[0], right_grads))
    left = shifted(right_grads, 0, 1)
    chunk = functools.reduce(jnp.add, got, half[0])
    terms = [chunk] + [partner(chunk, n_pos * k) for k in range(1, n_region)]
    while len(terms) > 1:
        terms = [terms[k] + terms[k + 1] for k in range(0, len(terms), 2)]
    chunk = terms[0]
    chunk, left = lax.optimization_barrier((chunk, left))
    above = shifted(below_grad + left[1], 1, 0)
    gathered = [chunk] + [partner(chunk, 2 * k) for k in range(1, pieces)]
    gathered += [partner(piece, 1) for piece in gathered]
    probe_grad, object_grad = pl.pallas_call(
        join_kernel,
        out_shape=(jax.ShapeDtypeStruct((lines, edge), f32), quadrant),
        in_specs=[smem] + [vmem] * (3 + n_pos),
        out_specs=(pl.BlockSpec(memory_space=pl.ANY),) * 2,
        scratch_shapes=[pltpu.VMEM((2, edge, edge), f32), pltpu.SemaphoreType.DMA((n_pos + 1,))],
        compiler_params=pltpu.CompilerParams(vmem_limit_bytes=4 * 1024 * 1024),
    )(place, own_grad, left, above, *gathered)
    return (object_grad, probe_grad.reshape(probe.shape))


def solution(mesh):
    return jax.shard_map(
        on_device,
        mesh=mesh,
        in_specs=(
            P(None, "region", "pos"),
            P(),
            P("region", "pos", None, None),
            P("region", None, "pos"),
            P("region", "pos"),
        ),
        out_specs=(P(None, "region", "pos"), P()),
        check_vma=False,
    )
```

```python
import functools
import math

import jax
import jax.numpy as jnp
import numpy as np
from jax import lax
from jax.experimental import pallas as pl
from jax.experimental.pallas import tpu as pltpu
from jax.sharding import PartitionSpec as P


def dft_tables(order):
    index = np.arange(order)
    angle = (index[:, None] * index[None, :] % order) * (2.0 * math.pi / order)
    tables = np.stack([np.cos(angle), np.sin(angle)]) / math.sqrt(order)
    return tables.astype(np.float32)


def split(value):
    high = value.astype(jnp.bfloat16)
    low = (value - high.astype(jnp.float32)).astype(jnp.bfloat16)
    return high, low


def dot(a, b):
    return jnp.dot(a, b, preferred_element_type=jnp.float32)


def times_table(value, table_high, table_low):
    high, low = split(value)
    return dot(high, table_high) + (dot(low, table_high) + dot(high, table_low))


def table_times(table_high, table_low, value):
    high, low = split(value)
    return dot(table_high, high) + (dot(table_high, low) + dot(table_low, high))


def slots_kernel(
    scale, modes, slot_total, edge, offsets, counts, place, held, own, below, right, diag,
    own_grad, below_grad, right_grads, keep, send,
    tables, field_left, field_right, grad_left, grad_right, probe_sum, corners, live, semaphores,
):
    scalars = (
        pltpu.make_async_copy(offsets, corners, semaphores.at[0]),
        pltpu.make_async_copy(counts, live, semaphores.at[1]),
    )
    for copy in scalars:
        copy.start()

    def probe(part, mode):
        return held[part, pl.ds(mode * edge, edge), :]

    amplitude_rows = modes * edge
    table_rows = amplitude_rows + slot_total * edge // 2
    cos_high, cos_low = split(held[0, pl.ds(table_rows, edge), :])
    sin_high, sin_low = split(held[1, pl.ds(table_rows, edge), :])
    spread_high, spread_low, turn_high, turn_low = (tables.at[k] for k in range(4))
    for spread, turn, cos_part, sin_part in (
        (spread_high, turn_high, cos_high, sin_high),
        (spread_low, turn_low, cos_low, sin_low),
    ):
        for target, upper, lower in ((spread, -sin_part, sin_part), (turn, sin_part, -sin_part)):
            target[:edge, :edge] = cos_part
            target[:edge, edge:] = upper
            target[edge:, :edge] = lower
            target[edge:, edge:] = cos_part
    has_below, has_right = place[2] > 0, place[3] > 0
    has_diag = jnp.logical_and(has_below, has_right)

    def present(flag, value):
        return jnp.where(flag, value, jnp.zeros_like(value))

    field_left[:, :edge] = own[...].astype(jnp.float32)
    field_left[:, edge:] = present(has_below, below[...].astype(jnp.float32))
    field_right[:, :edge] = present(has_right, right[...].astype(jnp.float32))
    field_right[:, edge:] = present(has_diag, diag[...].astype(jnp.float32))
    grad_left[...] = jnp.zeros_like(grad_left)
    grad_right[...] = jnp.zeros_like(grad_right)
    lane = lax.broadcasted_iota(jnp.int32, (edge, edge), 1)
    for copy in scalars:
        copy.wait()
    slots = range(slot_total)
    corner = [(corners[0, 0, slot], corners[0, 1, slot]) for slot in slots]
    in_left = [lane >= col0 for _, col0 in corner]
    crops, halves = [], []
    for slot in slots:
        row0, col0 = corner[slot]
        rows, shift = pl.ds(row0, edge), lax.rem(edge - col0, edge)
        crop_r, crop_i = (
            pltpu.roll(
                jnp.where(in_left[slot], field_left[part, rows, :], field_right[part, rows, :]), shift, 1
            )
            for part in range(2)
        )
        exits = [
            jnp.concatenate(
                [
                    probe(0, m) * crop_r - probe(1, m) * crop_i,
                    probe(0, m) * crop_i + probe(1, m) * crop_r,
                ],
                axis=1,
            )
            for m in range(modes)
        ]
        crops.append((crop_r, crop_i))
        halves.append(times_table(jnp.concatenate(exits, axis=0), spread_high[...], spread_low[...]))
    fars = []
    for half in halves:
        parts = [
            [half[m * edge : (m + 1) * edge, part * edge : (part + 1) * edge] for m in range(modes)]
            for part in range(2)
        ]
        half = jnp.concatenate([jnp.concatenate(part, axis=1) for part in parts], axis=0)
        fars.append(table_times(turn_high[...], turn_low[...], half))
    halves = []
    for slot in slots:
        far = fars[slot]
        squares = far * far
        squares = squares[:edge] + squares[edge:]
        intensity = functools.reduce(
            jnp.add, [squares[:, m * edge : (m + 1) * edge] for m in range(modes)]
        )
        weight = (slot < live[0, 0]).astype(jnp.float32)
        half_slots = slot_total // 2
        amplitude = held[slot // half_slots, pl.ds(amplitude_rows + slot % half_slots * edge, edge), :]
        factor = weight * (1.0 - amplitude * lax.rsqrt(intensity + 1.0))
        factor = jnp.concatenate([factor] * modes, axis=1)
        residual = far * jnp.concatenate([factor, factor], axis=0)
        halves.append(table_times(spread_high[...], spread_low[...], residual))
    backs = []
    for half in halves:
        parts = [
            [half[part * edge : (part + 1) * edge, m * edge : (m + 1) * edge] for part in range(2)]
            for m in range(modes)
        ]
        half = jnp.concatenate([jnp.concatenate(part, axis=1) for part in parts], axis=0)
        backs.append(times_table(half, turn_high[...], turn_low[...]))
    for slot in slots:
        crop_r, crop_i = crops[slot]
        row0, col0 = corner[slot]
        rows = pl.ds(row0, edge)
        object_r = jnp.zeros((edge, edge), jnp.float32)
        object_i = jnp.zeros((edge, edge), jnp.float32)
        for m in range(modes):
            back_r = backs[slot][m * edge : (m + 1) * edge, :edge]
            back_i = backs[slot][m * edge : (m + 1) * edge, edge:]
            object_r += probe(0, m) * back_r + probe(1, m) * back_i
            object_i += probe(0, m) * back_i - probe(1, m) * back_r
            term_r = crop_r * back_r + crop_i * back_i
            term_i = crop_r * back_i - crop_i * back_r
            if slot == 0:
                probe_sum[0, m] = term_r
                probe_sum[1, m] = term_i
            else:
                probe_sum[0, m] += term_r
                probe_sum[1, m] += term_i
        for part, term in enumerate((object_r, object_i)):
            term = pltpu.roll(term, col0, 1)
            grad_left[part, rows, :] += jnp.where(in_left[slot], term, 0.0)
            grad_right[part, rows, :] += jnp.where(in_left[slot], 0.0, term)
    own_grad[...] = grad_left[:, :edge]
    below_grad[...] = present(has_below, grad_left[:, edge:])
    right_grads[0] = present(has_right, grad_right[:, :edge])
    right_grads[1] = present(has_diag, grad_right[:, edge:])
    flat = probe_sum.reshape(2 * modes * edge, edge)
    pieces, depth = keep.shape[0], keep.shape[1]
    for target, half in ((keep, place[0]), (send, 1 - place[0])):
        for position in range(pieces):
            chunk = half * pieces + jnp.bitwise_xor(place[1], position)
            rows = pl.ds(pl.multiple_of(chunk * depth, depth), depth)
            target[position] = flat[rows, :] * scale


def join_kernel(place, own_grad, left, above, *refs):
    pieces, (out, object_grad, total, semaphores) = refs[:-4], refs[-4:]
    count, depth = len(pieces) // 2, pieces[0].shape[0]
    copies = []
    for index, piece in enumerate(pieces):
        half = place[0] if index < count else 1 - place[0]
        chunk = half * count + jnp.bitwise_xor(place[1], index % count)
        rows = pl.ds(pl.multiple_of(chunk * depth, depth), depth)
        copies.append(pltpu.make_async_copy(piece, out.at[rows, :], semaphores.at[index]))
    total[...] = own_grad[...] + left[0] + above[...]
    copies.insert(0, pltpu.make_async_copy(total, object_grad, semaphores.at[len(pieces)]))
    for copy in copies:
        copy.start()
    for copy in copies:
        copy.wait()


def on_device(object_tiles, probe, amplitudes, offsets, counts):
    modes, edge = probe.shape[1], probe.shape[2]
    slot_total = amplitudes.shape[1]
    n_region, n_pos = lax.axis_size("region"), lax.axis_size("pos")
    total = n_region * n_pos
    axes = ("region", "pos")
    f32 = jnp.float32

    row_index, column_index = lax.axis_index("region"), lax.axis_index("pos")

    def shifted(block, down, across):
        route = [
            (i * n_pos + j, (i + down) % n_region * n_pos + (j + across) % n_pos)
            for i in range(n_region)
            for j in range(n_pos)
        ]
        return lax.ppermute(block, axes, route)

    pieces = n_pos // 2

    def partner(block, mask):
        return lax.ppermute(block, axes, [(i, i ^ mask) for i in range(total)])

    place = jnp.stack(
        [
            column_index & 1,
            column_index >> 1,
            (row_index < n_region - 1).astype(jnp.int32),
            (column_index < n_pos - 1).astype(jnp.int32),
        ]
    )

    def swapped(block, first):
        route = []
        for i in range(n_region):
            a = i + 1 if (i - first) % 2 == 0 else i - 1
            a = a if 0 <= a < n_region else i
            route += [(i * n_pos + j, a * n_pos + j) for j in range(n_pos)]
        return lax.ppermute(block, axes, route)

    right = shifted(object_tiles, 0, -1)
    below = jnp.where(row_index % 2 == 0, swapped(object_tiles, 0), swapped(object_tiles, 1))
    diag = shifted(below, 0, -1)

    lines = 2 * modes * edge
    smem = pl.BlockSpec(memory_space=pltpu.SMEM)
    vmem = pl.BlockSpec(memory_space=pltpu.VMEM)
    held = jnp.concatenate(
        [
            probe.reshape(2, -1, edge),
            amplitudes.reshape(2, -1, edge),
            jnp.asarray(dft_tables(edge)),
        ],
        axis=1,
    )
    quadrant = jax.ShapeDtypeStruct((2, edge, edge), f32)
    part = jax.ShapeDtypeStruct((pieces, lines // n_pos, edge), f32)
    scale = 1.0 / math.sqrt(total * slot_total)
    own_grad, below_grad, right_grads, keep, send = pl.pallas_call(
        functools.partial(slots_kernel, scale, modes, slot_total, edge),
        out_shape=(quadrant, quadrant, jax.ShapeDtypeStruct((2, 2, edge, edge), f32), part, part),
        in_specs=[pl.BlockSpec(memory_space=pl.ANY)] * 2 + [smem] + [vmem] * 5,
        out_specs=(vmem,) * 5,
        scratch_shapes=[pltpu.VMEM((4, 2 * edge, 2 * edge), jnp.bfloat16)]
        + [pltpu.VMEM((2, 2 * edge, edge), f32)] * 4
        + [
            pltpu.VMEM((2, modes, edge, edge), f32),
            pltpu.SMEM(offsets.shape, jnp.int32),
            pltpu.SMEM(counts.shape, jnp.int32),
            pltpu.SemaphoreType.DMA((2,)),
        ],
        compiler_params=pltpu.CompilerParams(vmem_limit_bytes=16 * 1024 * 1024),
    )(offsets, counts, place, held, object_tiles, below, right, diag)

    half, right_grads = lax.optimization_barrier((keep + partner(send, 1), right_grads))
    got = [partner(half[k], 2 * k) for k in range(1, pieces)]
    left = shifted(right_grads, 0, 1)
    chunk = functools.reduce(jnp.add, got, half[0])
    chunk, left = lax.optimization_barrier((chunk, left))
    terms = [chunk] + [partner(chunk, n_pos * k) for k in range(1, n_region)]
    while len(terms) > 1:
        terms = [terms[k] + terms[k + 1] for k in range(0, len(terms), 2)]
    chunk, below_grad = lax.optimization_barrier((terms[0], below_grad))
    above = shifted(below_grad + left[1], 1, 0)
    gathered = [chunk] + [partner(chunk, 2 * k) for k in range(1, pieces)]
    gathered += [partner(piece, 1) for piece in gathered]
    probe_grad, object_grad = pl.pallas_call(
        join_kernel,
        out_shape=(jax.ShapeDtypeStruct((lines, edge), f32), quadrant),
        in_specs=[smem] + [vmem] * (3 + n_pos),
        out_specs=(pl.BlockSpec(memory_space=pl.ANY),) * 2,
        scratch_shapes=[pltpu.VMEM((2, edge, edge), f32), pltpu.SemaphoreType.DMA((n_pos + 1,))],
        compiler_params=pltpu.CompilerParams(vmem_limit_bytes=4 * 1024 * 1024),
    )(place, own_grad, left, above, *gathered)
    return (object_grad, probe_grad.reshape(probe.shape))


def solution(mesh):
    return jax.shard_map(
        on_device,
        mesh=mesh,
        in_specs=(
            P(None, "region", "pos"),
            P(),
            P("region", "pos", None, None),
            P("region", None, "pos"),
            P("region", "pos"),
        ),
        out_specs=(P(None, "region", "pos"), P()),
        check_vma=False,
    )
```

```python
import functools
import math

import jax
import jax.numpy as jnp
import numpy as np
from jax import lax
from jax.experimental import pallas as pl
from jax.experimental.pallas import tpu as pltpu
from jax.sharding import PartitionSpec as P


def dft_tables(order):
    index = np.arange(order)
    angle = (index[:, None] * index[None, :] % order) * (2.0 * math.pi / order)
    tables = np.stack([np.cos(angle), np.sin(angle)]) / math.sqrt(order)
    return tables.astype(np.float32)


def split(value):
    high = value.astype(jnp.bfloat16)
    low = (value - high.astype(jnp.float32)).astype(jnp.bfloat16)
    return high, low


def dot(a, b):
    return jnp.dot(a, b, preferred_element_type=jnp.float32)


def times_table(value, table_high, table_low):
    high, low = split(value)
    return dot(high, table_high) + (dot(low, table_high) + dot(high, table_low))


def table_times(table_high, table_low, value):
    high, low = split(value)
    return dot(table_high, high) + (dot(table_high, low) + dot(table_low, high))


def slots_kernel(
    scale, modes, slot_total, edge, offsets, counts, place, held, own, below, right, diag,
    own_grad, below_grad, right_grads, keep, send,
    tables, field_left, field_right, grad_left, grad_right, probe_sum, corners, live, semaphores,
):
    scalars = (
        pltpu.make_async_copy(offsets, corners, semaphores.at[0]),
        pltpu.make_async_copy(counts, live, semaphores.at[1]),
    )
    for copy in scalars:
        copy.start()

    def probe(part, mode):
        return held[part, pl.ds(mode * edge, edge), :]

    amplitude_rows = modes * edge
    table_rows = amplitude_rows + slot_total * edge // 2
    cos_high, cos_low = split(held[0, pl.ds(table_rows, edge), :])
    sin_high, sin_low = split(held[1, pl.ds(table_rows, edge), :])
    spread_high, spread_low, turn_high, turn_low = (tables.at[k] for k in range(4))
    for spread, turn, cos_part, sin_part in (
        (spread_high, turn_high, cos_high, sin_high),
        (spread_low, turn_low, cos_low, sin_low),
    ):
        for target, upper, lower in ((spread, -sin_part, sin_part), (turn, sin_part, -sin_part)):
            target[:edge, :edge] = cos_part
            target[:edge, edge:] = upper
            target[edge:, :edge] = lower
            target[edge:, edge:] = cos_part
    has_below, has_right = place[2] > 0, place[3] > 0
    has_diag = jnp.logical_and(has_below, has_right)

    def present(flag, value):
        return jnp.where(flag, value, jnp.zeros_like(value))

    field_left[:, :edge] = own[...].astype(jnp.float32)
    field_left[:, edge:] = present(has_below, below[...].astype(jnp.float32))
    field_right[:, :edge] = present(has_right, right[...].astype(jnp.float32))
    field_right[:, edge:] = present(has_diag, diag[...].astype(jnp.float32))
    grad_left[...] = jnp.zeros_like(grad_left)
    grad_right[...] = jnp.zeros_like(grad_right)
    lane = lax.broadcasted_iota(jnp.int32, (edge, edge), 1)
    for copy in scalars:
        copy.wait()
    slots = range(slot_total)
    corner = [(corners[0, 0, slot], corners[0, 1, slot]) for slot in slots]
    in_left = [lane >= col0 for _, col0 in corner]
    crops, halves = [], []
    for slot in slots:
        row0, col0 = corner[slot]
        rows, shift = pl.ds(row0, edge), lax.rem(edge - col0, edge)
        crop_r, crop_i = (
            pltpu.roll(
                jnp.where(in_left[slot], field_left[part, rows, :], field_right[part, rows, :]), shift, 1
            )
            for part in range(2)
        )
        exits = [
            jnp.concatenate(
                [
                    probe(0, m) * crop_r - probe(1, m) * crop_i,
                    probe(0, m) * crop_i + probe(1, m) * crop_r,
                ],
                axis=1,
            )
            for m in range(modes)
        ]
        crops.append((crop_r, crop_i))
        halves.append(times_table(jnp.concatenate(exits, axis=0), spread_high[...], spread_low[...]))
    fars = []
    for half in halves:
        parts = [
            [half[m * edge : (m + 1) * edge, part * edge : (part + 1) * edge] for m in range(modes)]
            for part in range(2)
        ]
        half = jnp.concatenate([jnp.concatenate(part, axis=1) for part in parts], axis=0)
        fars.append(table_times(turn_high[...], turn_low[...], half))
    halves = []
    for slot in slots:
        far = fars[slot]
        squares = far * far
        squares = squares[:edge] + squares[edge:]
        intensity = functools.reduce(
            jnp.add, [squares[:, m * edge : (m + 1) * edge] for m in range(modes)]
        )
        weight = (slot < live[0, 0]).astype(jnp.float32)
        half_slots = slot_total // 2
        amplitude = held[slot // half_slots, pl.ds(amplitude_rows + slot % half_slots * edge, edge), :]
        factor = weight * (1.0 - amplitude * lax.rsqrt(intensity + 1.0))
        factor = jnp.concatenate([factor] * modes, axis=1)
        residual = far * jnp.concatenate([factor, factor], axis=0)
        halves.append(table_times(spread_high[...], spread_low[...], residual))
    backs = []
    for half in halves:
        parts = [
            [half[part * edge : (part + 1) * edge, m * edge : (m + 1) * edge] for part in range(2)]
            for m in range(modes)
        ]
        half = jnp.concatenate([jnp.concatenate(part, axis=1) for part in parts], axis=0)
        backs.append(times_table(half, turn_high[...], turn_low[...]))
    for slot in slots:
        crop_r, crop_i = crops[slot]
        row0, col0 = corner[slot]
        rows = pl.ds(row0, edge)
        object_r = jnp.zeros((edge, edge), jnp.float32)
        object_i = jnp.zeros((edge, edge), jnp.float32)
        for m in range(modes):
            back_r = backs[slot][m * edge : (m + 1) * edge, :edge]
            back_i = backs[slot][m * edge : (m + 1) * edge, edge:]
            object_r += probe(0, m) * back_r + probe(1, m) * back_i
            object_i += probe(0, m) * back_i - probe(1, m) * back_r
            term_r = crop_r * back_r + crop_i * back_i
            term_i = crop_r * back_i - crop_i * back_r
            if slot == 0:
                probe_sum[0, m] = term_r
                probe_sum[1, m] = term_i
            else:
                probe_sum[0, m] += term_r
                probe_sum[1, m] += term_i
        for part, term in enumerate((object_r, object_i)):
            term = pltpu.roll(term, col0, 1)
            grad_left[part, rows, :] += jnp.where(in_left[slot], term, 0.0)
            grad_right[part, rows, :] += jnp.where(in_left[slot], 0.0, term)
    own_grad[...] = grad_left[:, :edge]
    below_grad[...] = present(has_below, grad_left[:, edge:])
    right_grads[0] = present(has_right, grad_right[:, :edge])
    right_grads[1] = present(has_diag, grad_right[:, edge:])
    flat = probe_sum.reshape(2 * modes * edge, edge)
    pieces, depth = keep.shape[0], keep.shape[1]
    for target, half in ((keep, place[0]), (send, 1 - place[0])):
        for position in range(pieces):
            chunk = half * pieces + jnp.bitwise_xor(place[1], position)
            rows = pl.ds(pl.multiple_of(chunk * depth, depth), depth)
            target[position] = flat[rows, :] * scale


def join_kernel(place, own_grad, left, above, *refs):
    pieces, (out, object_grad, total, semaphores) = refs[:-4], refs[-4:]
    count, depth = len(pieces) // 2, pieces[0].shape[0]
    copies = []
    for index, piece in enumerate(pieces):
        half = place[0] if index < count else 1 - place[0]
        chunk = half * count + jnp.bitwise_xor(place[1], index % count)
        rows = pl.ds(pl.multiple_of(chunk * depth, depth), depth)
        copies.append(pltpu.make_async_copy(piece, out.at[rows, :], semaphores.at[index]))
    total[...] = own_grad[...] + left[0] + above[...]
    copies.insert(0, pltpu.make_async_copy(total, object_grad, semaphores.at[len(pieces)]))
    for copy in copies:
        copy.start()
    for copy in copies:
        copy.wait()


def on_device(object_tiles, probe, amplitudes, offsets, counts):
    modes, edge = probe.shape[1], probe.shape[2]
    slot_total = amplitudes.shape[1]
    n_region, n_pos = lax.axis_size("region"), lax.axis_size("pos")
    total = n_region * n_pos
    axes = ("region", "pos")
    f32 = jnp.float32

    row_index, column_index = lax.axis_index("region"), lax.axis_index("pos")

    def shifted(block, down, across, closed=True):
        route = [
            (i * n_pos + j, (i + down) % n_region * n_pos + (j + across) % n_pos)
            for i in range(n_region)
            for j in range(n_pos)
            if closed or (0 <= i + down < n_region and 0 <= j + across < n_pos)
        ]
        return lax.ppermute(block, axes, route)

    pieces = n_pos // 2

    def partner(block, mask):
        return lax.ppermute(block, axes, [(i, i ^ mask) for i in range(total)])

    place = jnp.stack(
        [
            column_index & 1,
            column_index >> 1,
            (row_index < n_region - 1).astype(jnp.int32),
            (column_index < n_pos - 1).astype(jnp.int32),
        ]
    )

    below = shifted(object_tiles, -1, 0, closed=False)
    right = shifted(object_tiles, 0, -1)
    diag = shifted(object_tiles, -1, -1, closed=False)

    lines = 2 * modes * edge
    smem = pl.BlockSpec(memory_space=pltpu.SMEM)
    vmem = pl.BlockSpec(memory_space=pltpu.VMEM)
    held = jnp.concatenate(
        [
            probe.reshape(2, -1, edge),
            amplitudes.reshape(2, -1, edge),
            jnp.asarray(dft_tables(edge)),
        ],
        axis=1,
    )
    quadrant = jax.ShapeDtypeStruct((2, edge, edge), f32)
    part = jax.ShapeDtypeStruct((pieces, lines // n_pos, edge), f32)
    scale = 1.0 / math.sqrt(total * slot_total)
    own_grad, below_grad, right_grads, keep, send = pl.pallas_call(
        functools.partial(slots_kernel, scale, modes, slot_total, edge),
        out_shape=(quadrant, quadrant, jax.ShapeDtypeStruct((2, 2, edge, edge), f32), part, part),
        in_specs=[pl.BlockSpec(memory_space=pl.ANY)] * 2 + [smem] + [vmem] * 5,
        out_specs=(vmem,) * 5,
        scratch_shapes=[pltpu.VMEM((4, 2 * edge, 2 * edge), jnp.bfloat16)]
        + [pltpu.VMEM((2, 2 * edge, edge), f32)] * 4
        + [
            pltpu.VMEM((2, modes, edge, edge), f32),
            pltpu.SMEM(offsets.shape, jnp.int32),
            pltpu.SMEM(counts.shape, jnp.int32),
            pltpu.SemaphoreType.DMA((2,)),
        ],
        compiler_params=pltpu.CompilerParams(vmem_limit_bytes=16 * 1024 * 1024),
    )(offsets, counts, place, held, object_tiles, below, right, diag)

    half = keep + partner(send, 1)
    got = [partner(half[k], 2 * k) for k in range(1, pieces)]
    got[0], right_grads = lax.optimization_barrier((got[0], right_grads))
    left = shifted(right_grads, 0, 1)
    chunk = functools.reduce(jnp.add, got, half[0])
    terms = [chunk] + [partner(chunk, n_pos * k) for k in range(1, n_region)]
    while len(terms) > 1:
        terms = [terms[k] + terms[k + 1] for k in range(0, len(terms), 2)]
    chunk = terms[0]
    chunk, left = lax.optimization_barrier((chunk, left))
    above = shifted(below_grad + left[1], 1, 0)
    gathered = [chunk] + [partner(chunk, 2 * k) for k in range(1, pieces)]
    gathered += [partner(piece, 1) for piece in gathered]
    probe_grad, object_grad = pl.pallas_call(
        join_kernel,
        out_shape=(jax.ShapeDtypeStruct((lines, edge), f32), quadrant),
        in_specs=[smem] + [vmem] * (3 + n_pos),
        out_specs=(pl.BlockSpec(memory_space=pl.ANY),) * 2,
        scratch_shapes=[pltpu.VMEM((2, edge, edge), f32), pltpu.SemaphoreType.DMA((n_pos + 1,))],
        compiler_params=pltpu.CompilerParams(vmem_limit_bytes=4 * 1024 * 1024),
    )(place, own_grad, left, above, *gathered)
    return (object_grad, probe_grad.reshape(probe.shape))


def solution(mesh):
    return jax.shard_map(
        on_device,
        mesh=mesh,
        in_specs=(
            P(None, "region", "pos"),
            P(),
            P("region", "pos", None, None),
            P("region", None, "pos"),
            P("region", "pos"),
        ),
        out_specs=(P(None, "region", "pos"), P()),
        check_vma=False,
    )
```

```python
import functools
import math

import jax
import jax.numpy as jnp
import numpy as np
from jax import lax
from jax.experimental import pallas as pl
from jax.experimental.pallas import tpu as pltpu
from jax.sharding import PartitionSpec as P


def dft_tables(order):
    index = np.arange(order)
    angle = (index[:, None] * index[None, :] % order) * (2.0 * math.pi / order)
    tables = np.stack([np.cos(angle), np.sin(angle)]) / math.sqrt(order)
    return tables.astype(np.float32)


def split(value):
    high = value.astype(jnp.bfloat16)
    low = (value - high.astype(jnp.float32)).astype(jnp.bfloat16)
    return high, low


def dot(a, b):
    return jnp.dot(a, b, preferred_element_type=jnp.float32)


def times_table(value, table_high, table_low):
    high, low = split(value)
    return dot(high, table_high) + (dot(low, table_high) + dot(high, table_low))


def table_times(table_high, table_low, value):
    high, low = split(value)
    return dot(table_high, high) + (dot(table_high, low) + dot(table_low, high))


def slots_kernel(
    scale, modes, slot_total, edge, offsets, counts, place, held, own, below, right, diag,
    own_grad, below_grad, right_grads, keep, send,
    tables, field_left, field_right, grad_left, grad_right, probe_sum, corners, live, semaphores,
):
    scalars = (
        pltpu.make_async_copy(offsets, corners, semaphores.at[0]),
        pltpu.make_async_copy(counts, live, semaphores.at[1]),
    )
    for copy in scalars:
        copy.start()

    def probe(part, mode):
        return held[part, pl.ds(mode * edge, edge), :]

    amplitude_rows = modes * edge
    table_rows = amplitude_rows + slot_total * edge // 2
    cos_high, cos_low = split(held[0, pl.ds(table_rows, edge), :])
    sin_high, sin_low = split(held[1, pl.ds(table_rows, edge), :])
    spread_high, spread_low, turn_high, turn_low = (tables.at[k] for k in range(4))
    for spread, turn, cos_part, sin_part in (
        (spread_high, turn_high, cos_high, sin_high),
        (spread_low, turn_low, cos_low, sin_low),
    ):
        for target, upper, lower in ((spread, -sin_part, sin_part), (turn, sin_part, -sin_part)):
            target[:edge, :edge] = cos_part
            target[:edge, edge:] = upper
            target[edge:, :edge] = lower
            target[edge:, edge:] = cos_part
    has_below, has_right = place[2] > 0, place[3] > 0
    has_diag = jnp.logical_and(has_below, has_right)

    def present(flag, value):
        return jnp.where(flag, value, jnp.zeros_like(value))

    field_left[:, :edge] = own[...].astype(jnp.float32)
    field_left[:, edge:] = present(has_below, below[...].astype(jnp.float32))
    field_right[:, :edge] = present(has_right, right[...].astype(jnp.float32))
    field_right[:, edge:] = present(has_diag, diag[...].astype(jnp.float32))
    grad_left[...] = jnp.zeros_like(grad_left)
    grad_right[...] = jnp.zeros_like(grad_right)
    lane = lax.broadcasted_iota(jnp.int32, (edge, edge), 1)
    for copy in scalars:
        copy.wait()
    slots = range(slot_total)
    corner = [(corners[0, 0, slot], corners[0, 1, slot]) for slot in slots]
    in_left = [lane >= col0 for _, col0 in corner]
    crops, halves = [], []
    for slot in slots:
        row0, col0 = corner[slot]
        rows, shift = pl.ds(row0, edge), lax.rem(edge - col0, edge)
        crop_r, crop_i = (
            pltpu.roll(
                jnp.where(in_left[slot], field_left[part, rows, :], field_right[part, rows, :]), shift, 1
            )
            for part in range(2)
        )
        exits = [
            jnp.concatenate(
                [
                    probe(0, m) * crop_r - probe(1, m) * crop_i,
                    probe(0, m) * crop_i + probe(1, m) * crop_r,
                ],
                axis=1,
            )
            for m in range(modes)
        ]
        crops.append((crop_r, crop_i))
        halves.append(times_table(jnp.concatenate(exits, axis=0), spread_high[...], spread_low[...]))
    fars = []
    for half in halves:
        parts = [
            [half[m * edge : (m + 1) * edge, part * edge : (part + 1) * edge] for m in range(modes)]
            for part in range(2)
        ]
        half = jnp.concatenate([jnp.concatenate(part, axis=1) for part in parts], axis=0)
        fars.append(table_times(turn_high[...], turn_low[...], half))
    halves = []
    for slot in slots:
        far = fars[slot]
        squares = far * far
        squares = squares[:edge] + squares[edge:]
        intensity = functools.reduce(
            jnp.add, [squares[:, m * edge : (m + 1) * edge] for m in range(modes)]
        )
        weight = (slot < live[0, 0]).astype(jnp.float32)
        half_slots = slot_total // 2
        amplitude = held[slot // half_slots, pl.ds(amplitude_rows + slot % half_slots * edge, edge), :]
        factor = weight * (1.0 - amplitude * lax.rsqrt(intensity + 1.0))
        factor = jnp.concatenate([factor] * modes, axis=1)
        residual = far * jnp.concatenate([factor, factor], axis=0)
        halves.append(table_times(spread_high[...], spread_low[...], residual))
    backs = []
    for half in halves:
        parts = [
            [half[part * edge : (part + 1) * edge, m * edge : (m + 1) * edge] for part in range(2)]
            for m in range(modes)
        ]
        half = jnp.concatenate([jnp.concatenate(part, axis=1) for part in parts], axis=0)
        backs.append(times_table(half, turn_high[...], turn_low[...]))
    for slot in slots:
        crop_r, crop_i = crops[slot]
        row0, col0 = corner[slot]
        rows = pl.ds(row0, edge)
        object_r = jnp.zeros((edge, edge), jnp.float32)
        object_i = jnp.zeros((edge, edge), jnp.float32)
        for m in range(modes):
            back_r = backs[slot][m * edge : (m + 1) * edge, :edge]
            back_i = backs[slot][m * edge : (m + 1) * edge, edge:]
            object_r += probe(0, m) * back_r + probe(1, m) * back_i
            object_i += probe(0, m) * back_i - probe(1, m) * back_r
            term_r = crop_r * back_r + crop_i * back_i
            term_i = crop_r * back_i - crop_i * back_r
            if slot == 0:
                probe_sum[0, m] = term_r
                probe_sum[1, m] = term_i
            else:
                probe_sum[0, m] += term_r
                probe_sum[1, m] += term_i
        for part, term in enumerate((object_r, object_i)):
            term = pltpu.roll(term, col0, 1)
            grad_left[part, rows, :] += jnp.where(in_left[slot], term, 0.0)
            grad_right[part, rows, :] += jnp.where(in_left[slot], 0.0, term)
    own_grad[...] = grad_left[:, :edge]
    below_grad[...] = present(has_below, grad_left[:, edge:])
    right_grads[0] = present(has_right, grad_right[:, :edge])
    right_grads[1] = present(has_diag, grad_right[:, edge:])
    flat = probe_sum.reshape(2 * modes * edge, edge)
    pieces, depth = keep.shape[0], keep.shape[1]
    for target, half in ((keep, place[0]), (send, 1 - place[0])):
        for position in range(pieces):
            chunk = half * pieces + jnp.bitwise_xor(place[1], position)
            rows = pl.ds(pl.multiple_of(chunk * depth, depth), depth)
            target[position] = flat[rows, :] * scale


def join_kernel(place, own_grad, left, above, *refs):
    pieces, (out, object_grad, total, semaphores) = refs[:-4], refs[-4:]
    count, depth = len(pieces) // 2, pieces[0].shape[0]
    copies = []
    for index, piece in enumerate(pieces):
        half = place[0] if index < count else 1 - place[0]
        chunk = half * count + jnp.bitwise_xor(place[1], index % count)
        rows = pl.ds(pl.multiple_of(chunk * depth, depth), depth)
        copies.append(pltpu.make_async_copy(piece, out.at[rows, :], semaphores.at[index]))
    total[...] = own_grad[...] + left[0] + above[...]
    copies.insert(0, pltpu.make_async_copy(total, object_grad, semaphores.at[len(pieces)]))
    for copy in copies:
        copy.start()
    for copy in copies:
        copy.wait()


def on_device(object_tiles, probe, amplitudes, offsets, counts):
    modes, edge = probe.shape[1], probe.shape[2]
    slot_total = amplitudes.shape[1]
    n_region, n_pos = lax.axis_size("region"), lax.axis_size("pos")
    total = n_region * n_pos
    axes = ("region", "pos")
    f32 = jnp.float32

    row_index, column_index = lax.axis_index("region"), lax.axis_index("pos")

    def shifted(block, down, across):
        route = [
            (i * n_pos + j, (i + down) % n_region * n_pos + (j + across) % n_pos)
            for i in range(n_region)
            for j in range(n_pos)
        ]
        return lax.ppermute(block, axes, route)

    pieces = n_pos // 2

    def partner(block, mask):
        return lax.ppermute(block, axes, [(i, i ^ mask) for i in range(total)])

    place = jnp.stack(
        [
            column_index & 1,
            column_index >> 1,
            (row_index < n_region - 1).astype(jnp.int32),
            (column_index < n_pos - 1).astype(jnp.int32),
        ]
    )

    def swapped(block, first):
        route = []
        for i in range(n_region):
            a = i + 1 if (i - first) % 2 == 0 else i - 1
            for j in range(n_pos):
                route.append((i * n_pos + j, a * n_pos + j if 0 <= a < n_region else i * n_pos + (j ^ 1)))
        return lax.ppermute(block, axes, route)

    right = shifted(object_tiles, 0, -1)
    below = jnp.where(row_index % 2 == 0, swapped(object_tiles, 0), swapped(object_tiles, 1))
    diag = shifted(below, 0, -1)

    lines = 2 * modes * edge
    smem = pl.BlockSpec(memory_space=pltpu.SMEM)
    vmem = pl.BlockSpec(memory_space=pltpu.VMEM)
    held = jnp.concatenate(
        [
            probe.reshape(2, -1, edge),
            amplitudes.reshape(2, -1, edge),
            jnp.asarray(dft_tables(edge)),
        ],
        axis=1,
    )
    quadrant = jax.ShapeDtypeStruct((2, edge, edge), f32)
    part = jax.ShapeDtypeStruct((pieces, lines // n_pos, edge), f32)
    scale = 1.0 / math.sqrt(total * slot_total)
    own_grad, below_grad, right_grads, keep, send = pl.pallas_call(
        functools.partial(slots_kernel, scale, modes, slot_total, edge),
        out_shape=(quadrant, quadrant, jax.ShapeDtypeStruct((2, 2, edge, edge), f32), part, part),
        in_specs=[pl.BlockSpec(memory_space=pl.ANY)] * 2 + [smem] + [vmem] * 5,
        out_specs=(vmem,) * 5,
        scratch_shapes=[pltpu.VMEM((4, 2 * edge, 2 * edge), jnp.bfloat16)]
        + [pltpu.VMEM((2, 2 * edge, edge), f32)] * 4
        + [
            pltpu.VMEM((2, modes, edge, edge), f32),
            pltpu.SMEM(offsets.shape, jnp.int32),
            pltpu.SMEM(counts.shape, jnp.int32),
            pltpu.SemaphoreType.DMA((2,)),
        ],
        compiler_params=pltpu.CompilerParams(vmem_limit_bytes=16 * 1024 * 1024),
    )(offsets, counts, place, held, object_tiles, below, right, diag)

    half = keep + partner(send, 1)
    got = [partner(half[k], 2 * k) for k in range(1, pieces)]
    got[0], right_grads = lax.optimization_barrier((got[0], right_grads))
    left = shifted(right_grads, 0, 1)
    chunk = functools.reduce(jnp.add, got, half[0])
    terms = [chunk] + [partner(chunk, n_pos * k) for k in range(1, n_region)]
    while len(terms) > 1:
        terms = [terms[k] + terms[k + 1] for k in range(0, len(terms), 2)]
    chunk = terms[0]
    chunk, left = lax.optimization_barrier((chunk, left))
    above = shifted(below_grad + left[1], 1, 0)
    gathered = [chunk] + [partner(chunk, 2 * k) for k in range(1, pieces)]
    gathered += [partner(piece, 1) for piece in gathered]
    probe_grad, object_grad = pl.pallas_call(
        join_kernel,
        out_shape=(jax.ShapeDtypeStruct((lines, edge), f32), quadrant),
        in_specs=[smem] + [vmem] * (3 + n_pos),
        out_specs=(pl.BlockSpec(memory_space=pl.ANY),) * 2,
        scratch_shapes=[pltpu.VMEM((2, edge, edge), f32), pltpu.SemaphoreType.DMA((n_pos + 1,))],
        compiler_params=pltpu.CompilerParams(vmem_limit_bytes=4 * 1024 * 1024),
    )(place, own_grad, left, above, *gathered)
    return (object_grad, probe_grad.reshape(probe.shape))


def solution(mesh):
    return jax.shard_map(
        on_device,
        mesh=mesh,
        in_specs=(
            P(None, "region", "pos"),
            P(),
            P("region", "pos", None, None),
            P("region", None, "pos"),
            P("region", "pos"),
        ),
        out_specs=(P(None, "region", "pos"), P()),
        check_vma=False,
    )
```

```python
import functools
import math

import jax
import jax.numpy as jnp
import numpy as np
from jax import lax
from jax.experimental import pallas as pl
from jax.experimental.pallas import tpu as pltpu
from jax.sharding import PartitionSpec as P


def dft_tables(order):
    index = np.arange(order)
    angle = (index[:, None] * index[None, :] % order) * (2.0 * math.pi / order)
    tables = np.stack([np.cos(angle), np.sin(angle)]) / math.sqrt(order)
    return tables.astype(np.float32)


def dot(a, b):
    return jnp.dot(a, b, precision=lax.Precision.HIGH, preferred_element_type=jnp.float32)


def slots_kernel(
    scale, modes, slot_total, edge, offsets, counts, place, held, own, diag, below, right,
    own_grad, below_grad, right_grads, keep, send,
    tables, field_left, field_right, grad_left, grad_right, probe_sum, corners, live, semaphores,
):
    scalars = (
        pltpu.make_async_copy(offsets, corners, semaphores.at[0]),
        pltpu.make_async_copy(counts, live, semaphores.at[1]),
    )
    for copy in scalars:
        copy.start()

    def probe(part, mode):
        return held[part, pl.ds(mode * edge, edge), :]

    amplitude_rows = modes * edge
    table_rows = amplitude_rows + slot_total * edge // 2
    cos_table = held[0, pl.ds(table_rows, edge), :]
    sin_table = held[1, pl.ds(table_rows, edge), :]
    spread, turn = (tables.at[k] for k in range(2))
    for target, upper, lower in ((spread, -sin_table, sin_table), (turn, sin_table, -sin_table)):
        target[:edge, :edge] = cos_table
        target[:edge, edge:] = upper
        target[edge:, :edge] = lower
        target[edge:, edge:] = cos_table
    has_below, has_right = place[2] > 0, place[3] > 0
    has_diag = jnp.logical_and(has_below, has_right)

    def present(flag, value):
        return jnp.where(flag, value, jnp.zeros_like(value))

    field_left[:, :edge] = own[...].astype(jnp.float32)
    field_left[:, edge:] = present(has_below, below[...].astype(jnp.float32))
    field_right[:, :edge] = present(has_right, right[...].astype(jnp.float32))
    field_right[:, edge:] = present(has_diag, diag[...].astype(jnp.float32))
    grad_left[...] = jnp.zeros_like(grad_left)
    grad_right[...] = jnp.zeros_like(grad_right)
    lane = lax.broadcasted_iota(jnp.int32, (edge, edge), 1)
    for copy in scalars:
        copy.wait()
    slots = range(slot_total)
    corner = [(corners[0, 0, slot], corners[0, 1, slot]) for slot in slots]
    in_left = [lane >= col0 for _, col0 in corner]
    crops, halves = [], []
    for slot in slots:
        row0, col0 = corner[slot]
        rows, shift = pl.ds(row0, edge), lax.rem(edge - col0, edge)
        crop_r, crop_i = (
            pltpu.roll(
                jnp.where(in_left[slot], field_left[part, rows, :], field_right[part, rows, :]), shift, 1
            )
            for part in range(2)
        )
        exits = [
            jnp.concatenate(
                [
                    probe(0, m) * crop_r - probe(1, m) * crop_i,
                    probe(0, m) * crop_i + probe(1, m) * crop_r,
                ],
                axis=1,
            )
            for m in range(modes)
        ]
        crops.append((crop_r, crop_i))
        halves.append(dot(jnp.concatenate(exits, axis=0), spread[...]))
    fars = []
    for half in halves:
        parts = [
            [half[m * edge : (m + 1) * edge, part * edge : (part + 1) * edge] for m in range(modes)]
            for part in range(2)
        ]
        half = jnp.concatenate([jnp.concatenate(part, axis=1) for part in parts], axis=0)
        fars.append(dot(turn[...], half))
    halves = []
    for slot in slots:
        far = fars[slot]
        squares = far * far
        squares = squares[:edge] + squares[edge:]
        intensity = functools.reduce(
            jnp.add, [squares[:, m * edge : (m + 1) * edge] for m in range(modes)]
        )
        weight = (slot < live[0, 0]).astype(jnp.float32)
        half_slots = slot_total // 2
        amplitude = held[slot // half_slots, pl.ds(amplitude_rows + slot % half_slots * edge, edge), :]
        factor = weight * (1.0 - amplitude * lax.rsqrt(intensity + 1.0))
        factor = jnp.concatenate([factor] * modes, axis=1)
        residual = far * jnp.concatenate([factor, factor], axis=0)
        halves.append(dot(spread[...], residual))
    backs = []
    for half in halves:
        parts = [
            [half[part * edge : (part + 1) * edge, m * edge : (m + 1) * edge] for part in range(2)]
            for m in range(modes)
        ]
        half = jnp.concatenate([jnp.concatenate(part, axis=1) for part in parts], axis=0)
        backs.append(dot(half, turn[...]))
    for slot in slots:
        crop_r, crop_i = crops[slot]
        row0, col0 = corner[slot]
        rows = pl.ds(row0, edge)
        object_r = jnp.zeros((edge, edge), jnp.float32)
        object_i = jnp.zeros((edge, edge), jnp.float32)
        for m in range(modes):
            back_r = backs[slot][m * edge : (m + 1) * edge, :edge]
            back_i = backs[slot][m * edge : (m + 1) * edge, edge:]
            object_r += probe(0, m) * back_r + probe(1, m) * back_i
            object_i += probe(0, m) * back_i - probe(1, m) * back_r
            term_r = crop_r * back_r + crop_i * back_i
            term_i = crop_r * back_i - crop_i * back_r
            if slot == 0:
                probe_sum[0, m] = term_r
                probe_sum[1, m] = term_i
            else:
                probe_sum[0, m] += term_r
                probe_sum[1, m] += term_i
        for part, term in enumerate((object_r, object_i)):
            term = pltpu.roll(term, col0, 1)
            grad_left[part, rows, :] += jnp.where(in_left[slot], term, 0.0)
            grad_right[part, rows, :] += jnp.where(in_left[slot], 0.0, term)
    own_grad[...] = grad_left[:, :edge]
    below_grad[...] = present(has_below, grad_left[:, edge:])
    right_grads[0] = present(has_right, grad_right[:, :edge])
    right_grads[1] = present(has_diag, grad_right[:, edge:])
    flat = probe_sum.reshape(2 * modes * edge, edge)
    pieces, depth = keep.shape[0], keep.shape[1]
    for target, half in ((keep, place[0]), (send, 1 - place[0])):
        for position in range(pieces):
            chunk = half * pieces + jnp.bitwise_xor(place[1], position)
            rows = pl.ds(pl.multiple_of(chunk * depth, depth), depth)
            target[position] = flat[rows, :] * scale


def join_kernel(place, own_grad, left, above, *refs):
    pieces, (out, object_grad, total, semaphores) = refs[:-4], refs[-4:]
    count, depth = len(pieces) // 2, pieces[0].shape[0]
    copies = []
    for index, piece in enumerate(pieces):
        half = place[0] if index < count else 1 - place[0]
        chunk = half * count + jnp.bitwise_xor(place[1], index % count)
        rows = pl.ds(pl.multiple_of(chunk * depth, depth), depth)
        copies.append(pltpu.make_async_copy(piece, out.at[rows, :], semaphores.at[index]))
    total[...] = own_grad[...] + left[0] + above[...]
    copies.insert(0, pltpu.make_async_copy(total, object_grad, semaphores.at[len(pieces)]))
    for copy in copies:
        copy.start()
    for copy in copies:
        copy.wait()


def on_device(object_tiles, probe, amplitudes, offsets, counts):
    modes, edge = probe.shape[1], probe.shape[2]
    slot_total = amplitudes.shape[1]
    n_region, n_pos = lax.axis_size("region"), lax.axis_size("pos")
    total = n_region * n_pos
    axes = ("region", "pos")
    f32 = jnp.float32

    row_index, column_index = lax.axis_index("region"), lax.axis_index("pos")

    def shifted(block, down, across):
        route = [
            (i * n_pos + j, (i + down) % n_region * n_pos + (j + across) % n_pos)
            for i in range(n_region)
            for j in range(n_pos)
        ]
        return lax.ppermute(block, axes, route)

    pieces = n_pos // 2

    def partner(block, mask):
        return lax.ppermute(block, axes, [(i, i ^ mask) for i in range(total)])

    place = jnp.stack(
        [
            column_index & 1,
            column_index >> 1,
            (row_index < n_region - 1).astype(jnp.int32),
            (column_index < n_pos - 1).astype(jnp.int32),
        ]
    )

    below = shifted(object_tiles, -1, 0)
    right = shifted(object_tiles, 0, -1)
    diag = shifted(object_tiles, -1, -1)

    lines = 2 * modes * edge
    smem = pl.BlockSpec(memory_space=pltpu.SMEM)
    vmem = pl.BlockSpec(memory_space=pltpu.VMEM)
    held = jnp.concatenate(
        [
            probe.reshape(2, -1, edge),
            amplitudes.reshape(2, -1, edge),
            jnp.asarray(dft_tables(edge)),
        ],
        axis=1,
    )
    quadrant = jax.ShapeDtypeStruct((2, edge, edge), f32)
    part = jax.ShapeDtypeStruct((pieces, lines // n_pos, edge), f32)
    scale = 1.0 / math.sqrt(total * slot_total)
    own_grad, below_grad, right_grads, keep, send = pl.pallas_call(
        functools.partial(slots_kernel, scale, modes, slot_total, edge),
        out_shape=(quadrant, quadrant, jax.ShapeDtypeStruct((2, 2, edge, edge), f32), part, part),
        in_specs=[pl.BlockSpec(memory_space=pl.ANY)] * 2 + [smem] + [vmem] * 5,
        out_specs=(vmem,) * 5,
        scratch_shapes=[pltpu.VMEM((2, 2 * edge, 2 * edge), f32)]
        + [pltpu.VMEM((2, 2 * edge, edge), f32)] * 4
        + [
            pltpu.VMEM((2, modes, edge, edge), f32),
            pltpu.SMEM(offsets.shape, jnp.int32),
            pltpu.SMEM(counts.shape, jnp.int32),
            pltpu.SemaphoreType.DMA((2,)),
        ],
        compiler_params=pltpu.CompilerParams(vmem_limit_bytes=16 * 1024 * 1024),
    )(offsets, counts, place, held, object_tiles, diag, below, right)

    half = keep + partner(send, 1)
    got = [partner(half[k], 2 * k) for k in range(1, pieces)]
    got[0], right_grads = lax.optimization_barrier((got[0], right_grads))
    left = shifted(right_grads, 0, 1)
    chunk = functools.reduce(jnp.add, got, half[0])
    terms = [chunk] + [partner(chunk, n_pos * k) for k in range(1, n_region)]
    while len(terms) > 1:
        terms = [terms[k] + terms[k + 1] for k in range(0, len(terms), 2)]
    chunk = terms[0]
    chunk, left = lax.optimization_barrier((chunk, left))
    above = shifted(below_grad + left[1], 1, 0)
    gathered = [chunk] + [partner(chunk, 2 * k) for k in range(1, pieces)]
    gathered += [partner(piece, 1) for piece in gathered]
    probe_grad, object_grad = pl.pallas_call(
        join_kernel,
        out_shape=(jax.ShapeDtypeStruct((lines, edge), f32), quadrant),
        in_specs=[smem] + [vmem] * (3 + n_pos),
        out_specs=(pl.BlockSpec(memory_space=pl.ANY),) * 2,
        scratch_shapes=[pltpu.VMEM((2, edge, edge), f32), pltpu.SemaphoreType.DMA((n_pos + 1,))],
        compiler_params=pltpu.CompilerParams(vmem_limit_bytes=4 * 1024 * 1024),
    )(place, own_grad, left, above, *gathered)
    return (object_grad, probe_grad.reshape(probe.shape))


def solution(mesh):
    return jax.shard_map(
        on_device,
        mesh=mesh,
        in_specs=(
            P(None, "region", "pos"),
            P(),
            P("region", "pos", None, None),
            P("region", None, "pos"),
            P("region", "pos"),
        ),
        out_specs=(P(None, "region", "pos"), P()),
        check_vma=False,
    )
```

```python
import functools
import math

import jax
import jax.numpy as jnp
import numpy as np
from jax import lax
from jax.experimental import pallas as pl
from jax.experimental.pallas import tpu as pltpu
from jax.sharding import PartitionSpec as P


def dft_tables(order):
    index = np.arange(order)
    angle = (index[:, None] * index[None, :] % order) * (2.0 * math.pi / order)
    tables = np.stack([np.cos(angle), np.sin(angle)]) / math.sqrt(order)
    return tables.astype(np.float32)


def split(value):
    high = value.astype(jnp.bfloat16)
    low = (value - high.astype(jnp.float32)).astype(jnp.bfloat16)
    return high, low


def dot(a, b):
    return jnp.dot(a, b, preferred_element_type=jnp.float32)


def times_table(value, table_high, table_low):
    high, low = split(value)
    return dot(high, table_high) + (dot(low, table_high) + dot(high, table_low))


def table_times(table_high, table_low, value):
    high, low = split(value)
    return dot(table_high, high) + (dot(table_high, low) + dot(table_low, high))


def slots_kernel(
    scale, modes, slot_total, edge, offsets, counts, place, held, own, below, right, diag,
    own_grad, below_grad, right_grads, keep, send,
    tables, field_left, field_right, grad_left, grad_right, probe_sum, corners, live, semaphores,
):
    scalars = (
        pltpu.make_async_copy(offsets, corners, semaphores.at[0]),
        pltpu.make_async_copy(counts, live, semaphores.at[1]),
    )
    for copy in scalars:
        copy.start()

    def probe(part, mode):
        return held[part, pl.ds(mode * edge, edge), :]

    amplitude_rows = modes * edge
    table_rows = amplitude_rows + slot_total * edge // 2
    cos_high, cos_low = split(held[0, pl.ds(table_rows, edge), :])
    sin_high, sin_low = split(held[1, pl.ds(table_rows, edge), :])
    spread_high, spread_low, turn_high, turn_low = (tables.at[k] for k in range(4))
    for spread, turn, cos_part, sin_part in (
        (spread_high, turn_high, cos_high, sin_high),
        (spread_low, turn_low, cos_low, sin_low),
    ):
        for target, upper, lower in ((spread, -sin_part, sin_part), (turn, sin_part, -sin_part)):
            target[:edge, :edge] = cos_part
            target[:edge, edge:] = upper
            target[edge:, :edge] = lower
            target[edge:, edge:] = cos_part
    has_below, has_right = place[2] > 0, place[3] > 0
    has_diag = jnp.logical_and(has_below, has_right)

    def present(flag, value):
        return jnp.where(flag, value, jnp.zeros_like(value))

    field_left[:, :edge] = own[...].astype(jnp.float32)
    field_left[:, edge:] = present(has_below, below[...].astype(jnp.float32))
    field_right[:, :edge] = present(has_right, right[...].astype(jnp.float32))
    field_right[:, edge:] = present(has_diag, diag[...].astype(jnp.float32))
    grad_left[...] = jnp.zeros_like(grad_left)
    grad_right[...] = jnp.zeros_like(grad_right)
    lane = lax.broadcasted_iota(jnp.int32, (edge, edge), 1)
    for copy in scalars:
        copy.wait()
    slots = range(slot_total)
    corner = [(corners[0, 0, slot], corners[0, 1, slot]) for slot in slots]
    in_left = [lane >= col0 for _, col0 in corner]
    crops, halves = [], []
    for slot in slots:
        row0, col0 = corner[slot]
        rows, shift = pl.ds(row0, edge), lax.rem(edge - col0, edge)
        crop_r, crop_i = (
            pltpu.roll(
                jnp.where(in_left[slot], field_left[part, rows, :], field_right[part, rows, :]), shift, 1
            )
            for part in range(2)
        )
        exits = [
            jnp.concatenate(
                [
                    probe(0, m) * crop_r - probe(1, m) * crop_i,
                    probe(0, m) * crop_i + probe(1, m) * crop_r,
                ],
                axis=1,
            )
            for m in range(modes)
        ]
        crops.append((crop_r, crop_i))
        halves.append(times_table(jnp.concatenate(exits, axis=0), spread_high[...], spread_low[...]))
    fars = []
    for half in halves:
        parts = [
            [half[m * edge : (m + 1) * edge, part * edge : (part + 1) * edge] for m in range(modes)]
            for part in range(2)
        ]
        half = jnp.concatenate([jnp.concatenate(part, axis=1) for part in parts], axis=0)
        fars.append(table_times(turn_high[...], turn_low[...], half))
    halves = []
    for slot in slots:
        far = fars[slot]
        squares = far * far
        squares = squares[:edge] + squares[edge:]
        intensity = functools.reduce(
            jnp.add, [squares[:, m * edge : (m + 1) * edge] for m in range(modes)]
        )
        weight = (slot < live[0, 0]).astype(jnp.float32)
        half_slots = slot_total // 2
        amplitude = held[slot // half_slots, pl.ds(amplitude_rows + slot % half_slots * edge, edge), :]
        factor = weight * (1.0 - amplitude * lax.rsqrt(intensity + 1.0))
        factor = jnp.concatenate([factor] * modes, axis=1)
        residual = far * jnp.concatenate([factor, factor], axis=0)
        halves.append(table_times(spread_high[...], spread_low[...], residual))
    backs = []
    for half in halves:
        parts = [
            [half[part * edge : (part + 1) * edge, m * edge : (m + 1) * edge] for part in range(2)]
            for m in range(modes)
        ]
        half = jnp.concatenate([jnp.concatenate(part, axis=1) for part in parts], axis=0)
        backs.append(times_table(half, turn_high[...], turn_low[...]))
    for slot in slots:
        crop_r, crop_i = crops[slot]
        row0, col0 = corner[slot]
        rows = pl.ds(row0, edge)
        object_r = jnp.zeros((edge, edge), jnp.float32)
        object_i = jnp.zeros((edge, edge), jnp.float32)
        for m in range(modes):
            back_r = backs[slot][m * edge : (m + 1) * edge, :edge]
            back_i = backs[slot][m * edge : (m + 1) * edge, edge:]
            object_r += probe(0, m) * back_r + probe(1, m) * back_i
            object_i += probe(0, m) * back_i - probe(1, m) * back_r
            term_r = crop_r * back_r + crop_i * back_i
            term_i = crop_r * back_i - crop_i * back_r
            if slot == 0:
                probe_sum[0, m] = term_r
                probe_sum[1, m] = term_i
            else:
                probe_sum[0, m] += term_r
                probe_sum[1, m] += term_i
        for part, term in enumerate((object_r, object_i)):
            term = pltpu.roll(term, col0, 1)
            grad_left[part, rows, :] += jnp.where(in_left[slot], term, 0.0)
            grad_right[part, rows, :] += jnp.where(in_left[slot], 0.0, term)
    own_grad[...] = grad_left[:, :edge]
    below_grad[...] = present(has_below, grad_left[:, edge:])
    right_grads[0] = present(has_right, grad_right[:, :edge])
    right_grads[1] = present(has_diag, grad_right[:, edge:])
    flat = probe_sum.reshape(2 * modes * edge, edge)
    pieces, depth = keep.shape[0], keep.shape[1]
    for target, half in ((keep, place[0]), (send, 1 - place[0])):
        for position in range(pieces):
            chunk = half * pieces + jnp.bitwise_xor(place[1], position)
            rows = pl.ds(pl.multiple_of(chunk * depth, depth), depth)
            target[position] = flat[rows, :] * scale


def join_kernel(place, own_grad, left, above, *refs):
    pieces, (out, object_grad, total, semaphores) = refs[:-4], refs[-4:]
    count, depth = len(pieces) // 2, pieces[0].shape[0]
    copies = []
    for index, piece in enumerate(pieces):
        half = place[0] if index < count else 1 - place[0]
        chunk = half * count + jnp.bitwise_xor(place[1], index % count)
        rows = pl.ds(pl.multiple_of(chunk * depth, depth), depth)
        copies.append(pltpu.make_async_copy(piece, out.at[rows, :], semaphores.at[index]))
    total[...] = own_grad[...] + left[0] + above[...]
    copies.insert(0, pltpu.make_async_copy(total, object_grad, semaphores.at[len(pieces)]))
    for copy in copies:
        copy.start()
    for copy in copies:
        copy.wait()


def on_device(object_tiles, probe, amplitudes, offsets, counts):
    modes, edge = probe.shape[1], probe.shape[2]
    slot_total = amplitudes.shape[1]
    n_region, n_pos = lax.axis_size("region"), lax.axis_size("pos")
    total = n_region * n_pos
    axes = ("region", "pos")
    f32 = jnp.float32

    row_index, column_index = lax.axis_index("region"), lax.axis_index("pos")

    def shifted(block, down, across):
        route = [
            (i * n_pos + j, (i + down) % n_region * n_pos + (j + across) % n_pos)
            for i in range(n_region)
            for j in range(n_pos)
        ]
        return lax.ppermute(block, axes, route)

    pieces = n_pos // 2

    def partner(block, mask):
        return lax.ppermute(block, axes, [(i, i ^ mask) for i in range(total)])

    place = jnp.stack(
        [
            column_index & 1,
            column_index >> 1,
            (row_index < n_region - 1).astype(jnp.int32),
            (column_index < n_pos - 1).astype(jnp.int32),
        ]
    )

    below = shifted(object_tiles, -1, 0)
    right = shifted(object_tiles, 0, -1)
    diag = shifted(object_tiles, -1, -1)

    lines = 2 * modes * edge
    smem = pl.BlockSpec(memory_space=pltpu.SMEM)
    vmem = pl.BlockSpec(memory_space=pltpu.VMEM)
    held = jnp.concatenate(
        [
            probe.reshape(2, -1, edge),
            amplitudes.reshape(2, -1, edge),
            jnp.asarray(dft_tables(edge)),
        ],
        axis=1,
    )
    quadrant = jax.ShapeDtypeStruct((2, edge, edge), f32)
    part = jax.ShapeDtypeStruct((pieces, lines // n_pos, edge), f32)
    scale = 1.0 / math.sqrt(total * slot_total)
    own_grad, below_grad, right_grads, keep, send = pl.pallas_call(
        functools.partial(slots_kernel, scale, modes, slot_total, edge),
        out_shape=(quadrant, quadrant, jax.ShapeDtypeStruct((2, 2, edge, edge), f32), part, part),
        in_specs=[pl.BlockSpec(memory_space=pl.ANY)] * 2 + [smem] + [vmem] * 5,
        out_specs=(vmem,) * 5,
        scratch_shapes=[pltpu.VMEM((4, 2 * edge, 2 * edge), jnp.bfloat16)]
        + [pltpu.VMEM((2, 2 * edge, edge), f32)] * 4
        + [
            pltpu.VMEM((2, modes, edge, edge), f32),
            pltpu.SMEM(offsets.shape, jnp.int32),
            pltpu.SMEM(counts.shape, jnp.int32),
            pltpu.SemaphoreType.DMA((2,)),
        ],
        compiler_params=pltpu.CompilerParams(vmem_limit_bytes=16 * 1024 * 1024),
    )(offsets, counts, place, held, object_tiles, below, right, diag)

    half = keep + partner(send, 1)
    got = [partner(half[k], 2 * k) for k in range(1, pieces)]
    got[0], right_grads = lax.optimization_barrier((got[0], right_grads))
    left = shifted(right_grads, 0, 1)
    chunk = functools.reduce(jnp.add, got, half[0])
    terms = [chunk] + [partner(chunk, n_pos * k) for k in range(1, n_region)]
    while len(terms) > 1:
        terms = [terms[k] + terms[k + 1] for k in range(0, len(terms), 2)]
    chunk = terms[0]
    above = shifted(below_grad + left[1], 1, 0)
    gathered = [chunk] + [partner(chunk, 2 * k) for k in range(1, pieces)]
    gathered[1], left = lax.optimization_barrier((gathered[1], left))
    gathered += [partner(piece, 1) for piece in gathered]
    probe_grad, object_grad = pl.pallas_call(
        join_kernel,
        out_shape=(jax.ShapeDtypeStruct((lines, edge), f32), quadrant),
        in_specs=[smem] + [vmem] * (3 + n_pos),
        out_specs=(pl.BlockSpec(memory_space=pl.ANY),) * 2,
        scratch_shapes=[pltpu.VMEM((2, edge, edge), f32), pltpu.SemaphoreType.DMA((n_pos + 1,))],
        compiler_params=pltpu.CompilerParams(vmem_limit_bytes=4 * 1024 * 1024),
    )(place, own_grad, left, above, *gathered)
    return (object_grad, probe_grad.reshape(probe.shape))


def solution(mesh):
    return jax.shard_map(
        on_device,
        mesh=mesh,
        in_specs=(
            P(None, "region", "pos"),
            P(),
            P("region", "pos", None, None),
            P("region", None, "pos"),
            P("region", "pos"),
        ),
        out_specs=(P(None, "region", "pos"), P()),
        check_vma=False,
    )
```

```python
import functools
import math

import jax
import jax.numpy as jnp
import numpy as np
from jax import lax
from jax.experimental import pallas as pl
from jax.experimental.pallas import tpu as pltpu
from jax.sharding import PartitionSpec as P


def dft_tables(order):
    index = np.arange(order)
    angle = (index[:, None] * index[None, :] % order) * (2.0 * math.pi / order)
    tables = np.stack([np.cos(angle), np.sin(angle)]) / math.sqrt(order)
    return tables.astype(np.float32)


def split(value):
    high = value.astype(jnp.bfloat16)
    low = (value - high.astype(jnp.float32)).astype(jnp.bfloat16)
    return high, low


def dot(a, b):
    return jnp.dot(a, b, preferred_element_type=jnp.float32)


def times_table(value, table_high, table_low):
    high, low = split(value)
    return dot(high, table_high) + (dot(low, table_high) + dot(high, table_low))


def table_times(table_high, table_low, value):
    high, low = split(value)
    return dot(table_high, high) + (dot(table_high, low) + dot(table_low, high))


def slots_kernel(
    scale, modes, slot_total, edge, offsets, counts, place, held, own, below, right, diag,
    own_grad, right_grad, lower_grads, keep, send,
    tables, field_left, field_right, grad_left, grad_right, probe_sum, corners, live, semaphores,
):
    scalars = (
        pltpu.make_async_copy(offsets, corners, semaphores.at[0]),
        pltpu.make_async_copy(counts, live, semaphores.at[1]),
    )
    for copy in scalars:
        copy.start()

    def probe(part, mode):
        return held[part, pl.ds(mode * edge, edge), :]

    amplitude_rows = modes * edge
    table_rows = amplitude_rows + slot_total * edge // 2
    cos_high, cos_low = split(held[0, pl.ds(table_rows, edge), :])
    sin_high, sin_low = split(held[1, pl.ds(table_rows, edge), :])
    spread_high, spread_low, turn_high, turn_low = (tables.at[k] for k in range(4))
    for spread, turn, cos_part, sin_part in (
        (spread_high, turn_high, cos_high, sin_high),
        (spread_low, turn_low, cos_low, sin_low),
    ):
        for target, upper, lower in ((spread, -sin_part, sin_part), (turn, sin_part, -sin_part)):
            target[:edge, :edge] = cos_part
            target[:edge, edge:] = upper
            target[edge:, :edge] = lower
            target[edge:, edge:] = cos_part
    has_below, has_right = place[2] > 0, place[3] > 0
    has_diag = jnp.logical_and(has_below, has_right)

    def present(flag, value):
        return jnp.where(flag, value, jnp.zeros_like(value))

    field_left[:, :edge] = own[...].astype(jnp.float32)
    field_left[:, edge:] = present(has_below, below[...].astype(jnp.float32))
    field_right[:, :edge] = present(has_right, right[...].astype(jnp.float32))
    field_right[:, edge:] = present(has_diag, diag[...].astype(jnp.float32))
    grad_left[...] = jnp.zeros_like(grad_left)
    grad_right[...] = jnp.zeros_like(grad_right)
    lane = lax.broadcasted_iota(jnp.int32, (edge, edge), 1)
    for copy in scalars:
        copy.wait()
    slots = range(slot_total)
    corner = [(corners[0, 0, slot], corners[0, 1, slot]) for slot in slots]
    in_left = [lane >= col0 for _, col0 in corner]
    crops, halves = [], []
    for slot in slots:
        row0, col0 = corner[slot]
        rows, shift = pl.ds(row0, edge), lax.rem(edge - col0, edge)
        crop_r, crop_i = (
            pltpu.roll(
                jnp.where(in_left[slot], field_left[part, rows, :], field_right[part, rows, :]), shift, 1
            )
            for part in range(2)
        )
        exits = [
            jnp.concatenate(
                [
                    probe(0, m) * crop_r - probe(1, m) * crop_i,
                    probe(0, m) * crop_i + probe(1, m) * crop_r,
                ],
                axis=1,
            )
            for m in range(modes)
        ]
        crops.append((crop_r, crop_i))
        halves.append(times_table(jnp.concatenate(exits, axis=0), spread_high[...], spread_low[...]))
    fars = []
    for half in halves:
        parts = [
            [half[m * edge : (m + 1) * edge, part * edge : (part + 1) * edge] for m in range(modes)]
            for part in range(2)
        ]
        half = jnp.concatenate([jnp.concatenate(part, axis=1) for part in parts], axis=0)
        fars.append(table_times(turn_high[...], turn_low[...], half))
    halves = []
    for slot in slots:
        far = fars[slot]
        squares = far * far
        squares = squares[:edge] + squares[edge:]
        intensity = functools.reduce(
            jnp.add, [squares[:, m * edge : (m + 1) * edge] for m in range(modes)]
        )
        weight = (slot < live[0, 0]).astype(jnp.float32)
        half_slots = slot_total // 2
        amplitude = held[slot // half_slots, pl.ds(amplitude_rows + slot % half_slots * edge, edge), :]
        factor = weight * (1.0 - amplitude * lax.rsqrt(intensity + 1.0))
        factor = jnp.concatenate([factor] * modes, axis=1)
        residual = far * jnp.concatenate([factor, factor], axis=0)
        halves.append(table_times(spread_high[...], spread_low[...], residual))
    backs = []
    for half in halves:
        parts = [
            [half[part * edge : (part + 1) * edge, m * edge : (m + 1) * edge] for part in range(2)]
            for m in range(modes)
        ]
        half = jnp.concatenate([jnp.concatenate(part, axis=1) for part in parts], axis=0)
        backs.append(times_table(half, turn_high[...], turn_low[...]))
    for slot in slots:
        crop_r, crop_i = crops[slot]
        row0, col0 = corner[slot]
        rows = pl.ds(row0, edge)
        object_r = jnp.zeros((edge, edge), jnp.float32)
        object_i = jnp.zeros((edge, edge), jnp.float32)
        for m in range(modes):
            back_r = backs[slot][m * edge : (m + 1) * edge, :edge]
            back_i = backs[slot][m * edge : (m + 1) * edge, edge:]
            object_r += probe(0, m) * back_r + probe(1, m) * back_i
            object_i += probe(0, m) * back_i - probe(1, m) * back_r
            term_r = crop_r * back_r + crop_i * back_i
            term_i = crop_r * back_i - crop_i * back_r
            if slot == 0:
                probe_sum[0, m] = term_r
                probe_sum[1, m] = term_i
            else:
                probe_sum[0, m] += term_r
                probe_sum[1, m] += term_i
        for part, term in enumerate((object_r, object_i)):
            term = pltpu.roll(term, col0, 1)
            grad_left[part, rows, :] += jnp.where(in_left[slot], term, 0.0)
            grad_right[part, rows, :] += jnp.where(in_left[slot], 0.0, term)
    own_grad[...] = grad_left[:, :edge]
    right_grad[...] = present(has_right, grad_right[:, :edge])
    lower_grads[0] = present(has_below, grad_left[:, edge:])
    lower_grads[1] = present(has_diag, grad_right[:, edge:])
    flat = probe_sum.reshape(2 * modes * edge, edge)
    pieces, depth = keep.shape[0], keep.shape[1]
    for target, half in ((keep, place[0]), (send, 1 - place[0])):
        for position in range(pieces):
            chunk = half * pieces + jnp.bitwise_xor(place[1], position)
            rows = pl.ds(pl.multiple_of(chunk * depth, depth), depth)
            target[position] = flat[rows, :] * scale


def join_kernel(place, own_grad, above, left, *refs):
    pieces, (out, object_grad, total, semaphores) = refs[:-4], refs[-4:]
    count, depth = len(pieces) // 2, pieces[0].shape[0]
    copies = []
    for index, piece in enumerate(pieces):
        half = place[0] if index < count else 1 - place[0]
        chunk = half * count + jnp.bitwise_xor(place[1], index % count)
        rows = pl.ds(pl.multiple_of(chunk * depth, depth), depth)
        copies.append(pltpu.make_async_copy(piece, out.at[rows, :], semaphores.at[index]))
    total[...] = own_grad[...] + above[0] + left[...]
    copies.insert(0, pltpu.make_async_copy(total, object_grad, semaphores.at[len(pieces)]))
    for copy in copies:
        copy.start()
    for copy in copies:
        copy.wait()


def on_device(object_tiles, probe, amplitudes, offsets, counts):
    modes, edge = probe.shape[1], probe.shape[2]
    slot_total = amplitudes.shape[1]
    n_region, n_pos = lax.axis_size("region"), lax.axis_size("pos")
    total = n_region * n_pos
    axes = ("region", "pos")
    f32 = jnp.float32

    row_index, column_index = lax.axis_index("region"), lax.axis_index("pos")

    def shifted(block, down, across):
        route = [
            (i * n_pos + j, (i + down) % n_region * n_pos + (j + across) % n_pos)
            for i in range(n_region)
            for j in range(n_pos)
        ]
        return lax.ppermute(block, axes, route)

    pieces = n_pos // 2

    def partner(block, mask):
        return lax.ppermute(block, axes, [(i, i ^ mask) for i in range(total)])

    place = jnp.stack(
        [
            column_index & 1,
            column_index >> 1,
            (row_index < n_region - 1).astype(jnp.int32),
            (column_index < n_pos - 1).astype(jnp.int32),
        ]
    )

    below = shifted(object_tiles, -1, 0)
    right = shifted(object_tiles, 0, -1)
    diag = shifted(object_tiles, -1, -1)

    lines = 2 * modes * edge
    smem = pl.BlockSpec(memory_space=pltpu.SMEM)
    vmem = pl.BlockSpec(memory_space=pltpu.VMEM)
    held = jnp.concatenate(
        [
            probe.reshape(2, -1, edge),
            amplitudes.reshape(2, -1, edge),
            jnp.asarray(dft_tables(edge)),
        ],
        axis=1,
    )
    quadrant = jax.ShapeDtypeStruct((2, edge, edge), f32)
    part = jax.ShapeDtypeStruct((pieces, lines // n_pos, edge), f32)
    scale = 1.0 / math.sqrt(total * slot_total)
    own_grad, right_grad, lower_grads, keep, send = pl.pallas_call(
        functools.partial(slots_kernel, scale, modes, slot_total, edge),
        out_shape=(quadrant, quadrant, jax.ShapeDtypeStruct((2, 2, edge, edge), f32), part, part),
        in_specs=[pl.BlockSpec(memory_space=pl.ANY)] * 2 + [smem] + [vmem] * 5,
        out_specs=(vmem,) * 5,
        scratch_shapes=[pltpu.VMEM((4, 2 * edge, 2 * edge), jnp.bfloat16)]
        + [pltpu.VMEM((2, 2 * edge, edge), f32)] * 4
        + [
            pltpu.VMEM((2, modes, edge, edge), f32),
            pltpu.SMEM(offsets.shape, jnp.int32),
            pltpu.SMEM(counts.shape, jnp.int32),
            pltpu.SemaphoreType.DMA((2,)),
        ],
        compiler_params=pltpu.CompilerParams(vmem_limit_bytes=16 * 1024 * 1024),
    )(offsets, counts, place, held, object_tiles, below, right, diag)

    half, lower_grads = lax.optimization_barrier((keep + partner(send, 1), lower_grads))
    above = shifted(lower_grads, 1, 0)
    got = [partner(half[k], 2 * k) for k in range(1, pieces)]
    chunk = functools.reduce(jnp.add, got, half[0])
    terms = [chunk] + [partner(chunk, n_pos * k) for k in range(1, n_region)]
    terms[1], above = lax.optimization_barrier((terms[1], above))
    left = shifted(right_grad + above[1], 0, 1)
    while len(terms) > 1:
        terms = [terms[k] + terms[k + 1] for k in range(0, len(terms), 2)]
    chunk = terms[0]
    gathered = [chunk] + [partner(chunk, 2 * k) for k in range(1, pieces)]
    gathered[1], left = lax.optimization_barrier((gathered[1], left))
    gathered += [partner(piece, 1) for piece in gathered]
    probe_grad, object_grad = pl.pallas_call(
        join_kernel,
        out_shape=(jax.ShapeDtypeStruct((lines, edge), f32), quadrant),
        in_specs=[smem] + [vmem] * (3 + n_pos),
        out_specs=(pl.BlockSpec(memory_space=pl.ANY),) * 2,
        scratch_shapes=[pltpu.VMEM((2, edge, edge), f32), pltpu.SemaphoreType.DMA((n_pos + 1,))],
        compiler_params=pltpu.CompilerParams(vmem_limit_bytes=4 * 1024 * 1024),
    )(place, own_grad, above, left, *gathered)
    return (object_grad, probe_grad.reshape(probe.shape))


def solution(mesh):
    return jax.shard_map(
        on_device,
        mesh=mesh,
        in_specs=(
            P(None, "region", "pos"),
            P(),
            P("region", "pos", None, None),
            P("region", None, "pos"),
            P("region", "pos"),
        ),
        out_specs=(P(None, "region", "pos"), P()),
        check_vma=False,
    )
```

```python
import functools
import math

import jax
import jax.numpy as jnp
import numpy as np
from jax import lax
from jax.experimental import pallas as pl
from jax.experimental.pallas import tpu as pltpu
from jax.sharding import PartitionSpec as P


def dft_tables(order):
    index = np.arange(order)
    angle = (index[:, None] * index[None, :] % order) * (2.0 * math.pi / order)
    tables = np.stack([np.cos(angle), np.sin(angle)]) / math.sqrt(order)
    return tables.astype(np.float32)


def split(value):
    high = value.astype(jnp.bfloat16)
    low = (value - high.astype(jnp.float32)).astype(jnp.bfloat16)
    return high, low


def dot(a, b):
    return jnp.dot(a, b, preferred_element_type=jnp.float32)


def times_table(value, table_high, table_low):
    high, low = split(value)
    return dot(high, table_high) + (dot(low, table_high) + dot(high, table_low))


def table_times(table_high, table_low, value):
    high, low = split(value)
    return dot(table_high, high) + (dot(table_high, low) + dot(table_low, high))


def slots_kernel(
    scale, modes, slot_total, edge, offsets, counts, place, held, own, below, right, diag,
    own_grad, right_grad, lower_grads, keep, send,
    tables, field_left, field_right, grad_left, grad_right, probe_sum, corners, live, semaphores,
):
    scalars = (
        pltpu.make_async_copy(offsets, corners, semaphores.at[0]),
        pltpu.make_async_copy(counts, live, semaphores.at[1]),
    )
    for copy in scalars:
        copy.start()

    def probe(part, mode):
        return held[part, pl.ds(mode * edge, edge), :]

    amplitude_rows = modes * edge
    table_rows = amplitude_rows + slot_total * edge // 2
    cos_high, cos_low = split(held[0, pl.ds(table_rows, edge), :])
    sin_high, sin_low = split(held[1, pl.ds(table_rows, edge), :])
    spread_high, spread_low, turn_high, turn_low = (tables.at[k] for k in range(4))
    for spread, turn, cos_part, sin_part in (
        (spread_high, turn_high, cos_high, sin_high),
        (spread_low, turn_low, cos_low, sin_low),
    ):
        for target, upper, lower in ((spread, -sin_part, sin_part), (turn, sin_part, -sin_part)):
            target[:edge, :edge] = cos_part
            target[:edge, edge:] = upper
            target[edge:, :edge] = lower
            target[edge:, edge:] = cos_part
    has_below, has_right = place[2] > 0, place[3] > 0
    has_diag = jnp.logical_and(has_below, has_right)

    def present(flag, value):
        return jnp.where(flag, value, jnp.zeros_like(value))

    field_left[:, :edge] = own[...].astype(jnp.float32)
    field_left[:, edge:] = present(has_below, below[...].astype(jnp.float32))
    field_right[:, :edge] = present(has_right, right[...].astype(jnp.float32))
    field_right[:, edge:] = present(has_diag, diag[...].astype(jnp.float32))
    grad_left[...] = jnp.zeros_like(grad_left)
    grad_right[...] = jnp.zeros_like(grad_right)
    lane = lax.broadcasted_iota(jnp.int32, (edge, edge), 1)
    for copy in scalars:
        copy.wait()
    slots = range(slot_total)
    corner = [(corners[0, 0, slot], corners[0, 1, slot]) for slot in slots]
    in_left = [lane >= col0 for _, col0 in corner]
    crops, halves = [], []
    for slot in slots:
        row0, col0 = corner[slot]
        rows, shift = pl.ds(row0, edge), lax.rem(edge - col0, edge)
        crop_r, crop_i = (
            pltpu.roll(
                jnp.where(in_left[slot], field_left[part, rows, :], field_right[part, rows, :]), shift, 1
            )
            for part in range(2)
        )
        exits = [
            jnp.concatenate(
                [
                    probe(0, m) * crop_r - probe(1, m) * crop_i,
                    probe(0, m) * crop_i + probe(1, m) * crop_r,
                ],
                axis=1,
            )
            for m in range(modes)
        ]
        crops.append((crop_r, crop_i))
        halves.append(times_table(jnp.concatenate(exits, axis=0), spread_high[...], spread_low[...]))
    fars = []
    for half in halves:
        parts = [
            [half[m * edge : (m + 1) * edge, part * edge : (part + 1) * edge] for m in range(modes)]
            for part in range(2)
        ]
        half = jnp.concatenate([jnp.concatenate(part, axis=1) for part in parts], axis=0)
        fars.append(table_times(turn_high[...], turn_low[...], half))
    halves = []
    for slot in slots:
        far = fars[slot]
        squares = far * far
        squares = squares[:edge] + squares[edge:]
        intensity = functools.reduce(
            jnp.add, [squares[:, m * edge : (m + 1) * edge] for m in range(modes)]
        )
        weight = (slot < live[0, 0]).astype(jnp.float32)
        half_slots = slot_total // 2
        amplitude = held[slot // half_slots, pl.ds(amplitude_rows + slot % half_slots * edge, edge), :]
        factor = weight * (1.0 - amplitude * lax.rsqrt(intensity + 1.0))
        factor = jnp.concatenate([factor] * modes, axis=1)
        residual = far * jnp.concatenate([factor, factor], axis=0)
        halves.append(table_times(spread_high[...], spread_low[...], residual))
    backs = []
    for half in halves:
        parts = [
            [half[part * edge : (part + 1) * edge, m * edge : (m + 1) * edge] for part in range(2)]
            for m in range(modes)
        ]
        half = jnp.concatenate([jnp.concatenate(part, axis=1) for part in parts], axis=0)
        backs.append(times_table(half, turn_high[...], turn_low[...]))
    for slot in slots:
        crop_r, crop_i = crops[slot]
        row0, col0 = corner[slot]
        rows = pl.ds(row0, edge)
        object_r = jnp.zeros((edge, edge), jnp.float32)
        object_i = jnp.zeros((edge, edge), jnp.float32)
        for m in range(modes):
            back_r = backs[slot][m * edge : (m + 1) * edge, :edge]
            back_i = backs[slot][m * edge : (m + 1) * edge, edge:]
            object_r += probe(0, m) * back_r + probe(1, m) * back_i
            object_i += probe(0, m) * back_i - probe(1, m) * back_r
            term_r = crop_r * back_r + crop_i * back_i
            term_i = crop_r * back_i - crop_i * back_r
            if slot == 0:
                probe_sum[0, m] = term_r
                probe_sum[1, m] = term_i
            else:
                probe_sum[0, m] += term_r
                probe_sum[1, m] += term_i
        for part, term in enumerate((object_r, object_i)):
            term = pltpu.roll(term, col0, 1)
            grad_left[part, rows, :] += jnp.where(in_left[slot], term, 0.0)
            grad_right[part, rows, :] += jnp.where(in_left[slot], 0.0, term)
    own_grad[...] = grad_left[:, :edge]
    right_grad[...] = present(has_right, grad_right[:, :edge])
    lower_grads[0] = present(has_below, grad_left[:, edge:])
    lower_grads[1] = present(has_diag, grad_right[:, edge:])
    flat = probe_sum.reshape(2 * modes * edge, edge)
    pieces, depth = keep.shape[0], keep.shape[1]
    for target, half in ((keep, place[0]), (send, 1 - place[0])):
        for position in range(pieces):
            chunk = half * pieces + jnp.bitwise_xor(place[1], position)
            rows = pl.ds(pl.multiple_of(chunk * depth, depth), depth)
            target[position] = flat[rows, :] * scale


def join_kernel(place, own_grad, above, left, *refs):
    pieces, (out, object_grad, total, semaphores) = refs[:-4], refs[-4:]
    count, depth = len(pieces) // 2, pieces[0].shape[0]
    copies = []
    for index, piece in enumerate(pieces):
        half = place[0] if index < count else 1 - place[0]
        chunk = half * count + jnp.bitwise_xor(place[1], index % count)
        rows = pl.ds(pl.multiple_of(chunk * depth, depth), depth)
        copies.append(pltpu.make_async_copy(piece, out.at[rows, :], semaphores.at[index]))
    total[...] = own_grad[...] + above[0] + left[...]
    copies.insert(0, pltpu.make_async_copy(total, object_grad, semaphores.at[len(pieces)]))
    for copy in copies:
        copy.start()
    for copy in copies:
        copy.wait()


def on_device(object_tiles, probe, amplitudes, offsets, counts):
    modes, edge = probe.shape[1], probe.shape[2]
    slot_total = amplitudes.shape[1]
    n_region, n_pos = lax.axis_size("region"), lax.axis_size("pos")
    total = n_region * n_pos
    axes = ("region", "pos")
    f32 = jnp.float32

    row_index, column_index = lax.axis_index("region"), lax.axis_index("pos")

    def shifted(block, down, across):
        route = [
            (i * n_pos + j, (i + down) % n_region * n_pos + (j + across) % n_pos)
            for i in range(n_region)
            for j in range(n_pos)
        ]
        return lax.ppermute(block, axes, route)

    pieces = n_pos // 2

    def partner(block, mask):
        return lax.ppermute(block, axes, [(i, i ^ mask) for i in range(total)])

    place = jnp.stack(
        [
            column_index & 1,
            column_index >> 1,
            (row_index < n_region - 1).astype(jnp.int32),
            (column_index < n_pos - 1).astype(jnp.int32),
        ]
    )

    below = shifted(object_tiles, -1, 0)
    right = shifted(object_tiles, 0, -1)
    diag = shifted(object_tiles, -1, -1)

    lines = 2 * modes * edge
    smem = pl.BlockSpec(memory_space=pltpu.SMEM)
    vmem = pl.BlockSpec(memory_space=pltpu.VMEM)
    held = jnp.concatenate(
        [
            probe.reshape(2, -1, edge),
            amplitudes.reshape(2, -1, edge),
            jnp.asarray(dft_tables(edge)),
        ],
        axis=1,
    )
    quadrant = jax.ShapeDtypeStruct((2, edge, edge), f32)
    part = jax.ShapeDtypeStruct((pieces, lines // n_pos, edge), f32)
    scale = 1.0 / math.sqrt(total * slot_total)
    own_grad, right_grad, lower_grads, keep, send = pl.pallas_call(
        functools.partial(slots_kernel, scale, modes, slot_total, edge),
        out_shape=(quadrant, quadrant, jax.ShapeDtypeStruct((2, 2, edge, edge), f32), part, part),
        in_specs=[pl.BlockSpec(memory_space=pl.ANY)] * 2 + [smem] + [vmem] * 5,
        out_specs=(vmem,) * 5,
        scratch_shapes=[pltpu.VMEM((4, 2 * edge, 2 * edge), jnp.bfloat16)]
        + [pltpu.VMEM((2, 2 * edge, edge), f32)] * 4
        + [
            pltpu.VMEM((2, modes, edge, edge), f32),
            pltpu.SMEM(offsets.shape, jnp.int32),
            pltpu.SMEM(counts.shape, jnp.int32),
            pltpu.SemaphoreType.DMA((2,)),
        ],
        compiler_params=pltpu.CompilerParams(vmem_limit_bytes=16 * 1024 * 1024),
    )(offsets, counts, place, held, object_tiles, below, right, diag)

    half = keep + partner(send, 1)
    above = shifted(lower_grads, 1, 0)
    got = [partner(half[k], 2 * k) for k in range(1, pieces)]
    got[0], above = lax.optimization_barrier((got[0], above))
    chunk = functools.reduce(jnp.add, got, half[0])
    terms = [chunk] + [partner(chunk, n_pos * k) for k in range(1, n_region)]
    left = shifted(right_grad + above[1], 0, 1)
    while len(terms) > 1:
        terms = [terms[k] + terms[k + 1] for k in range(0, len(terms), 2)]
    chunk = terms[0]
    gathered = [chunk] + [partner(chunk, 2 * k) for k in range(1, pieces)]
    gathered[1], left = lax.optimization_barrier((gathered[1], left))
    gathered += [partner(piece, 1) for piece in gathered]
    probe_grad, object_grad = pl.pallas_call(
        join_kernel,
        out_shape=(jax.ShapeDtypeStruct((lines, edge), f32), quadrant),
        in_specs=[smem] + [vmem] * (3 + n_pos),
        out_specs=(pl.BlockSpec(memory_space=pl.ANY),) * 2,
        scratch_shapes=[pltpu.VMEM((2, edge, edge), f32), pltpu.SemaphoreType.DMA((n_pos + 1,))],
        compiler_params=pltpu.CompilerParams(vmem_limit_bytes=4 * 1024 * 1024),
    )(place, own_grad, above, left, *gathered)
    return (object_grad, probe_grad.reshape(probe.shape))


def solution(mesh):
    return jax.shard_map(
        on_device,
        mesh=mesh,
        in_specs=(
            P(None, "region", "pos"),
            P(),
            P("region", "pos", None, None),
            P("region", None, "pos"),
            P("region", "pos"),
        ),
        out_specs=(P(None, "region", "pos"), P()),
        check_vma=False,
    )
```

```python
import functools
import math

import jax
import jax.numpy as jnp
import numpy as np
from jax import lax
from jax.experimental import pallas as pl
from jax.experimental.pallas import tpu as pltpu
from jax.sharding import PartitionSpec as P


def dft_tables(order):
    index = np.arange(order)
    angle = (index[:, None] * index[None, :] % order) * (2.0 * math.pi / order)
    tables = np.stack([np.cos(angle), np.sin(angle)]) / math.sqrt(order)
    return tables.astype(np.float32)


def split(value):
    high = value.astype(jnp.bfloat16)
    low = (value - high.astype(jnp.float32)).astype(jnp.bfloat16)
    return high, low


def dot(a, b):
    return jnp.dot(a, b, preferred_element_type=jnp.float32)


def times_table(value, table_high, table_low):
    high, low = split(value)
    return dot(high, table_high) + (dot(low, table_high) + dot(high, table_low))


def table_times(table_high, table_low, value):
    high, low = split(value)
    return dot(table_high, high) + (dot(table_high, low) + dot(table_low, high))


def slots_kernel(
    scale, modes, slot_total, edge, offsets, counts, place, held, own, below, other_below, right, diag, other_diag,
    own_grad, right_grad, lower_grads, keep, send,
    tables, field_left, field_right, grad_left, grad_right, probe_sum, corners, live, semaphores,
):
    scalars = (
        pltpu.make_async_copy(offsets, corners, semaphores.at[0]),
        pltpu.make_async_copy(counts, live, semaphores.at[1]),
    )
    for copy in scalars:
        copy.start()

    def probe(part, mode):
        return held[part, pl.ds(mode * edge, edge), :]

    amplitude_rows = modes * edge
    table_rows = amplitude_rows + slot_total * edge // 2
    cos_high, cos_low = split(held[0, pl.ds(table_rows, edge), :])
    sin_high, sin_low = split(held[1, pl.ds(table_rows, edge), :])
    spread_high, spread_low, turn_high, turn_low = (tables.at[k] for k in range(4))
    for spread, turn, cos_part, sin_part in (
        (spread_high, turn_high, cos_high, sin_high),
        (spread_low, turn_low, cos_low, sin_low),
    ):
        for target, upper, lower in ((spread, -sin_part, sin_part), (turn, sin_part, -sin_part)):
            target[:edge, :edge] = cos_part
            target[:edge, edge:] = upper
            target[edge:, :edge] = lower
            target[edge:, edge:] = cos_part
    has_below, has_right, odd_row = place[2] > 0, place[3] > 0, place[4] > 0
    has_diag = jnp.logical_and(has_below, has_right)

    def present(flag, value):
        return jnp.where(flag, value, jnp.zeros_like(value))

    def arrived(flag, first, second):
        return present(flag, jnp.where(odd_row, second[...], first[...]).astype(jnp.float32))

    field_left[:, :edge] = own[...].astype(jnp.float32)
    field_left[:, edge:] = arrived(has_below, below, other_below)
    field_right[:, :edge] = present(has_right, right[...].astype(jnp.float32))
    field_right[:, edge:] = arrived(has_diag, diag, other_diag)
    grad_left[...] = jnp.zeros_like(grad_left)
    grad_right[...] = jnp.zeros_like(grad_right)
    lane = lax.broadcasted_iota(jnp.int32, (edge, edge), 1)
    for copy in scalars:
        copy.wait()
    slots = range(slot_total)
    corner = [(corners[0, 0, slot], corners[0, 1, slot]) for slot in slots]
    in_left = [lane >= col0 for _, col0 in corner]
    crops, halves = [], []
    for slot in slots:
        row0, col0 = corner[slot]
        rows, shift = pl.ds(row0, edge), lax.rem(edge - col0, edge)
        crop_r, crop_i = (
            pltpu.roll(
                jnp.where(in_left[slot], field_left[part, rows, :], field_right[part, rows, :]), shift, 1
            )
            for part in range(2)
        )
        exits = [
            jnp.concatenate(
                [
                    probe(0, m) * crop_r - probe(1, m) * crop_i,
                    probe(0, m) * crop_i + probe(1, m) * crop_r,
                ],
                axis=1,
            )
            for m in range(modes)
        ]
        crops.append((crop_r, crop_i))
        halves.append(times_table(jnp.concatenate(exits, axis=0), spread_high[...], spread_low[...]))
    fars = []
    for half in halves:
        parts = [
            [half[m * edge : (m + 1) * edge, part * edge : (part + 1) * edge] for m in range(modes)]
            for part in range(2)
        ]
        half = jnp.concatenate([jnp.concatenate(part, axis=1) for part in parts], axis=0)
        fars.append(table_times(turn_high[...], turn_low[...], half))
    halves = []
    for slot in slots:
        far = fars[slot]
        squares = far * far
        squares = squares[:edge] + squares[edge:]
        intensity = functools.reduce(
            jnp.add, [squares[:, m * edge : (m + 1) * edge] for m in range(modes)]
        )
        weight = (slot < live[0, 0]).astype(jnp.float32)
        half_slots = slot_total // 2
        amplitude = held[slot // half_slots, pl.ds(amplitude_rows + slot % half_slots * edge, edge), :]
        factor = weight * (1.0 - amplitude * lax.rsqrt(intensity + 1.0))
        factor = jnp.concatenate([factor] * modes, axis=1)
        residual = far * jnp.concatenate([factor, factor], axis=0)
        halves.append(table_times(spread_high[...], spread_low[...], residual))
    backs = []
    for half in halves:
        parts = [
            [half[part * edge : (part + 1) * edge, m * edge : (m + 1) * edge] for part in range(2)]
            for m in range(modes)
        ]
        half = jnp.concatenate([jnp.concatenate(part, axis=1) for part in parts], axis=0)
        backs.append(times_table(half, turn_high[...], turn_low[...]))
    for slot in slots:
        crop_r, crop_i = crops[slot]
        row0, col0 = corner[slot]
        rows = pl.ds(row0, edge)
        object_r = jnp.zeros((edge, edge), jnp.float32)
        object_i = jnp.zeros((edge, edge), jnp.float32)
        for m in range(modes):
            back_r = backs[slot][m * edge : (m + 1) * edge, :edge]
            back_i = backs[slot][m * edge : (m + 1) * edge, edge:]
            object_r += probe(0, m) * back_r + probe(1, m) * back_i
            object_i += probe(0, m) * back_i - probe(1, m) * back_r
            term_r = crop_r * back_r + crop_i * back_i
            term_i = crop_r * back_i - crop_i * back_r
            if slot == 0:
                probe_sum[0, m] = term_r
                probe_sum[1, m] = term_i
            else:
                probe_sum[0, m] += term_r
                probe_sum[1, m] += term_i
        for part, term in enumerate((object_r, object_i)):
            term = pltpu.roll(term, col0, 1)
            grad_left[part, rows, :] += jnp.where(in_left[slot], term, 0.0)
            grad_right[part, rows, :] += jnp.where(in_left[slot], 0.0, term)
    own_grad[...] = grad_left[:, :edge]
    right_grad[...] = present(has_right, grad_right[:, :edge])
    lower_grads[0] = present(has_below, grad_left[:, edge:])
    lower_grads[1] = present(has_diag, grad_right[:, edge:])
    flat = probe_sum.reshape(2 * modes * edge, edge)
    pieces, depth = keep.shape[0], keep.shape[1]
    for target, half in ((keep, place[0]), (send, 1 - place[0])):
        for position in range(pieces):
            chunk = half * pieces + jnp.bitwise_xor(place[1], position)
            rows = pl.ds(pl.multiple_of(chunk * depth, depth), depth)
            target[position] = flat[rows, :] * scale


def join_kernel(place, own_grad, above, left, *refs):
    pieces, (out, object_grad, total, semaphores) = refs[:-4], refs[-4:]
    count, depth = len(pieces) // 2, pieces[0].shape[0]
    copies = []
    for index, piece in enumerate(pieces):
        half = place[0] if index < count else 1 - place[0]
        chunk = half * count + jnp.bitwise_xor(place[1], index % count)
        rows = pl.ds(pl.multiple_of(chunk * depth, depth), depth)
        copies.append(pltpu.make_async_copy(piece, out.at[rows, :], semaphores.at[index]))
    total[...] = own_grad[...] + above[0] + left[...]
    copies.insert(0, pltpu.make_async_copy(total, object_grad, semaphores.at[len(pieces)]))
    for copy in copies:
        copy.start()
    for copy in copies:
        copy.wait()


def on_device(object_tiles, probe, amplitudes, offsets, counts):
    modes, edge = probe.shape[1], probe.shape[2]
    slot_total = amplitudes.shape[1]
    n_region, n_pos = lax.axis_size("region"), lax.axis_size("pos")
    total = n_region * n_pos
    axes = ("region", "pos")
    f32 = jnp.float32

    row_index, column_index = lax.axis_index("region"), lax.axis_index("pos")

    def shifted(block, down, across):
        route = [
            (i * n_pos + j, (i + down) % n_region * n_pos + (j + across) % n_pos)
            for i in range(n_region)
            for j in range(n_pos)
        ]
        return lax.ppermute(block, axes, route)

    pieces = n_pos // 2

    def partner(block, mask):
        return lax.ppermute(block, axes, [(i, i ^ mask) for i in range(total)])

    place = jnp.stack(
        [
            column_index & 1,
            column_index >> 1,
            (row_index < n_region - 1).astype(jnp.int32),
            (column_index < n_pos - 1).astype(jnp.int32),
            row_index & 1,
        ]
    )

    def swapped(first, across):
        route = []
        for i in range(n_region):
            a = i + 1 if (i - first) % 2 == 0 else i - 1
            for j in range(n_pos):
                if 0 <= a < n_region:
                    target = a * n_pos + (j + across) % n_pos
                else:
                    target = i * n_pos + ((j + across) % n_pos if across else j ^ 1)
                route.append((i * n_pos + j, target))
        return lax.ppermute(object_tiles, axes, route)

    right = shifted(object_tiles, 0, -1)
    halo = (swapped(0, 0), swapped(1, 0), right, swapped(0, -1), swapped(1, -1))

    lines = 2 * modes * edge
    smem = pl.BlockSpec(memory_space=pltpu.SMEM)
    vmem = pl.BlockSpec(memory_space=pltpu.VMEM)
    held = jnp.concatenate(
        [
            probe.reshape(2, -1, edge),
            amplitudes.reshape(2, -1, edge),
            jnp.asarray(dft_tables(edge)),
        ],
        axis=1,
    )
    quadrant = jax.ShapeDtypeStruct((2, edge, edge), f32)
    part = jax.ShapeDtypeStruct((pieces, lines // n_pos, edge), f32)
    scale = 1.0 / math.sqrt(total * slot_total)
    own_grad, right_grad, lower_grads, keep, send = pl.pallas_call(
        functools.partial(slots_kernel, scale, modes, slot_total, edge),
        out_shape=(quadrant, quadrant, jax.ShapeDtypeStruct((2, 2, edge, edge), f32), part, part),
        in_specs=[pl.BlockSpec(memory_space=pl.ANY)] * 2 + [smem] + [vmem] * 7,
        out_specs=(vmem,) * 5,
        scratch_shapes=[pltpu.VMEM((4, 2 * edge, 2 * edge), jnp.bfloat16)]
        + [pltpu.VMEM((2, 2 * edge, edge), f32)] * 4
        + [
            pltpu.VMEM((2, modes, edge, edge), f32),
            pltpu.SMEM(offsets.shape, jnp.int32),
            pltpu.SMEM(counts.shape, jnp.int32),
            pltpu.SemaphoreType.DMA((2,)),
        ],
        compiler_params=pltpu.CompilerParams(vmem_limit_bytes=16 * 1024 * 1024),
    )(offsets, counts, place, held, object_tiles, *halo)

    half = keep + partner(send, 1)
    above = shifted(lower_grads, 1, 0)
    got = [partner(half[k], 2 * k) for k in range(1, pieces)]
    got[0], above = lax.optimization_barrier((got[0], above))
    chunk = functools.reduce(jnp.add, got, half[0])
    terms = [chunk] + [partner(chunk, n_pos * k) for k in range(1, n_region)]
    left = shifted(right_grad + above[1], 0, 1)
    while len(terms) > 1:
        terms = [terms[k] + terms[k + 1] for k in range(0, len(terms), 2)]
    chunk = terms[0]
    gathered = [chunk] + [partner(chunk, 2 * k) for k in range(1, pieces)]
    gathered[1], left = lax.optimization_barrier((gathered[1], left))
    gathered += [partner(piece, 1) for piece in gathered]
    probe_grad, object_grad = pl.pallas_call(
        join_kernel,
        out_shape=(jax.ShapeDtypeStruct((lines, edge), f32), quadrant),
        in_specs=[smem] + [vmem] * (3 + n_pos),
        out_specs=(pl.BlockSpec(memory_space=pl.ANY),) * 2,
        scratch_shapes=[pltpu.VMEM((2, edge, edge), f32), pltpu.SemaphoreType.DMA((n_pos + 1,))],
        compiler_params=pltpu.CompilerParams(vmem_limit_bytes=4 * 1024 * 1024),
    )(place, own_grad, above, left, *gathered)
    return (object_grad, probe_grad.reshape(probe.shape))


def solution(mesh):
    return jax.shard_map(
        on_device,
        mesh=mesh,
        in_specs=(
            P(None, "region", "pos"),
            P(),
            P("region", "pos", None, None),
            P("region", None, "pos"),
            P("region", "pos"),
        ),
        out_specs=(P(None, "region", "pos"), P()),
        check_vma=False,
    )
```

```python
import functools
import math

import jax
import jax.numpy as jnp
import numpy as np
from jax import lax
from jax.experimental import pallas as pl
from jax.experimental.pallas import tpu as pltpu
from jax.sharding import PartitionSpec as P


def dft_tables(order):
    index = np.arange(order)
    angle = (index[:, None] * index[None, :] % order) * (2.0 * math.pi / order)
    tables = np.stack([np.cos(angle), np.sin(angle)]) / math.sqrt(order)
    return tables.astype(np.float32)


def split(value):
    high = value.astype(jnp.bfloat16)
    low = (value - high.astype(jnp.float32)).astype(jnp.bfloat16)
    return high, low


def dot(a, b):
    return jnp.dot(a, b, preferred_element_type=jnp.float32)


def times_table(values, table_high, table_low, sums):
    parts = [split(value) for value in values]
    units = range(len(sums))
    rows = sums[0][0].shape[0]
    for unit in units:
        pltpu.matmul_push_rhs(table_high, 0, unit)
        pltpu.matmul_push_rhs(table_low, 1, unit)
    for index, (high, low) in enumerate(parts):
        for unit in units:
            mine = slice(unit * rows, (unit + 1) * rows)
            pltpu.matmul_acc_lhs(sums[unit][index], high[mine], None if index else 0)
            pltpu.matmul_acc_lhs(sums[unit][index], low[mine])
    results = []
    for index, (high, low) in enumerate(parts):
        for unit in units:
            mine = slice(unit * rows, (unit + 1) * rows)
            pltpu.matmul_acc_lhs(sums[unit][index], high[mine], None if index else 1)
        results.append(jnp.concatenate([pltpu.matmul_pop(sums[unit][index]) for unit in units], axis=0))
    return results


def table_times(table_high, table_low, values, sums):
    units = range(len(sums))
    columns = sums[0][0].shape[1]
    results = []
    for index, value in enumerate(values):
        high, low = split(value)
        for unit in units:
            mine = slice(unit * columns, (unit + 1) * columns)
            pltpu.matmul_push_rhs(high[:, mine], 0, unit)
            pltpu.matmul_push_rhs(low[:, mine], 1, unit)
            pltpu.matmul_acc_lhs(sums[unit][index], table_high, 0)
            pltpu.matmul_acc_lhs(sums[unit][index], table_low)
            pltpu.matmul_acc_lhs(sums[unit][index], table_high, 1)
        results.append(jnp.concatenate([pltpu.matmul_pop(sums[unit][index]) for unit in units], axis=1))
    return results


def slots_kernel(
    scale, modes, slot_total, edge, offsets, place, counts, held, own, below, other_below, right, diag, other_diag,
    own_grad, right_grad, lower_grads, keep, send,
    tables, field_left, field_right, grad_left, grad_right, probe_sum, corners, semaphore,
):
    scalars = pltpu.make_async_copy(offsets, corners, semaphore)
    scalars.start()

    def probe(part, mode):
        return held[part, pl.ds(mode * edge, edge), :]

    amplitude_rows = modes * edge
    table_rows = amplitude_rows + slot_total * edge // 2
    cos_high, cos_low = split(held[0, pl.ds(table_rows, edge), :])
    sin_high, sin_low = split(held[1, pl.ds(table_rows, edge), :])
    spread_high, spread_low, turn_high, turn_low = (tables.at[k] for k in range(4))
    for spread, turn, cos_part, sin_part in (
        (spread_high, turn_high, cos_high, sin_high),
        (spread_low, turn_low, cos_low, sin_low),
    ):
        for target, upper, lower in ((spread, -sin_part, sin_part), (turn, sin_part, -sin_part)):
            target[:edge, :edge] = cos_part
            target[:edge, edge:] = upper
            target[edge:, :edge] = lower
            target[edge:, edge:] = cos_part
    has_below, has_right, odd_row = place[2] > 0, place[3] > 0, place[4] > 0
    has_diag = jnp.logical_and(has_below, has_right)

    def present(flag, value):
        return jnp.where(flag, value, jnp.zeros_like(value))

    def arrived(flag, first, second):
        return present(flag, jnp.where(odd_row, second[...], first[...]).astype(jnp.float32))

    field_left[:, :edge] = own[...].astype(jnp.float32)
    field_left[:, edge:] = arrived(has_below, below, other_below)
    field_right[:, :edge] = present(has_right, right[...].astype(jnp.float32))
    field_right[:, edge:] = arrived(has_diag, diag, other_diag)
    grad_left[...] = jnp.zeros_like(grad_left)
    grad_right[...] = jnp.zeros_like(grad_right)
    lane = lax.broadcasted_iota(jnp.int32, (edge, edge), 1)
    scalars.wait()
    live = jnp.broadcast_to(counts[...], (edge, edge))
    def visit(*accumulators):
        sums = accumulators[:slot_total], accumulators[slot_total:]
        slots = range(slot_total)
        corner = [(corners[0, 0, slot], corners[0, 1, slot]) for slot in slots]
        in_left = [lane >= col0 for _, col0 in corner]
        crops, halves = [], []
        for slot in slots:
            row0, col0 = corner[slot]
            rows, shift = pl.ds(row0, edge), lax.rem(edge - col0, edge)
            crop_r, crop_i = (
                pltpu.roll(
                    jnp.where(in_left[slot], field_left[part, rows, :], field_right[part, rows, :]), shift, 1
                )
                for part in range(2)
            )
            exits = [
                jnp.concatenate(
                    [
                        probe(0, m) * crop_r - probe(1, m) * crop_i,
                        probe(0, m) * crop_i + probe(1, m) * crop_r,
                    ],
                    axis=1,
                )
                for m in range(modes)
            ]
            crops.append((crop_r, crop_i))
            halves.append(jnp.concatenate(exits, axis=0))
        turned = []
        for half in times_table(halves, spread_high[...], spread_low[...], sums):
            parts = [
                [half[m * edge : (m + 1) * edge, part * edge : (part + 1) * edge] for m in range(modes)]
                for part in range(2)
            ]
            turned.append(jnp.concatenate([jnp.concatenate(part, axis=1) for part in parts], axis=0))
        fars = table_times(turn_high[...], turn_low[...], turned, sums)
        halves = []
        for slot in slots:
            far = fars[slot]
            squares = far * far
            squares = squares[:edge] + squares[edge:]
            intensity = functools.reduce(
                jnp.add, [squares[:, m * edge : (m + 1) * edge] for m in range(modes)]
            )
            half_slots = slot_total // 2
            amplitude = held[slot // half_slots, pl.ds(amplitude_rows + slot % half_slots * edge, edge), :]
            factor = jnp.where(live > slot, 1.0 - amplitude * lax.rsqrt(intensity + 1.0), 0.0)
            factor = jnp.concatenate([factor] * modes, axis=1)
            halves.append(far * jnp.concatenate([factor, factor], axis=0))
        turned = []
        for half in table_times(spread_high[...], spread_low[...], halves, sums):
            parts = [
                [half[part * edge : (part + 1) * edge, m * edge : (m + 1) * edge] for part in range(2)]
                for m in range(modes)
            ]
            turned.append(jnp.concatenate([jnp.concatenate(part, axis=1) for part in parts], axis=0))
        backs = times_table(turned, turn_high[...], turn_low[...], sums)
        for slot in slots:
            crop_r, crop_i = crops[slot]
            row0, col0 = corner[slot]
            rows = pl.ds(row0, edge)
            object_r = jnp.zeros((edge, edge), jnp.float32)
            object_i = jnp.zeros((edge, edge), jnp.float32)
            for m in range(modes):
                back_r = backs[slot][m * edge : (m + 1) * edge, :edge]
                back_i = backs[slot][m * edge : (m + 1) * edge, edge:]
                object_r += probe(0, m) * back_r + probe(1, m) * back_i
                object_i += probe(0, m) * back_i - probe(1, m) * back_r
                term_r = crop_r * back_r + crop_i * back_i
                term_i = crop_r * back_i - crop_i * back_r
                if slot == 0:
                    probe_sum[0, m] = term_r
                    probe_sum[1, m] = term_i
                else:
                    probe_sum[0, m] += term_r
                    probe_sum[1, m] += term_i
            for part, term in enumerate((object_r, object_i)):
                term = pltpu.roll(term, col0, 1)
                grad_left[part, rows, :] += jnp.where(in_left[slot], term, 0.0)
                grad_right[part, rows, :] += jnp.where(in_left[slot], 0.0, term)

    pl.run_scoped(
        visit,
        *(
            pltpu.ACC(unit)((modes // 2 * edge, 2 * edge), jnp.float32)
            for unit in range(2)
            for _ in range(slot_total)
        ),
    )
    own_grad[...] = grad_left[:, :edge]
    right_grad[...] = present(has_right, grad_right[:, :edge])
    lower_grads[0] = present(has_below, grad_left[:, edge:])
    lower_grads[1] = present(has_diag, grad_right[:, edge:])
    flat = probe_sum.reshape(2 * modes * edge, edge)
    pieces, depth = keep.shape[0], keep.shape[1]
    for target, half in ((keep, place[0]), (send, 1 - place[0])):
        for position in range(pieces):
            chunk = half * pieces + jnp.bitwise_xor(place[1], position)
            rows = pl.ds(pl.multiple_of(chunk * depth, depth), depth)
            target[position] = flat[rows, :] * scale


def join_kernel(place, own_grad, above, left, *refs):
    pieces, (out, object_grad, total, semaphores) = refs[:-4], refs[-4:]
    count, depth = len(pieces) // 2, pieces[0].shape[0]
    copies = []
    for index, piece in enumerate(pieces):
        half = place[0] if index < count else 1 - place[0]
        chunk = half * count + jnp.bitwise_xor(place[1], index % count)
        rows = pl.ds(pl.multiple_of(chunk * depth, depth), depth)
        copies.append(pltpu.make_async_copy(piece, out.at[rows, :], semaphores.at[index]))
    total[...] = own_grad[...] + above[0] + left[...]
    copies.insert(0, pltpu.make_async_copy(total, object_grad, semaphores.at[len(pieces)]))
    for copy in copies:
        copy.start()
    for copy in copies:
        copy.wait()


def on_device(object_tiles, probe, amplitudes, offsets, counts):
    modes, edge = probe.shape[1], probe.shape[2]
    slot_total = amplitudes.shape[1]
    n_region, n_pos = lax.axis_size("region"), lax.axis_size("pos")
    total = n_region * n_pos
    axes = ("region", "pos")
    f32 = jnp.float32

    row_index, column_index = lax.axis_index("region"), lax.axis_index("pos")

    def shifted(block, down, across):
        route = [
            (i * n_pos + j, (i + down) % n_region * n_pos + (j + across) % n_pos)
            for i in range(n_region)
            for j in range(n_pos)
        ]
        return lax.ppermute(block, axes, route)

    pieces = n_pos // 2

    def partner(block, mask):
        return lax.ppermute(block, axes, [(i, i ^ mask) for i in range(total)])

    place = jnp.stack(
        [
            column_index & 1,
            column_index >> 1,
            (row_index < n_region - 1).astype(jnp.int32),
            (column_index < n_pos - 1).astype(jnp.int32),
            row_index & 1,
        ]
    )

    def swapped(first, across):
        route = []
        for i in range(n_region):
            a = i + 1 if (i - first) % 2 == 0 else i - 1
            for j in range(n_pos):
                if 0 <= a < n_region:
                    target = a * n_pos + (j + across) % n_pos
                else:
                    target = i * n_pos + ((j + across) % n_pos if across else j ^ 1)
                route.append((i * n_pos + j, target))
        return lax.ppermute(object_tiles, axes, route)

    right = shifted(object_tiles, 0, -1)
    halo = (swapped(0, 0), swapped(1, 0), right, swapped(0, -1), swapped(1, -1))

    lines = 2 * modes * edge
    smem = pl.BlockSpec(memory_space=pltpu.SMEM)
    vmem = pl.BlockSpec(memory_space=pltpu.VMEM)
    held = jnp.concatenate(
        [
            probe.reshape(2, -1, edge),
            amplitudes.reshape(2, -1, edge),
            jnp.asarray(dft_tables(edge)),
        ],
        axis=1,
    )
    quadrant = jax.ShapeDtypeStruct((2, edge, edge), f32)
    part = jax.ShapeDtypeStruct((pieces, lines // n_pos, edge), f32)
    scale = 1.0 / math.sqrt(total * slot_total)
    own_grad, right_grad, lower_grads, keep, send = pl.pallas_call(
        functools.partial(slots_kernel, scale, modes, slot_total, edge),
        out_shape=(quadrant, quadrant, jax.ShapeDtypeStruct((2, 2, edge, edge), f32), part, part),
        in_specs=[pl.BlockSpec(memory_space=pl.ANY), smem] + [vmem] * 8,
        out_specs=(vmem,) * 5,
        scratch_shapes=[pltpu.VMEM((4, 2 * edge, 2 * edge), jnp.bfloat16)]
        + [pltpu.VMEM((2, 2 * edge, edge), f32)] * 4
        + [
            pltpu.VMEM((2, modes, edge, edge), f32),
            pltpu.SMEM(offsets.shape, jnp.int32),
            pltpu.SemaphoreType.DMA,
        ],
        compiler_params=pltpu.CompilerParams(vmem_limit_bytes=16 * 1024 * 1024),
    )(offsets, place, counts, held, object_tiles, *halo)

    half = keep + partner(send, 1)
    above = shifted(lower_grads, 1, 0)
    got = [partner(half[k], 2 * k) for k in range(1, pieces)]
    got[0], above = lax.optimization_barrier((got[0], above))
    chunk = functools.reduce(jnp.add, got, half[0])
    terms = [chunk] + [partner(chunk, n_pos * k) for k in range(1, n_region)]
    left = shifted(right_grad + above[1], 0, 1)
    while len(terms) > 1:
        terms = [terms[k] + terms[k + 1] for k in range(0, len(terms), 2)]
    chunk = terms[0]
    gathered = [chunk] + [partner(chunk, 2 * k) for k in range(1, pieces)]
    gathered[1], left = lax.optimization_barrier((gathered[1], left))
    gathered += [partner(piece, 1) for piece in gathered]
    probe_grad, object_grad = pl.pallas_call(
        join_kernel,
        out_shape=(jax.ShapeDtypeStruct((lines, edge), f32), quadrant),
        in_specs=[smem] + [vmem] * (3 + n_pos),
        out_specs=(pl.BlockSpec(memory_space=pl.ANY),) * 2,
        scratch_shapes=[pltpu.VMEM((2, edge, edge), f32), pltpu.SemaphoreType.DMA((n_pos + 1,))],
        compiler_params=pltpu.CompilerParams(vmem_limit_bytes=4 * 1024 * 1024),
    )(place, own_grad, above, left, *gathered)
    return (object_grad, probe_grad.reshape(probe.shape))


def solution(mesh):
    return jax.shard_map(
        on_device,
        mesh=mesh,
        in_specs=(
            P(None, "region", "pos"),
            P(),
            P("region", "pos", None, None),
            P("region", None, "pos"),
            P("region", "pos"),
        ),
        out_specs=(P(None, "region", "pos"), P()),
        check_vma=False,
    )
```

```python
import functools
import math

import jax
import jax.numpy as jnp
import numpy as np
from jax import lax
from jax.experimental import pallas as pl
from jax.experimental.pallas import tpu as pltpu
from jax.sharding import PartitionSpec as P


def dft_tables(order):
    index = np.arange(order)
    angle = (index[:, None] * index[None, :] % order) * (2.0 * math.pi / order)
    tables = np.stack([np.cos(angle), np.sin(angle)]) / math.sqrt(order)
    return tables.astype(np.float32)


def split(value):
    high = value.astype(jnp.bfloat16)
    low = (value - high.astype(jnp.float32)).astype(jnp.bfloat16)
    return high, low


def dot(a, b):
    return jnp.dot(a, b, preferred_element_type=jnp.float32)


def times_table(value, table_high, table_low):
    high, low = split(value)
    rows = value.shape[0]
    both = dot(jnp.concatenate([high, low], axis=0), table_high)
    return both[:rows] + (both[rows:] + dot(high, table_low))


def table_times(tables, value):
    high, low = split(value)
    rows = tables.shape[0] // 2
    both = dot(tables, high)
    return both[:rows] + (both[rows:] + dot(tables[:rows], low))


def slots_kernel(
    scale, modes, slot_total, edge, offsets, counts, place, probes, held, own, below, other_below, right, diag, other_diag,
    own_grad, right_grad, lower_grads, keep, send,
    tables, field_left, field_right, grad_left, grad_right, probe_sum, corners, live, semaphores,
):
    scalars = (
        pltpu.make_async_copy(offsets, corners, semaphores.at[0]),
        pltpu.make_async_copy(counts, live, semaphores.at[1]),
    )
    for copy in scalars:
        copy.start()

    def probe(part, mode):
        return probes[part, mode]

    amplitude_rows = 0
    table_rows = amplitude_rows + slot_total * edge // 2
    cos_high, cos_low = split(held[0, pl.ds(table_rows, edge), :])
    sin_high, sin_low = split(held[1, pl.ds(table_rows, edge), :])
    spread_high, spread_low, turn_high, turn_low = (tables.at[k] for k in range(4))
    for spread, turn, cos_part, sin_part in (
        (spread_high, turn_high, cos_high, sin_high),
        (spread_low, turn_low, cos_low, sin_low),
    ):
        for target, upper, lower in ((spread, -sin_part, sin_part), (turn, sin_part, -sin_part)):
            target[:edge, :edge] = cos_part
            target[:edge, edge:] = upper
            target[edge:, :edge] = lower
            target[edge:, edge:] = cos_part
    turn_both = jnp.concatenate([turn_high[...], turn_low[...]], axis=0)
    spread_both = jnp.concatenate([spread_high[...], spread_low[...]], axis=0)
    has_below, has_right, odd_row = place[2] > 0, place[3] > 0, place[4] > 0
    has_diag = jnp.logical_and(has_below, has_right)

    def present(flag, value):
        return jnp.where(flag, value, jnp.zeros_like(value))

    def arrived(flag, first, second):
        return present(flag, jnp.where(odd_row, second[...], first[...]).astype(jnp.float32))

    field_left[:, :edge] = own[...].astype(jnp.float32)
    field_left[:, edge:] = arrived(has_below, below, other_below)
    field_right[:, :edge] = present(has_right, right[...].astype(jnp.float32))
    field_right[:, edge:] = arrived(has_diag, diag, other_diag)
    grad_left[...] = jnp.zeros_like(grad_left)
    grad_right[...] = jnp.zeros_like(grad_right)
    lane = lax.broadcasted_iota(jnp.int32, (edge, edge), 1)
    for copy in scalars:
        copy.wait()
    slots = range(slot_total)
    corner = [(corners[0, 0, slot], corners[0, 1, slot]) for slot in slots]
    in_left = [lane >= col0 for _, col0 in corner]
    crops, halves = [], []
    for slot in slots:
        row0, col0 = corner[slot]
        rows, shift = pl.ds(row0, edge), lax.rem(edge - col0, edge)
        crop_r, crop_i = (
            pltpu.roll(
                jnp.where(in_left[slot], field_left[part, rows, :], field_right[part, rows, :]), shift, 1
            )
            for part in range(2)
        )
        exits = [
            jnp.concatenate(
                [
                    probe(0, m) * crop_r - probe(1, m) * crop_i,
                    probe(0, m) * crop_i + probe(1, m) * crop_r,
                ],
                axis=1,
            )
            for m in range(modes)
        ]
        crops.append((crop_r, crop_i))
        halves.append(times_table(jnp.concatenate(exits, axis=0), spread_high[...], spread_low[...]))
    fars = []
    for half in halves:
        parts = [
            [half[m * edge : (m + 1) * edge, part * edge : (part + 1) * edge] for m in range(modes)]
            for part in range(2)
        ]
        half = jnp.concatenate([jnp.concatenate(part, axis=1) for part in parts], axis=0)
        fars.append(table_times(turn_both, half))
    halves = []
    for slot in slots:
        far = fars[slot]
        squares = far * far
        squares = squares[:edge] + squares[edge:]
        intensity = functools.reduce(
            jnp.add, [squares[:, m * edge : (m + 1) * edge] for m in range(modes)]
        )
        weight = (slot < live[0, 0]).astype(jnp.float32)
        half_slots = slot_total // 2
        amplitude = held[slot // half_slots, pl.ds(amplitude_rows + slot % half_slots * edge, edge), :]
        factor = weight * (1.0 - amplitude * lax.rsqrt(intensity + 1.0))
        factor = jnp.concatenate([factor] * modes, axis=1)
        residual = far * jnp.concatenate([factor, factor], axis=0)
        halves.append(table_times(spread_both, residual))
    backs = []
    for half in halves:
        parts = [
            [half[part * edge : (part + 1) * edge, m * edge : (m + 1) * edge] for part in range(2)]
            for m in range(modes)
        ]
        half = jnp.concatenate([jnp.concatenate(part, axis=1) for part in parts], axis=0)
        backs.append(times_table(half, turn_high[...], turn_low[...]))
    for slot in slots:
        crop_r, crop_i = crops[slot]
        row0, col0 = corner[slot]
        rows = pl.ds(row0, edge)
        object_r = jnp.zeros((edge, edge), jnp.float32)
        object_i = jnp.zeros((edge, edge), jnp.float32)
        for m in range(modes):
            back_r = backs[slot][m * edge : (m + 1) * edge, :edge]
            back_i = backs[slot][m * edge : (m + 1) * edge, edge:]
            object_r += probe(0, m) * back_r + probe(1, m) * back_i
            object_i += probe(0, m) * back_i - probe(1, m) * back_r
            term_r = crop_r * back_r + crop_i * back_i
            term_i = crop_r * back_i - crop_i * back_r
            if slot == 0:
                probe_sum[0, m] = term_r
                probe_sum[1, m] = term_i
            else:
                probe_sum[0, m] += term_r
                probe_sum[1, m] += term_i
        for part, term in enumerate((object_r, object_i)):
            term = pltpu.roll(term, col0, 1)
            grad_left[part, rows, :] += jnp.where(in_left[slot], term, 0.0)
            grad_right[part, rows, :] += jnp.where(in_left[slot], 0.0, term)
    own_grad[...] = grad_left[:, :edge]
    right_grad[...] = present(has_right, grad_right[:, :edge])
    lower_grads[0] = present(has_below, grad_left[:, edge:])
    lower_grads[1] = present(has_diag, grad_right[:, edge:])
    flat = probe_sum.reshape(2 * modes * edge, edge)
    pieces, depth = keep.shape[0], keep.shape[1]
    for target, half in ((keep, place[0]), (send, 1 - place[0])):
        for position in range(pieces):
            chunk = half * pieces + jnp.bitwise_xor(place[1], position)
            rows = pl.ds(pl.multiple_of(chunk * depth, depth), depth)
            target[position] = flat[rows, :] * scale


def join_kernel(place, own_grad, above, left, *refs):
    pieces, (out, object_grad, total, semaphores) = refs[:-4], refs[-4:]
    count, depth = len(pieces) // 2, pieces[0].shape[0]
    copies = []
    for index, piece in enumerate(pieces):
        half = place[0] if index < count else 1 - place[0]
        chunk = half * count + jnp.bitwise_xor(place[1], index % count)
        rows = pl.ds(pl.multiple_of(chunk * depth, depth), depth)
        copies.append(pltpu.make_async_copy(piece, out.at[rows, :], semaphores.at[index]))
    total[...] = own_grad[...] + above[0] + left[...]
    copies.insert(0, pltpu.make_async_copy(total, object_grad, semaphores.at[len(pieces)]))
    for copy in copies:
        copy.start()
    for copy in copies:
        copy.wait()


def on_device(object_tiles, probe, amplitudes, offsets, counts):
    modes, edge = probe.shape[1], probe.shape[2]
    slot_total = amplitudes.shape[1]
    n_region, n_pos = lax.axis_size("region"), lax.axis_size("pos")
    total = n_region * n_pos
    axes = ("region", "pos")
    f32 = jnp.float32

    row_index, column_index = lax.axis_index("region"), lax.axis_index("pos")

    def shifted(block, down, across):
        route = [
            (i * n_pos + j, (i + down) % n_region * n_pos + (j + across) % n_pos)
            for i in range(n_region)
            for j in range(n_pos)
        ]
        return lax.ppermute(block, axes, route)

    pieces = n_pos // 2

    def partner(block, mask):
        return lax.ppermute(block, axes, [(i, i ^ mask) for i in range(total)])

    place = jnp.stack(
        [
            column_index & 1,
            column_index >> 1,
            (row_index < n_region - 1).astype(jnp.int32),
            (column_index < n_pos - 1).astype(jnp.int32),
            row_index & 1,
        ]
    )

    def swapped(first, across):
        route = []
        for i in range(n_region):
            a = i + 1 if (i - first) % 2 == 0 else i - 1
            for j in range(n_pos):
                if 0 <= a < n_region:
                    target = a * n_pos + (j + across) % n_pos
                else:
                    target = i * n_pos + ((j + across) % n_pos if across else j ^ 1)
                route.append((i * n_pos + j, target))
        return lax.ppermute(object_tiles, axes, route)

    right = shifted(object_tiles, 0, -1)
    halo = (swapped(0, 0), swapped(1, 0), right, swapped(0, -1), swapped(1, -1))

    lines = 2 * modes * edge
    smem = pl.BlockSpec(memory_space=pltpu.SMEM)
    vmem = pl.BlockSpec(memory_space=pltpu.VMEM)
    held = jnp.concatenate(
        [
            amplitudes.reshape(2, -1, edge),
            jnp.asarray(dft_tables(edge)),
        ],
        axis=1,
    )
    quadrant = jax.ShapeDtypeStruct((2, edge, edge), f32)
    part = jax.ShapeDtypeStruct((pieces, lines // n_pos, edge), f32)
    scale = 1.0 / math.sqrt(total * slot_total)
    own_grad, right_grad, lower_grads, keep, send = pl.pallas_call(
        functools.partial(slots_kernel, scale, modes, slot_total, edge),
        out_shape=(quadrant, quadrant, jax.ShapeDtypeStruct((2, 2, edge, edge), f32), part, part),
        in_specs=[pl.BlockSpec(memory_space=pl.ANY)] * 2 + [smem] + [vmem] * 8,
        out_specs=(vmem,) * 5,
        scratch_shapes=[pltpu.VMEM((4, 2 * edge, 2 * edge), jnp.bfloat16)]
        + [pltpu.VMEM((2, 2 * edge, edge), f32)] * 4
        + [
            pltpu.VMEM((2, modes, edge, edge), f32),
            pltpu.SMEM(offsets.shape, jnp.int32),
            pltpu.SMEM(counts.shape, jnp.int32),
            pltpu.SemaphoreType.DMA((2,)),
        ],
        compiler_params=pltpu.CompilerParams(vmem_limit_bytes=16 * 1024 * 1024),
    )(offsets, counts, place, probe, held, object_tiles, *halo)

    half = keep + partner(send, 1)
    above = shifted(lower_grads, 1, 0)
    got = [partner(half[k], 2 * k) for k in range(1, pieces)]
    got[0], above = lax.optimization_barrier((got[0], above))
    chunk = functools.reduce(jnp.add, got, half[0])
    terms = [chunk] + [partner(chunk, n_pos * k) for k in range(1, n_region)]
    left = shifted(right_grad + above[1], 0, 1)
    while len(terms) > 1:
        terms = [terms[k] + terms[k + 1] for k in range(0, len(terms), 2)]
    chunk = terms[0]
    gathered = [chunk] + [partner(chunk, 2 * k) for k in range(1, pieces)]
    gathered[1], left = lax.optimization_barrier((gathered[1], left))
    gathered += [partner(piece, 1) for piece in gathered]
    probe_grad, object_grad = pl.pallas_call(
        join_kernel,
        out_shape=(jax.ShapeDtypeStruct((lines, edge), f32), quadrant),
        in_specs=[smem] + [vmem] * (3 + n_pos),
        out_specs=(pl.BlockSpec(memory_space=pl.ANY),) * 2,
        scratch_shapes=[pltpu.VMEM((2, edge, edge), f32), pltpu.SemaphoreType.DMA((n_pos + 1,))],
        compiler_params=pltpu.CompilerParams(vmem_limit_bytes=4 * 1024 * 1024),
    )(place, own_grad, above, left, *gathered)
    return (object_grad, probe_grad.reshape(probe.shape))


def solution(mesh):
    return jax.shard_map(
        on_device,
        mesh=mesh,
        in_specs=(
            P(None, "region", "pos"),
            P(),
            P("region", "pos", None, None),
            P("region", None, "pos"),
            P("region", "pos"),
        ),
        out_specs=(P(None, "region", "pos"), P()),
        check_vma=False,
    )
```

```python
import functools
import math

import jax
import jax.numpy as jnp
import numpy as np
from jax import lax
from jax.experimental import pallas as pl
from jax.experimental.pallas import tpu as pltpu
from jax.sharding import PartitionSpec as P


def dft_tables(order):
    index = np.arange(order)
    angle = (index[:, None] * index[None, :] % order) * (2.0 * math.pi / order)
    tables = np.stack([np.cos(angle), np.sin(angle)]) / math.sqrt(order)
    return tables.astype(np.float32)


def split(value):
    high = value.astype(jnp.bfloat16)
    low = (value - high.astype(jnp.float32)).astype(jnp.bfloat16)
    return high, low


def dot(a, b):
    return jnp.dot(a, b, preferred_element_type=jnp.float32)


def times_table(value, table_high, table_low):
    high, low = split(value)
    rows = value.shape[0]
    both = dot(jnp.concatenate([high, low], axis=0), table_high)
    return both[:rows] + (both[rows:] + dot(high, table_low))


def table_times(tables, value):
    high, low = split(value)
    rows = tables.shape[0] // 2
    both = dot(tables, high)
    return both[:rows] + (both[rows:] + dot(tables[:rows], low))


def slots_kernel(
    scale, modes, slot_total, edge, offsets, counts, place, probes, held, own, below, other_below, right, diag, other_diag,
    own_grad, right_grad, lower_grads, keep, send,
    tables, field_left, field_right, grad_left, grad_right, probe_sum, corners, live, semaphores,
):
    scalars = (
        pltpu.make_async_copy(offsets, corners, semaphores.at[0]),
        pltpu.make_async_copy(counts, live, semaphores.at[1]),
    )
    for copy in scalars:
        copy.start()

    def probe(part, mode):
        return probes[part, mode]

    amplitude_rows = 0
    table_rows = amplitude_rows + slot_total * edge // 2
    cos_high, cos_low = split(held[0, pl.ds(table_rows, edge), :])
    sin_high, sin_low = split(held[1, pl.ds(table_rows, edge), :])
    spread_high, spread_low, turn_high, turn_low = (tables.at[k] for k in range(4))
    for spread, turn, cos_part, sin_part in (
        (spread_high, turn_high, cos_high, sin_high),
        (spread_low, turn_low, cos_low, sin_low),
    ):
        for target, upper, lower in ((spread, -sin_part, sin_part), (turn, sin_part, -sin_part)):
            target[:edge, :edge] = cos_part
            target[:edge, edge:] = upper
            target[edge:, :edge] = lower
            target[edge:, edge:] = cos_part
    turn_both = jnp.concatenate([turn_high[...], turn_low[...]], axis=0)
    spread_both = jnp.concatenate([spread_high[...], spread_low[...]], axis=0)
    has_below, has_right, odd_row = place[2] > 0, place[3] > 0, place[4] > 0
    has_diag = jnp.logical_and(has_below, has_right)

    def present(flag, value):
        return jnp.where(flag, value, jnp.zeros_like(value))

    def arrived(flag, first, second):
        return present(flag, jnp.where(odd_row, second[...], first[...]).astype(jnp.float32))

    field_left[:, :edge] = own[...].astype(jnp.float32)
    field_left[:, edge:] = arrived(has_below, below, other_below)
    field_right[:, :edge] = present(has_right, right[...].astype(jnp.float32))
    field_right[:, edge:] = arrived(has_diag, diag, other_diag)
    grad_left[...] = jnp.zeros_like(grad_left)
    grad_right[...] = jnp.zeros_like(grad_right)
    lane = lax.broadcasted_iota(jnp.int32, (edge, edge), 1)
    for copy in scalars:
        copy.wait()
    slots = range(slot_total)
    corner = [(corners[0, 0, slot], corners[0, 1, slot]) for slot in slots]
    in_left = [lane >= col0 for _, col0 in corner]
    crops, halves = [], []
    for slot in slots:
        row0, col0 = corner[slot]
        rows, shift = pl.ds(row0, edge), lax.rem(edge - col0, edge)
        crop_r, crop_i = (
            pltpu.roll(
                jnp.where(in_left[slot], field_left[part, rows, :], field_right[part, rows, :]), shift, 1
            )
            for part in range(2)
        )
        exits = [
            jnp.concatenate(
                [
                    probe(0, m) * crop_r - probe(1, m) * crop_i,
                    probe(0, m) * crop_i + probe(1, m) * crop_r,
                ],
                axis=1,
            )
            for m in range(modes)
        ]
        crops.append((crop_r, crop_i))
        halves.append(times_table(jnp.concatenate(exits, axis=0), spread_high[...], spread_low[...]))
    fars = []
    for half in halves:
        parts = [
            [half[m * edge : (m + 1) * edge, part * edge : (part + 1) * edge] for m in range(modes)]
            for part in range(2)
        ]
        half = jnp.concatenate([jnp.concatenate(part, axis=1) for part in parts], axis=0)
        fars.append(table_times(turn_both, half))
    halves = []
    for slot in slots:
        far = fars[slot]
        squares = far * far
        squares = squares[:edge] + squares[edge:]
        intensity = functools.reduce(
            jnp.add, [squares[:, m * edge : (m + 1) * edge] for m in range(modes)]
        )
        weight = (slot < live[0, 0]).astype(jnp.float32)
        half_slots = slot_total // 2
        amplitude = held[slot // half_slots, pl.ds(amplitude_rows + slot % half_slots * edge, edge), :]
        factor = weight * (1.0 - amplitude * lax.rsqrt(intensity + 1.0))
        factor = jnp.concatenate([factor] * modes, axis=1)
        residual = far * jnp.concatenate([factor, factor], axis=0)
        halves.append(table_times(spread_both, residual))
    backs = []
    for half in halves:
        parts = [
            [half[part * edge : (part + 1) * edge, m * edge : (m + 1) * edge] for part in range(2)]
            for m in range(modes)
        ]
        half = jnp.concatenate([jnp.concatenate(part, axis=1) for part in parts], axis=0)
        backs.append(times_table(half, turn_high[...], turn_low[...]))
    for slot in slots:
        crop_r, crop_i = crops[slot]
        row0, col0 = corner[slot]
        rows = pl.ds(row0, edge)
        object_r = jnp.zeros((edge, edge), jnp.float32)
        object_i = jnp.zeros((edge, edge), jnp.float32)
        for m in range(modes):
            back_r = backs[slot][m * edge : (m + 1) * edge, :edge]
            back_i = backs[slot][m * edge : (m + 1) * edge, edge:]
            object_r += probe(0, m) * back_r + probe(1, m) * back_i
            object_i += probe(0, m) * back_i - probe(1, m) * back_r
            term_r = crop_r * back_r + crop_i * back_i
            term_i = crop_r * back_i - crop_i * back_r
            if slot == 0:
                probe_sum[0, m] = term_r
                probe_sum[1, m] = term_i
            else:
                probe_sum[0, m] += term_r
                probe_sum[1, m] += term_i
        for part, term in enumerate((object_r, object_i)):
            term = pltpu.roll(term, col0, 1)
            grad_left[part, rows, :] += jnp.where(in_left[slot], term, 0.0)
            grad_right[part, rows, :] += jnp.where(in_left[slot], 0.0, term)
    own_grad[...] = grad_left[:, :edge]
    right_grad[...] = present(has_right, grad_right[:, :edge])
    lower_grads[0] = present(has_below, grad_left[:, edge:])
    lower_grads[1] = present(has_diag, grad_right[:, edge:])
    flat = probe_sum.reshape(2 * modes * edge, edge)
    pieces, depth = keep.shape[0], keep.shape[1]
    for target, half in ((keep, place[0]), (send, 1 - place[0])):
        for position in range(pieces):
            chunk = half * pieces + jnp.bitwise_xor(place[1], position)
            rows = pl.ds(pl.multiple_of(chunk * depth, depth), depth)
            target[position] = flat[rows, :] * scale


def join_kernel(place, own_grad, above, left, *refs):
    pieces, (out, object_grad, total, semaphores) = refs[:-4], refs[-4:]
    mine, forwarded = pieces[:-2], pieces[-2:]
    count, depth = len(mine), mine[0].shape[0]
    theirs = [part.at[index] for part in forwarded for index in range(part.shape[0])]
    copies = []
    for half, parts in ((place[0], mine), (1 - place[0], theirs)):
        for index, part in enumerate(parts):
            chunk = half * count + jnp.bitwise_xor(place[1], index)
            rows = pl.ds(pl.multiple_of(chunk * depth, depth), depth)
            copies.append(pltpu.make_async_copy(part, out.at[rows, :], semaphores.at[len(copies)]))
    total[...] = own_grad[...] + above[0] + left[...]
    copies.insert(0, pltpu.make_async_copy(total, object_grad, semaphores.at[2 * count]))
    for copy in copies:
        copy.start()
    for copy in copies:
        copy.wait()


def on_device(object_tiles, probe, amplitudes, offsets, counts):
    modes, edge = probe.shape[1], probe.shape[2]
    slot_total = amplitudes.shape[1]
    n_region, n_pos = lax.axis_size("region"), lax.axis_size("pos")
    total = n_region * n_pos
    axes = ("region", "pos")
    f32 = jnp.float32

    row_index, column_index = lax.axis_index("region"), lax.axis_index("pos")

    def shifted(block, down, across):
        route = [
            (i * n_pos + j, (i + down) % n_region * n_pos + (j + across) % n_pos)
            for i in range(n_region)
            for j in range(n_pos)
        ]
        return lax.ppermute(block, axes, route)

    pieces = n_pos // 2

    def partner(block, mask):
        return lax.ppermute(block, axes, [(i, i ^ mask) for i in range(total)])

    place = jnp.stack(
        [
            column_index & 1,
            column_index >> 1,
            (row_index < n_region - 1).astype(jnp.int32),
            (column_index < n_pos - 1).astype(jnp.int32),
            row_index & 1,
        ]
    )

    def swapped(first, across):
        route = []
        for i in range(n_region):
            a = i + 1 if (i - first) % 2 == 0 else i - 1
            for j in range(n_pos):
                if 0 <= a < n_region:
                    target = a * n_pos + (j + across) % n_pos
                else:
                    target = i * n_pos + ((j + across) % n_pos if across else j ^ 1)
                route.append((i * n_pos + j, target))
        return lax.ppermute(object_tiles, axes, route)

    right = shifted(object_tiles, 0, -1)
    halo = (swapped(0, 0), swapped(1, 0), right, swapped(0, -1), swapped(1, -1))

    lines = 2 * modes * edge
    smem = pl.BlockSpec(memory_space=pltpu.SMEM)
    vmem = pl.BlockSpec(memory_space=pltpu.VMEM)
    held = jnp.concatenate(
        [
            amplitudes.reshape(2, -1, edge),
            jnp.asarray(dft_tables(edge)),
        ],
        axis=1,
    )
    quadrant = jax.ShapeDtypeStruct((2, edge, edge), f32)
    part = jax.ShapeDtypeStruct((pieces, lines // n_pos, edge), f32)
    scale = 1.0 / math.sqrt(total * slot_total)
    own_grad, right_grad, lower_grads, keep, send = pl.pallas_call(
        functools.partial(slots_kernel, scale, modes, slot_total, edge),
        out_shape=(quadrant, quadrant, jax.ShapeDtypeStruct((2, 2, edge, edge), f32), part, part),
        in_specs=[pl.BlockSpec(memory_space=pl.ANY)] * 2 + [smem] + [vmem] * 8,
        out_specs=(vmem,) * 5,
        scratch_shapes=[pltpu.VMEM((4, 2 * edge, 2 * edge), jnp.bfloat16)]
        + [pltpu.VMEM((2, 2 * edge, edge), f32)] * 4
        + [
            pltpu.VMEM((2, modes, edge, edge), f32),
            pltpu.SMEM(offsets.shape, jnp.int32),
            pltpu.SMEM(counts.shape, jnp.int32),
            pltpu.SemaphoreType.DMA((2,)),
        ],
        compiler_params=pltpu.CompilerParams(vmem_limit_bytes=16 * 1024 * 1024),
    )(offsets, counts, place, probe, held, object_tiles, *halo)

    half = keep + partner(send, 1)
    above = shifted(lower_grads, 1, 0)
    got = [partner(half[k], 2 * k) for k in range(1, pieces)]
    got[0], above = lax.optimization_barrier((got[0], above))
    chunk = functools.reduce(jnp.add, got, half[0])
    terms = [chunk] + [partner(chunk, n_pos * k) for k in range(1, n_region)]
    left = shifted(right_grad + above[1], 0, 1)
    while len(terms) > 1:
        terms = [terms[k] + terms[k + 1] for k in range(0, len(terms), 2)]
    chunk, left = lax.optimization_barrier((terms[0], left))
    gathered = [chunk] + [partner(chunk, 2 * k) for k in range(1, pieces)]
    middle = pieces // 2
    forwarded = [
        partner(jnp.stack(part), 1) for part in (gathered[:middle], gathered[middle:])
    ]
    probe_grad, object_grad = pl.pallas_call(
        join_kernel,
        out_shape=(jax.ShapeDtypeStruct((lines, edge), f32), quadrant),
        in_specs=[smem] + [vmem] * (5 + pieces),
        out_specs=(pl.BlockSpec(memory_space=pl.ANY),) * 2,
        scratch_shapes=[pltpu.VMEM((2, edge, edge), f32), pltpu.SemaphoreType.DMA((n_pos + 1,))],
        compiler_params=pltpu.CompilerParams(vmem_limit_bytes=4 * 1024 * 1024),
    )(place, own_grad, above, left, *gathered, *forwarded)
    return (object_grad, probe_grad.reshape(probe.shape))


def solution(mesh):
    return jax.shard_map(
        on_device,
        mesh=mesh,
        in_specs=(
            P(None, "region", "pos"),
            P(),
            P("region", "pos", None, None),
            P("region", None, "pos"),
            P("region", "pos"),
        ),
        out_specs=(P(None, "region", "pos"), P()),
        check_vma=False,
    )
```

```python
import functools
import math

import jax
import jax.numpy as jnp
import numpy as np
from jax import lax
from jax.experimental import pallas as pl
from jax.experimental.pallas import tpu as pltpu
from jax.sharding import PartitionSpec as P


def dft_tables(order):
    index = np.arange(order)
    angle = (index[:, None] * index[None, :] % order) * (2.0 * math.pi / order)
    tables = np.stack([np.cos(angle), np.sin(angle)]) / math.sqrt(order)
    return tables.astype(np.float32)


def split(value):
    high = value.astype(jnp.bfloat16)
    low = (value - high.astype(jnp.float32)).astype(jnp.bfloat16)
    return high, low


def dot(a, b):
    return jnp.dot(a, b, preferred_element_type=jnp.float32)


def times_table(value, table_high, table_low):
    high, low = split(value)
    rows = value.shape[0]
    both = dot(jnp.concatenate([high, low], axis=0), table_high)
    return both[:rows] + (both[rows:] + dot(high, table_low))


def table_times(tables, value):
    high, low = split(value)
    rows = tables.shape[0] // 2
    both = dot(tables, high)
    return both[:rows] + (both[rows:] + dot(tables[:rows], low))


def slots_kernel(
    scale, modes, slot_total, edge, offsets, counts, place, probes, held, own, below, right, other_diag, diag, other_below,
    own_grad, right_grad, lower_grads, keep, send,
    tables, field_left, field_right, grad_left, grad_right, probe_sum, corners, live, semaphores,
):
    scalars = (
        pltpu.make_async_copy(offsets, corners, semaphores.at[0]),
        pltpu.make_async_copy(counts, live, semaphores.at[1]),
    )
    for copy in scalars:
        copy.start()

    def probe(part, mode):
        return probes[part, mode]

    amplitude_rows = 0
    table_rows = amplitude_rows + slot_total * edge // 2
    cos_high, cos_low = split(held[0, pl.ds(table_rows, edge), :])
    sin_high, sin_low = split(held[1, pl.ds(table_rows, edge), :])
    spread_high, spread_low, turn_high, turn_low = (tables.at[k] for k in range(4))
    for spread, turn, cos_part, sin_part in (
        (spread_high, turn_high, cos_high, sin_high),
        (spread_low, turn_low, cos_low, sin_low),
    ):
        for target, upper, lower in ((spread, -sin_part, sin_part), (turn, sin_part, -sin_part)):
            target[:edge, :edge] = cos_part
            target[:edge, edge:] = upper
            target[edge:, :edge] = lower
            target[edge:, edge:] = cos_part
    turn_both = jnp.concatenate([turn_high[...], turn_low[...]], axis=0)
    spread_both = jnp.concatenate([spread_high[...], spread_low[...]], axis=0)
    has_below, has_right, odd_row = place[2] > 0, place[3] > 0, place[4] > 0
    has_diag = jnp.logical_and(has_below, has_right)

    def present(flag, value):
        return jnp.where(flag, value, jnp.zeros_like(value))

    def arrived(flag, first, second):
        return present(flag, jnp.where(odd_row, second[...], first[...]).astype(jnp.float32))

    field_left[:, :edge] = own[...].astype(jnp.float32)
    field_left[:, edge:] = arrived(has_below, below, other_below)
    field_right[:, :edge] = present(has_right, right[...].astype(jnp.float32))
    field_right[:, edge:] = arrived(has_diag, diag, other_diag)
    grad_left[...] = jnp.zeros_like(grad_left)
    grad_right[...] = jnp.zeros_like(grad_right)
    lane = lax.broadcasted_iota(jnp.int32, (edge, edge), 1)
    for copy in scalars:
        copy.wait()
    slots = range(slot_total)
    corner = [(corners[0, 0, slot], corners[0, 1, slot]) for slot in slots]
    in_left = [lane >= col0 for _, col0 in corner]
    crops, halves = [], []
    for slot in slots:
        row0, col0 = corner[slot]
        rows, shift = pl.ds(row0, edge), lax.rem(edge - col0, edge)
        crop_r, crop_i = (
            pltpu.roll(
                jnp.where(in_left[slot], field_left[part, rows, :], field_right[part, rows, :]), shift, 1
            )
            for part in range(2)
        )
        exits = [
            jnp.concatenate(
                [
                    probe(0, m) * crop_r - probe(1, m) * crop_i,
                    probe(0, m) * crop_i + probe(1, m) * crop_r,
                ],
                axis=1,
            )
            for m in range(modes)
        ]
        crops.append((crop_r, crop_i))
        halves += exits
    halves = times_table(jnp.concatenate(halves, axis=0), spread_high[...], spread_low[...])
    images = range(slot_total * modes)
    turned = [
        jnp.concatenate(
            [halves[m * edge : (m + 1) * edge, part * edge : (part + 1) * edge] for m in images], axis=1
        )
        for part in range(2)
    ]
    fars = table_times(turn_both, jnp.concatenate(turned, axis=0))
    halves = []
    for slot in slots:
        far = fars[:, slot * modes * edge : (slot + 1) * modes * edge]
        squares = far * far
        squares = squares[:edge] + squares[edge:]
        intensity = functools.reduce(
            jnp.add, [squares[:, m * edge : (m + 1) * edge] for m in range(modes)]
        )
        weight = (slot < live[0, 0]).astype(jnp.float32)
        half_slots = slot_total // 2
        amplitude = held[slot // half_slots, pl.ds(amplitude_rows + slot % half_slots * edge, edge), :]
        factor = weight * (1.0 - amplitude * lax.rsqrt(intensity + 1.0))
        factor = jnp.concatenate([factor] * modes, axis=1)
        residual = far * jnp.concatenate([factor, factor], axis=0)
        halves.append(residual)
    halves = table_times(spread_both, jnp.concatenate(halves, axis=1))
    turned = [
        jnp.concatenate(
            [halves[part * edge : (part + 1) * edge, m * edge : (m + 1) * edge] for part in range(2)], axis=1
        )
        for m in images
    ]
    backs = times_table(jnp.concatenate(turned, axis=0), turn_high[...], turn_low[...])
    for slot in slots:
        crop_r, crop_i = crops[slot]
        row0, col0 = corner[slot]
        rows = pl.ds(row0, edge)
        object_r = jnp.zeros((edge, edge), jnp.float32)
        object_i = jnp.zeros((edge, edge), jnp.float32)
        for m in range(modes):
            rows_m = slice((slot * modes + m) * edge, (slot * modes + m + 1) * edge)
            back_r, back_i = backs[rows_m, :edge], backs[rows_m, edge:]
            object_r += probe(0, m) * back_r + probe(1, m) * back_i
            object_i += probe(0, m) * back_i - probe(1, m) * back_r
            term_r = crop_r * back_r + crop_i * back_i
            term_i = crop_r * back_i - crop_i * back_r
            if slot == 0:
                probe_sum[0, m] = term_r
                probe_sum[1, m] = term_i
            else:
                probe_sum[0, m] += term_r
                probe_sum[1, m] += term_i
        for part, term in enumerate((object_r, object_i)):
            term = pltpu.roll(term, col0, 1)
            grad_left[part, rows, :] += jnp.where(in_left[slot], term, 0.0)
            grad_right[part, rows, :] += jnp.where(in_left[slot], 0.0, term)
    own_grad[...] = grad_left[:, :edge]
    right_grad[...] = present(has_right, grad_right[:, :edge])
    lower_grads[0] = present(has_below, grad_left[:, edge:])
    lower_grads[1] = present(has_diag, grad_right[:, edge:])
    flat = probe_sum.reshape(2 * modes * edge, edge)
    pieces, depth = keep.shape[0], keep.shape[1]
    for target, half in ((keep, place[0]), (send, 1 - place[0])):
        for position in range(pieces):
            chunk = half * pieces + jnp.bitwise_xor(place[1], position)
            rows = pl.ds(pl.multiple_of(chunk * depth, depth), depth)
            target[position] = flat[rows, :] * scale


def join_kernel(place, own_grad, above, left, *refs):
    pieces, (out, object_grad, total, semaphores) = refs[:-4], refs[-4:]
    count, depth = len(pieces) // 2, pieces[0].shape[0]
    copies = []
    for index, piece in enumerate(pieces):
        half = place[0] if index < count else 1 - place[0]
        chunk = half * count + jnp.bitwise_xor(place[1], index % count)
        rows = pl.ds(pl.multiple_of(chunk * depth, depth), depth)
        copies.append(pltpu.make_async_copy(piece, out.at[rows, :], semaphores.at[index]))
    total[...] = own_grad[...] + above[0] + left[...]
    copies.insert(0, pltpu.make_async_copy(total, object_grad, semaphores.at[len(pieces)]))
    for copy in copies:
        copy.start()
    for copy in copies:
        copy.wait()


def on_device(object_tiles, probe, amplitudes, offsets, counts):
    modes, edge = probe.shape[1], probe.shape[2]
    slot_total = amplitudes.shape[1]
    n_region, n_pos = lax.axis_size("region"), lax.axis_size("pos")
    total = n_region * n_pos
    axes = ("region", "pos")
    f32 = jnp.float32

    row_index, column_index = lax.axis_index("region"), lax.axis_index("pos")

    def shifted(block, down, across):
        route = [
            (i * n_pos + j, (i + down) % n_region * n_pos + (j + across) % n_pos)
            for i in range(n_region)
            for j in range(n_pos)
        ]
        return lax.ppermute(block, axes, route)

    pieces = n_pos // 2

    def partner(block, mask):
        return lax.ppermute(block, axes, [(i, i ^ mask) for i in range(total)])

    place = jnp.stack(
        [
            column_index & 1,
            column_index >> 1,
            (row_index < n_region - 1).astype(jnp.int32),
            (column_index < n_pos - 1).astype(jnp.int32),
            row_index & 1,
        ]
    )

    def swapped(first, across):
        route = []
        for i in range(n_region):
            a = i + 1 if (i - first) % 2 == 0 else i - 1
            for j in range(n_pos):
                if 0 <= a < n_region:
                    target = a * n_pos + (j + across) % n_pos
                else:
                    target = i * n_pos + ((j + across) % n_pos if across else j ^ 1)
                route.append((i * n_pos + j, target))
        return lax.ppermute(object_tiles, axes, route)

    right = shifted(object_tiles, 0, -1)
    halo = (swapped(0, 0), right, swapped(1, -1), swapped(0, -1), swapped(1, 0))

    lines = 2 * modes * edge
    smem = pl.BlockSpec(memory_space=pltpu.SMEM)
    vmem = pl.BlockSpec(memory_space=pltpu.VMEM)
    held = jnp.concatenate(
        [
            amplitudes.reshape(2, -1, edge),
            jnp.asarray(dft_tables(edge)),
        ],
        axis=1,
    )
    quadrant = jax.ShapeDtypeStruct((2, edge, edge), f32)
    part = jax.ShapeDtypeStruct((pieces, lines // n_pos, edge), f32)
    scale = 1.0 / math.sqrt(total * slot_total)
    own_grad, right_grad, lower_grads, keep, send = pl.pallas_call(
        functools.partial(slots_kernel, scale, modes, slot_total, edge),
        out_shape=(quadrant, quadrant, jax.ShapeDtypeStruct((2, 2, edge, edge), f32), part, part),
        in_specs=[pl.BlockSpec(memory_space=pl.ANY)] * 2 + [smem] + [vmem] * 8,
        out_specs=(vmem,) * 5,
        scratch_shapes=[pltpu.VMEM((4, 2 * edge, 2 * edge), jnp.bfloat16)]
        + [pltpu.VMEM((2, 2 * edge, edge), f32)] * 4
        + [
            pltpu.VMEM((2, modes, edge, edge), f32),
            pltpu.SMEM(offsets.shape, jnp.int32),
            pltpu.SMEM(counts.shape, jnp.int32),
            pltpu.SemaphoreType.DMA((2,)),
        ],
        compiler_params=pltpu.CompilerParams(vmem_limit_bytes=16 * 1024 * 1024),
    )(offsets, counts, place, probe, held, object_tiles, *halo)

    half = keep + partner(send, 1)
    above = shifted(lower_grads, 1, 0)
    got = [partner(half[k], 2 * k) for k in range(1, pieces)]
    got[0], above = lax.optimization_barrier((got[0], above))
    chunk = functools.reduce(jnp.add, got, half[0])
    terms = [chunk] + [partner(chunk, n_pos * k) for k in range(1, n_region)]
    left = shifted(right_grad + above[1], 0, 1)
    while len(terms) > 1:
        terms = [terms[k] + terms[k + 1] for k in range(0, len(terms), 2)]
    chunk = terms[0]
    gathered = [chunk] + [partner(chunk, 2 * k) for k in range(1, pieces)]
    gathered[1], left = lax.optimization_barrier((gathered[1], left))
    gathered += [partner(piece, 1) for piece in gathered]
    probe_grad, object_grad = pl.pallas_call(
        join_kernel,
        out_shape=(jax.ShapeDtypeStruct((lines, edge), f32), quadrant),
        in_specs=[smem] + [vmem] * (3 + n_pos),
        out_specs=(pl.BlockSpec(memory_space=pl.ANY),) * 2,
        scratch_shapes=[pltpu.VMEM((2, edge, edge), f32), pltpu.SemaphoreType.DMA((n_pos + 1,))],
        compiler_params=pltpu.CompilerParams(vmem_limit_bytes=4 * 1024 * 1024),
    )(place, own_grad, above, left, *gathered)
    return (object_grad, probe_grad.reshape(probe.shape))


def solution(mesh):
    return jax.shard_map(
        on_device,
        mesh=mesh,
        in_specs=(
            P(None, "region", "pos"),
            P(),
            P("region", "pos", None, None),
            P("region", None, "pos"),
            P("region", "pos"),
        ),
        out_specs=(P(None, "region", "pos"), P()),
        check_vma=False,
    )
```

```python
import functools
import math

import jax
import jax.numpy as jnp
import numpy as np
from jax import lax
from jax.experimental import pallas as pl
from jax.experimental.pallas import tpu as pltpu
from jax.sharding import PartitionSpec as P


def dft_tables(order):
    index = np.arange(order)
    angle = (index[:, None] * index[None, :] % order) * (2.0 * math.pi / order)
    tables = np.stack([np.cos(angle), np.sin(angle)]) / math.sqrt(order)
    return tables.astype(np.float32)


def split(value):
    high = value.astype(jnp.bfloat16)
    low = (value - high.astype(jnp.float32)).astype(jnp.bfloat16)
    return high, low


def dot(a, b):
    return jnp.dot(a, b, preferred_element_type=jnp.float32)


def times_table(value, table_high, table_low):
    rows = table_high.shape[0]
    sums = []
    for start in range(0, value.shape[0], rows):
        high, low = split(value[start : start + rows])
        both = dot(jnp.concatenate([high, low], axis=0), table_high)
        sums.append(both[:rows] + (both[rows:] + dot(high, table_low)))
    return jnp.concatenate(sums, axis=0)


def table_times(tables, value):
    rows = tables.shape[0] // 2
    sums = []
    for start in range(0, value.shape[1], rows):
        high, low = split(value[:, start : start + rows])
        both = dot(tables, high)
        sums.append(both[:rows] + (both[rows:] + dot(tables[:rows], low)))
    return jnp.concatenate(sums, axis=1)


def slots_kernel(
    scale, modes, slot_total, edge, offsets, counts, place, probes, held, own, below, right, other_diag, diag, other_below,
    own_grad, right_grad, lower_grads, keep, send,
    tables, field_left, field_right, grad_left, grad_right, probe_sum, corners, live, semaphores,
):
    scalars = (
        pltpu.make_async_copy(offsets, corners, semaphores.at[0]),
        pltpu.make_async_copy(counts, live, semaphores.at[1]),
    )
    for copy in scalars:
        copy.start()

    def probe(part, mode):
        return probes[part, mode]

    amplitude_rows = 0
    table_rows = amplitude_rows + slot_total * edge // 2
    cos_high, cos_low = split(held[0, pl.ds(table_rows, edge), :])
    sin_high, sin_low = split(held[1, pl.ds(table_rows, edge), :])
    spread_high, spread_low, turn_high, turn_low = (tables.at[k] for k in range(4))
    for spread, turn, cos_part, sin_part in (
        (spread_high, turn_high, cos_high, sin_high),
        (spread_low, turn_low, cos_low, sin_low),
    ):
        for target, upper, lower in ((spread, -sin_part, sin_part), (turn, sin_part, -sin_part)):
            target[:edge, :edge] = cos_part
            target[:edge, edge:] = upper
            target[edge:, :edge] = lower
            target[edge:, edge:] = cos_part
    turn_both = jnp.concatenate([turn_high[...], turn_low[...]], axis=0)
    spread_both = jnp.concatenate([spread_high[...], spread_low[...]], axis=0)
    has_below, has_right, odd_row = place[2] > 0, place[3] > 0, place[4] > 0
    has_diag = jnp.logical_and(has_below, has_right)

    def present(flag, value):
        return jnp.where(flag, value, jnp.zeros_like(value))

    def arrived(flag, first, second):
        return present(flag, jnp.where(odd_row, second[...], first[...]).astype(jnp.float32))

    field_left[:, :edge] = own[...].astype(jnp.float32)
    field_left[:, edge:] = arrived(has_below, below, other_below)
    field_right[:, :edge] = present(has_right, right[...].astype(jnp.float32))
    field_right[:, edge:] = arrived(has_diag, diag, other_diag)
    grad_left[...] = jnp.zeros_like(grad_left)
    grad_right[...] = jnp.zeros_like(grad_right)
    lane = lax.broadcasted_iota(jnp.int32, (edge, edge), 1)
    for copy in scalars:
        copy.wait()
    slots = range(slot_total)
    corner = [(corners[0, 0, slot], corners[0, 1, slot]) for slot in slots]
    in_left = [lane >= col0 for _, col0 in corner]
    crops, halves = [], []
    for slot in slots:
        row0, col0 = corner[slot]
        rows, shift = pl.ds(row0, edge), lax.rem(edge - col0, edge)
        crop_r, crop_i = (
            pltpu.roll(
                jnp.where(in_left[slot], field_left[part, rows, :], field_right[part, rows, :]), shift, 1
            )
            for part in range(2)
        )
        exits = [
            jnp.concatenate(
                [
                    probe(0, m) * crop_r - probe(1, m) * crop_i,
                    probe(0, m) * crop_i + probe(1, m) * crop_r,
                ],
                axis=1,
            )
            for m in range(modes)
        ]
        crops.append((crop_r, crop_i))
        halves.append(times_table(jnp.concatenate(exits, axis=0), spread_high[...], spread_low[...]))
    fars = []
    for half in halves:
        parts = [
            [half[m * edge : (m + 1) * edge, part * edge : (part + 1) * edge] for m in range(modes)]
            for part in range(2)
        ]
        half = jnp.concatenate([jnp.concatenate(part, axis=1) for part in parts], axis=0)
        fars.append(table_times(turn_both, half))
    halves = []
    for slot in slots:
        far = fars[slot]
        squares = far * far
        squares = squares[:edge] + squares[edge:]
        intensity = functools.reduce(
            jnp.add, [squares[:, m * edge : (m + 1) * edge] for m in range(modes)]
        )
        weight = (slot < live[0, 0]).astype(jnp.float32)
        half_slots = slot_total // 2
        amplitude = held[slot // half_slots, pl.ds(amplitude_rows + slot % half_slots * edge, edge), :]
        factor = weight * (1.0 - amplitude * lax.rsqrt(intensity + 1.0))
        factor = jnp.concatenate([factor] * modes, axis=1)
        residual = far * jnp.concatenate([factor, factor], axis=0)
        halves.append(table_times(spread_both, residual))
    backs = []
    for half in halves:
        parts = [
            [half[part * edge : (part + 1) * edge, m * edge : (m + 1) * edge] for part in range(2)]
            for m in range(modes)
        ]
        half = jnp.concatenate([jnp.concatenate(part, axis=1) for part in parts], axis=0)
        backs.append(times_table(half, turn_high[...], turn_low[...]))
    for slot in slots:
        crop_r, crop_i = crops[slot]
        row0, col0 = corner[slot]
        rows = pl.ds(row0, edge)
        object_r = jnp.zeros((edge, edge), jnp.float32)
        object_i = jnp.zeros((edge, edge), jnp.float32)
        for m in range(modes):
            back_r = backs[slot][m * edge : (m + 1) * edge, :edge]
            back_i = backs[slot][m * edge : (m + 1) * edge, edge:]
            object_r += probe(0, m) * back_r + probe(1, m) * back_i
            object_i += probe(0, m) * back_i - probe(1, m) * back_r
            term_r = crop_r * back_r + crop_i * back_i
            term_i = crop_r * back_i - crop_i * back_r
            if slot == 0:
                probe_sum[0, m] = term_r
                probe_sum[1, m] = term_i
            else:
                probe_sum[0, m] += term_r
                probe_sum[1, m] += term_i
        for part, term in enumerate((object_r, object_i)):
            term = pltpu.roll(term, col0, 1)
            grad_left[part, rows, :] += jnp.where(in_left[slot], term, 0.0)
            grad_right[part, rows, :] += jnp.where(in_left[slot], 0.0, term)
    own_grad[...] = grad_left[:, :edge]
    right_grad[...] = present(has_right, grad_right[:, :edge])
    lower_grads[0] = present(has_below, grad_left[:, edge:])
    lower_grads[1] = present(has_diag, grad_right[:, edge:])
    flat = probe_sum.reshape(2 * modes * edge, edge)
    pieces, depth = keep.shape[0], keep.shape[1]
    for target, half in ((keep, place[0]), (send, 1 - place[0])):
        for position in range(pieces):
            chunk = half * pieces + jnp.bitwise_xor(place[1], position)
            rows = pl.ds(pl.multiple_of(chunk * depth, depth), depth)
            target[position] = flat[rows, :] * scale


def join_kernel(place, own_grad, above, left, *refs):
    pieces, (out, object_grad, total, semaphores) = refs[:-4], refs[-4:]
    count, depth = len(pieces) // 2, pieces[0].shape[0]
    copies = []
    for index, piece in enumerate(pieces):
        half = place[0] if index < count else 1 - place[0]
        chunk = half * count + jnp.bitwise_xor(place[1], index % count)
        rows = pl.ds(pl.multiple_of(chunk * depth, depth), depth)
        copies.append(pltpu.make_async_copy(piece, out.at[rows, :], semaphores.at[index]))
    total[...] = own_grad[...] + above[0] + left[...]
    copies.insert(0, pltpu.make_async_copy(total, object_grad, semaphores.at[len(pieces)]))
    for copy in copies:
        copy.start()
    for copy in copies:
        copy.wait()


def on_device(object_tiles, probe, amplitudes, offsets, counts):
    modes, edge = probe.shape[1], probe.shape[2]
    slot_total = amplitudes.shape[1]
    n_region, n_pos = lax.axis_size("region"), lax.axis_size("pos")
    total = n_region * n_pos
    axes = ("region", "pos")
    f32 = jnp.float32

    row_index, column_index = lax.axis_index("region"), lax.axis_index("pos")

    def shifted(block, down, across):
        route = [
            (i * n_pos + j, (i + down) % n_region * n_pos + (j + across) % n_pos)
            for i in range(n_region)
            for j in range(n_pos)
        ]
        return lax.ppermute(block, axes, route)

    pieces = n_pos // 2

    def partner(block, mask):
        return lax.ppermute(block, axes, [(i, i ^ mask) for i in range(total)])

    place = jnp.stack(
        [
            column_index & 1,
            column_index >> 1,
            (row_index < n_region - 1).astype(jnp.int32),
            (column_index < n_pos - 1).astype(jnp.int32),
            row_index & 1,
        ]
    )

    def swapped(first, across):
        route = []
        for i in range(n_region):
            a = i + 1 if (i - first) % 2 == 0 else i - 1
            for j in range(n_pos):
                if 0 <= a < n_region:
                    target = a * n_pos + (j + across) % n_pos
                else:
                    target = i * n_pos + ((j + across) % n_pos if across else j ^ 1)
                route.append((i * n_pos + j, target))
        return lax.ppermute(object_tiles, axes, route)

    right = shifted(object_tiles, 0, -1)
    halo = (swapped(0, 0), right, swapped(1, -1), swapped(0, -1), swapped(1, 0))

    lines = 2 * modes * edge
    smem = pl.BlockSpec(memory_space=pltpu.SMEM)
    vmem = pl.BlockSpec(memory_space=pltpu.VMEM)
    held = jnp.concatenate(
        [
            amplitudes.reshape(2, -1, edge),
            jnp.asarray(dft_tables(edge)),
        ],
        axis=1,
    )
    quadrant = jax.ShapeDtypeStruct((2, edge, edge), f32)
    part = jax.ShapeDtypeStruct((pieces, lines // n_pos, edge), f32)
    scale = 1.0 / math.sqrt(total * slot_total)
    own_grad, right_grad, lower_grads, keep, send = pl.pallas_call(
        functools.partial(slots_kernel, scale, modes, slot_total, edge),
        out_shape=(quadrant, quadrant, jax.ShapeDtypeStruct((2, 2, edge, edge), f32), part, part),
        in_specs=[pl.BlockSpec(memory_space=pl.ANY)] * 2 + [smem] + [vmem] * 8,
        out_specs=(vmem,) * 5,
        scratch_shapes=[pltpu.VMEM((4, 2 * edge, 2 * edge), jnp.bfloat16)]
        + [pltpu.VMEM((2, 2 * edge, edge), f32)] * 4
        + [
            pltpu.VMEM((2, modes, edge, edge), f32),
            pltpu.SMEM(offsets.shape, jnp.int32),
            pltpu.SMEM(counts.shape, jnp.int32),
            pltpu.SemaphoreType.DMA((2,)),
        ],
        compiler_params=pltpu.CompilerParams(vmem_limit_bytes=16 * 1024 * 1024),
    )(offsets, counts, place, probe, held, object_tiles, *halo)

    half = keep + partner(send, 1)
    above = shifted(lower_grads, 1, 0)
    got = [partner(half[k], 2 * k) for k in range(1, pieces)]
    got[0], above = lax.optimization_barrier((got[0], above))
    chunk = functools.reduce(jnp.add, got, half[0])
    terms = [chunk] + [partner(chunk, n_pos * k) for k in range(1, n_region)]
    left = shifted(right_grad + above[1], 0, 1)
    while len(terms) > 1:
        terms = [terms[k] + terms[k + 1] for k in range(0, len(terms), 2)]
    chunk = terms[0]
    gathered = [chunk] + [partner(chunk, 2 * k) for k in range(1, pieces)]
    gathered[1], left = lax.optimization_barrier((gathered[1], left))
    gathered += [partner(piece, 1) for piece in gathered]
    probe_grad, object_grad = pl.pallas_call(
        join_kernel,
        out_shape=(jax.ShapeDtypeStruct((lines, edge), f32), quadrant),
        in_specs=[smem] + [vmem] * (3 + n_pos),
        out_specs=(pl.BlockSpec(memory_space=pl.ANY),) * 2,
        scratch_shapes=[pltpu.VMEM((2, edge, edge), f32), pltpu.SemaphoreType.DMA((n_pos + 1,))],
        compiler_params=pltpu.CompilerParams(vmem_limit_bytes=4 * 1024 * 1024),
    )(place, own_grad, above, left, *gathered)
    return (object_grad, probe_grad.reshape(probe.shape))


def solution(mesh):
    return jax.shard_map(
        on_device,
        mesh=mesh,
        in_specs=(
            P(None, "region", "pos"),
            P(),
            P("region", "pos", None, None),
            P("region", None, "pos"),
            P("region", "pos"),
        ),
        out_specs=(P(None, "region", "pos"), P()),
        check_vma=False,
    )
```

```python
import functools
import math

import jax
import jax.numpy as jnp
import numpy as np
from jax import lax
from jax.experimental import pallas as pl
from jax.experimental.pallas import tpu as pltpu
from jax.sharding import PartitionSpec as P


def dft_tables(order):
    index = np.arange(order)
    angle = (index[:, None] * index[None, :] % order) * (2.0 * math.pi / order)
    tables = np.stack([np.cos(angle), np.sin(angle)]) / math.sqrt(order)
    return tables.astype(np.float32)


def split(value):
    high = value.astype(jnp.bfloat16)
    low = (value - high.astype(jnp.float32)).astype(jnp.bfloat16)
    return high, low


def dot(a, b):
    return jnp.dot(a, b, preferred_element_type=jnp.float32)


def times_table(value, table_high, table_low):
    rows = table_high.shape[0]
    sums = []
    for start in range(0, value.shape[0], rows):
        high, low = split(value[start : start + rows])
        both = dot(jnp.concatenate([high, low], axis=0), table_high)
        sums.append(both[:rows] + (both[rows:] + dot(high, table_low)))
    return jnp.concatenate(sums, axis=0)


def table_times(tables, value):
    rows = tables.shape[0] // 2
    sums = []
    for start in range(0, value.shape[1], rows):
        high, low = split(value[:, start : start + rows])
        both = dot(tables, high)
        sums.append(both[:rows] + (both[rows:] + dot(tables[:rows], low)))
    return jnp.concatenate(sums, axis=1)


def slots_kernel(
    scale, modes, slot_total, edge, offsets, counts, place, probes, held, own, below, right, other_diag, diag, other_below,
    own_grad, right_grad, below_grad, diag_grad, keep, send,
    tables, field_left, field_right, grad_left, grad_right, probe_sum, corners, live, semaphores,
):
    scalars = (
        pltpu.make_async_copy(offsets, corners, semaphores.at[0]),
        pltpu.make_async_copy(counts, live, semaphores.at[1]),
    )
    for copy in scalars:
        copy.start()

    def probe(part, mode):
        return probes[part, mode]

    amplitude_rows = 0
    table_rows = amplitude_rows + slot_total * edge // 2
    cos_high, cos_low = split(held[0, pl.ds(table_rows, edge), :])
    sin_high, sin_low = split(held[1, pl.ds(table_rows, edge), :])
    spread_high, spread_low, turn_high, turn_low = (tables.at[k] for k in range(4))
    for spread, turn, cos_part, sin_part in (
        (spread_high, turn_high, cos_high, sin_high),
        (spread_low, turn_low, cos_low, sin_low),
    ):
        for target, upper, lower in ((spread, -sin_part, sin_part), (turn, sin_part, -sin_part)):
            target[:edge, :edge] = cos_part
            target[:edge, edge:] = upper
            target[edge:, :edge] = lower
            target[edge:, edge:] = cos_part
    turn_both = jnp.concatenate([turn_high[...], turn_low[...]], axis=0)
    spread_both = jnp.concatenate([spread_high[...], spread_low[...]], axis=0)
    has_below, has_right, odd_row = place[2] > 0, place[3] > 0, place[4] > 0
    has_diag = jnp.logical_and(has_below, has_right)

    def present(flag, value):
        return jnp.where(flag, value, jnp.zeros_like(value))

    def arrived(flag, first, second):
        return present(flag, jnp.where(odd_row, second[...], first[...]).astype(jnp.float32))

    field_left[:, :edge] = own[...].astype(jnp.float32)
    field_left[:, edge:] = arrived(has_below, below, other_below)
    field_right[:, :edge] = present(has_right, right[...].astype(jnp.float32))
    field_right[:, edge:] = arrived(has_diag, diag, other_diag)
    grad_left[...] = jnp.zeros_like(grad_left)
    grad_right[...] = jnp.zeros_like(grad_right)
    lane = lax.broadcasted_iota(jnp.int32, (edge, edge), 1)
    for copy in scalars:
        copy.wait()
    slots = range(slot_total)
    corner = [(corners[0, 0, slot], corners[0, 1, slot]) for slot in slots]
    in_left = [lane >= col0 for _, col0 in corner]
    crops, halves = [], []
    for slot in slots:
        row0, col0 = corner[slot]
        rows, shift = pl.ds(row0, edge), lax.rem(edge - col0, edge)
        crop_r, crop_i = (
            pltpu.roll(
                jnp.where(in_left[slot], field_left[part, rows, :], field_right[part, rows, :]), shift, 1
            )
            for part in range(2)
        )
        exits = [
            jnp.concatenate(
                [
                    probe(0, m) * crop_r - probe(1, m) * crop_i,
                    probe(0, m) * crop_i + probe(1, m) * crop_r,
                ],
                axis=1,
            )
            for m in range(modes)
        ]
        crops.append((crop_r, crop_i))
        halves.append(times_table(jnp.concatenate(exits, axis=0), spread_high[...], spread_low[...]))
    fars = []
    for half in halves:
        parts = [
            [half[m * edge : (m + 1) * edge, part * edge : (part + 1) * edge] for m in range(modes)]
            for part in range(2)
        ]
        half = jnp.concatenate([jnp.concatenate(part, axis=1) for part in parts], axis=0)
        fars.append(table_times(turn_both, half))
    halves = []
    for slot in slots:
        far = fars[slot]
        squares = far * far
        squares = squares[:edge] + squares[edge:]
        intensity = functools.reduce(
            jnp.add, [squares[:, m * edge : (m + 1) * edge] for m in range(modes)]
        )
        weight = (slot < live[0, 0]).astype(jnp.float32)
        half_slots = slot_total // 2
        amplitude = held[slot // half_slots, pl.ds(amplitude_rows + slot % half_slots * edge, edge), :]
        factor = weight * (1.0 - amplitude * lax.rsqrt(intensity + 1.0))
        factor = jnp.concatenate([factor] * modes, axis=1)
        residual = far * jnp.concatenate([factor, factor], axis=0)
        halves.append(table_times(spread_both, residual))
    backs = []
    for half in halves:
        parts = [
            [half[part * edge : (part + 1) * edge, m * edge : (m + 1) * edge] for part in range(2)]
            for m in range(modes)
        ]
        half = jnp.concatenate([jnp.concatenate(part, axis=1) for part in parts], axis=0)
        backs.append(times_table(half, turn_high[...], turn_low[...]))
    for slot in slots:
        crop_r, crop_i = crops[slot]
        row0, col0 = corner[slot]
        rows = pl.ds(row0, edge)
        object_r = jnp.zeros((edge, edge), jnp.float32)
        object_i = jnp.zeros((edge, edge), jnp.float32)
        for m in range(modes):
            back_r = backs[slot][m * edge : (m + 1) * edge, :edge]
            back_i = backs[slot][m * edge : (m + 1) * edge, edge:]
            object_r += probe(0, m) * back_r + probe(1, m) * back_i
            object_i += probe(0, m) * back_i - probe(1, m) * back_r
            term_r = crop_r * back_r + crop_i * back_i
            term_i = crop_r * back_i - crop_i * back_r
            if slot == 0:
                probe_sum[0, m] = term_r
                probe_sum[1, m] = term_i
            else:
                probe_sum[0, m] += term_r
                probe_sum[1, m] += term_i
        for part, term in enumerate((object_r, object_i)):
            term = pltpu.roll(term, col0, 1)
            grad_left[part, rows, :] += jnp.where(in_left[slot], term, 0.0)
            grad_right[part, rows, :] += jnp.where(in_left[slot], 0.0, term)
    own_grad[...] = grad_left[:, :edge]
    right_grad[...] = present(has_right, grad_right[:, :edge])
    below_grad[...] = present(has_below, grad_left[:, edge:])
    diag_grad[...] = present(has_diag, grad_right[:, edge:])
    flat = probe_sum.reshape(2 * modes * edge, edge)
    pieces, depth = keep.shape[0], keep.shape[1]
    for target, half in ((keep, place[0]), (send, 1 - place[0])):
        for position in range(pieces):
            chunk = half * pieces + jnp.bitwise_xor(place[1], position)
            rows = pl.ds(pl.multiple_of(chunk * depth, depth), depth)
            target[position] = flat[rows, :] * scale


def join_kernel(place, own_grad, above, left, *refs):
    pieces, (out, object_grad, total, semaphores) = refs[:-4], refs[-4:]
    count, depth = len(pieces) // 2, pieces[0].shape[0]
    copies = []
    for index, piece in enumerate(pieces):
        half = place[0] if index < count else 1 - place[0]
        chunk = half * count + jnp.bitwise_xor(place[1], index % count)
        rows = pl.ds(pl.multiple_of(chunk * depth, depth), depth)
        copies.append(pltpu.make_async_copy(piece, out.at[rows, :], semaphores.at[index]))
    total[...] = own_grad[...] + above[...] + left[...]
    copies.insert(0, pltpu.make_async_copy(total, object_grad, semaphores.at[len(pieces)]))
    for copy in copies:
        copy.start()
    for copy in copies:
        copy.wait()


def on_device(object_tiles, probe, amplitudes, offsets, counts):
    modes, edge = probe.shape[1], probe.shape[2]
    slot_total = amplitudes.shape[1]
    n_region, n_pos = lax.axis_size("region"), lax.axis_size("pos")
    total = n_region * n_pos
    axes = ("region", "pos")
    f32 = jnp.float32

    row_index, column_index = lax.axis_index("region"), lax.axis_index("pos")

    def shifted(block, down, across):
        route = [
            (i * n_pos + j, (i + down) % n_region * n_pos + (j + across) % n_pos)
            for i in range(n_region)
            for j in range(n_pos)
        ]
        return lax.ppermute(block, axes, route)

    pieces = n_pos // 2

    def partner(block, mask):
        return lax.ppermute(block, axes, [(i, i ^ mask) for i in range(total)])

    place = jnp.stack(
        [
            column_index & 1,
            column_index >> 1,
            (row_index < n_region - 1).astype(jnp.int32),
            (column_index < n_pos - 1).astype(jnp.int32),
            row_index & 1,
        ]
    )

    def swapped(first, across):
        route = []
        for i in range(n_region):
            a = i + 1 if (i - first) % 2 == 0 else i - 1
            for j in range(n_pos):
                if 0 <= a < n_region:
                    target = a * n_pos + (j + across) % n_pos
                else:
                    target = i * n_pos + ((j + across) % n_pos if across else j ^ 1)
                route.append((i * n_pos + j, target))
        return lax.ppermute(object_tiles, axes, route)

    right = shifted(object_tiles, 0, -1)
    halo = (swapped(0, 0), right, swapped(1, -1), swapped(0, -1), swapped(1, 0))

    lines = 2 * modes * edge
    smem = pl.BlockSpec(memory_space=pltpu.SMEM)
    vmem = pl.BlockSpec(memory_space=pltpu.VMEM)
    held = jnp.concatenate(
        [
            amplitudes.reshape(2, -1, edge),
            jnp.asarray(dft_tables(edge)),
        ],
        axis=1,
    )
    quadrant = jax.ShapeDtypeStruct((2, edge, edge), f32)
    part = jax.ShapeDtypeStruct((pieces, lines // n_pos, edge), f32)
    scale = 1.0 / math.sqrt(total * slot_total)
    own_grad, right_grad, below_grad, diag_grad, keep, send = pl.pallas_call(
        functools.partial(slots_kernel, scale, modes, slot_total, edge),
        out_shape=(quadrant,) * 4 + (part, part),
        in_specs=[pl.BlockSpec(memory_space=pl.ANY)] * 2 + [smem] + [vmem] * 8,
        out_specs=(vmem,) * 6,
        scratch_shapes=[pltpu.VMEM((4, 2 * edge, 2 * edge), jnp.bfloat16)]
        + [pltpu.VMEM((2, 2 * edge, edge), f32)] * 4
        + [
            pltpu.VMEM((2, modes, edge, edge), f32),
            pltpu.SMEM(offsets.shape, jnp.int32),
            pltpu.SMEM(counts.shape, jnp.int32),
            pltpu.SemaphoreType.DMA((2,)),
        ],
        compiler_params=pltpu.CompilerParams(vmem_limit_bytes=16 * 1024 * 1024),
    )(offsets, counts, place, probe, held, object_tiles, *halo)

    half = keep + partner(send, 1)
    right_part = shifted(diag_grad, 1, 0)
    above = shifted(below_grad, 1, 0)
    got = [partner(half[k], 2 * k) for k in range(1, pieces)]
    got[0], right_part = lax.optimization_barrier((got[0], right_part))
    left = shifted(right_grad + right_part, 0, 1)
    chunk = functools.reduce(jnp.add, got, half[0])
    terms = [chunk] + [partner(chunk, n_pos * k) for k in range(1, n_region)]
    terms[1], above = lax.optimization_barrier((terms[1], above))
    while len(terms) > 1:
        terms = [terms[k] + terms[k + 1] for k in range(0, len(terms), 2)]
    chunk = terms[0]
    gathered = [chunk] + [partner(chunk, 2 * k) for k in range(1, pieces)]
    gathered[1], left = lax.optimization_barrier((gathered[1], left))
    gathered += [partner(piece, 1) for piece in gathered]
    probe_grad, object_grad = pl.pallas_call(
        join_kernel,
        out_shape=(jax.ShapeDtypeStruct((lines, edge), f32), quadrant),
        in_specs=[smem] + [vmem] * (3 + n_pos),
        out_specs=(pl.BlockSpec(memory_space=pl.ANY),) * 2,
        scratch_shapes=[pltpu.VMEM((2, edge, edge), f32), pltpu.SemaphoreType.DMA((n_pos + 1,))],
        compiler_params=pltpu.CompilerParams(vmem_limit_bytes=4 * 1024 * 1024),
    )(place, own_grad, above, left, *gathered)
    return (object_grad, probe_grad.reshape(probe.shape))


def solution(mesh):
    return jax.shard_map(
        on_device,
        mesh=mesh,
        in_specs=(
            P(None, "region", "pos"),
            P(),
            P("region", "pos", None, None),
            P("region", None, "pos"),
            P("region", "pos"),
        ),
        out_specs=(P(None, "region", "pos"), P()),
        check_vma=False,
    )
```

```python
import functools
import math

import jax
import jax.numpy as jnp
import numpy as np
from jax import lax
from jax.experimental import pallas as pl
from jax.experimental.pallas import tpu as pltpu
from jax.sharding import PartitionSpec as P


def dft_tables(order):
    index = np.arange(order)
    angle = (index[:, None] * index[None, :] % order) * (2.0 * math.pi / order)
    tables = np.stack([np.cos(angle), np.sin(angle)]) / math.sqrt(order)
    return tables.astype(np.float32)


def split(value):
    high = value.astype(jnp.bfloat16)
    low = (value - high.astype(jnp.float32)).astype(jnp.bfloat16)
    return high, low


def dot(a, b):
    return jnp.dot(a, b, preferred_element_type=jnp.float32)


def times_table(value, table_high, table_low):
    rows = table_high.shape[0]
    sums = []
    for start in range(0, value.shape[0], rows):
        high, low = split(value[start : start + rows])
        both = dot(jnp.concatenate([high, low], axis=0), table_high)
        sums.append(both[:rows] + (both[rows:] + dot(high, table_low)))
    return jnp.concatenate(sums, axis=0)


def table_times(tables, value):
    rows = tables.shape[0] // 2
    sums = []
    for start in range(0, value.shape[1], rows):
        high, low = split(value[:, start : start + rows])
        both = dot(tables, high)
        sums.append(both[:rows] + (both[rows:] + dot(tables[:rows], low)))
    return jnp.concatenate(sums, axis=1)


def slots_kernel(
    scale, modes, slot_total, edge, offsets, counts, place, probes, held, own, below, right, other_diag, diag, other_below,
    own_grad, right_grad, lower_grads, keep, send,
    tables, field_left, field_right, grad_left, grad_right, probe_sum, corners, live, semaphores,
):
    scalars = (
        pltpu.make_async_copy(offsets, corners, semaphores.at[0]),
        pltpu.make_async_copy(counts, live, semaphores.at[1]),
    )
    for copy in scalars:
        copy.start()

    def probe(part, mode):
        return probes[part, mode]

    amplitude_rows = 0
    table_rows = amplitude_rows + slot_total * edge // 2
    cos_high, cos_low = split(held[0, pl.ds(table_rows, edge), :])
    sin_high, sin_low = split(held[1, pl.ds(table_rows, edge), :])
    spread_high, spread_low, turn_high, turn_low = (tables.at[k] for k in range(4))
    for spread, turn, cos_part, sin_part in (
        (spread_high, turn_high, cos_high, sin_high),
        (spread_low, turn_low, cos_low, sin_low),
    ):
        for target, upper, lower in ((spread, -sin_part, sin_part), (turn, sin_part, -sin_part)):
            target[:edge, :edge] = cos_part
            target[:edge, edge:] = upper
            target[edge:, :edge] = lower
            target[edge:, edge:] = cos_part
    turn_both = jnp.concatenate([turn_high[...], turn_low[...]], axis=0)
    spread_both = jnp.concatenate([spread_high[...], spread_low[...]], axis=0)
    has_below, has_right, odd_row = place[2] > 0, place[3] > 0, place[4] > 0
    has_diag = jnp.logical_and(has_below, has_right)

    def present(flag, value):
        return jnp.where(flag, value, jnp.zeros_like(value))

    def arrived(flag, first, second):
        return present(flag, jnp.where(odd_row, second[...], first[...]).astype(jnp.float32))

    field_left[:, :edge] = own[...].astype(jnp.float32)
    field_left[:, edge:] = arrived(has_below, below, other_below)
    field_right[:, :edge] = present(has_right, right[...].astype(jnp.float32))
    field_right[:, edge:] = arrived(has_diag, diag, other_diag)
    grad_left[...] = jnp.zeros_like(grad_left)
    grad_right[...] = jnp.zeros_like(grad_right)
    lane = lax.broadcasted_iota(jnp.int32, (edge, edge), 1)
    for copy in scalars:
        copy.wait()
    slots = range(slot_total)
    corner = [(corners[0, 0, slot], corners[0, 1, slot]) for slot in slots]
    in_left = [lane >= col0 for _, col0 in corner]
    crops, halves = [], []
    for slot in slots:
        row0, col0 = corner[slot]
        rows, shift = pl.ds(row0, edge), lax.rem(edge - col0, edge)
        crop_r, crop_i = (
            pltpu.roll(
                jnp.where(in_left[slot], field_left[part, rows, :], field_right[part, rows, :]), shift, 1
            )
            for part in range(2)
        )
        exits = [
            jnp.concatenate(
                [
                    probe(0, m) * crop_r - probe(1, m) * crop_i,
                    probe(0, m) * crop_i + probe(1, m) * crop_r,
                ],
                axis=1,
            )
            for m in range(modes)
        ]
        crops.append((crop_r, crop_i))
        halves.append(times_table(jnp.concatenate(exits, axis=0), spread_high[...], spread_low[...]))
    fars = []
    for half in halves:
        parts = [
            [half[m * edge : (m + 1) * edge, part * edge : (part + 1) * edge] for m in range(modes)]
            for part in range(2)
        ]
        half = jnp.concatenate([jnp.concatenate(part, axis=1) for part in parts], axis=0)
        fars.append(table_times(turn_both, half))
    halves = []
    for slot in slots:
        far = fars[slot]
        squares = far * far
        squares = squares[:edge] + squares[edge:]
        intensity = functools.reduce(
            jnp.add, [squares[:, m * edge : (m + 1) * edge] for m in range(modes)]
        )
        weight = (slot < live[0, 0]).astype(jnp.float32)
        half_slots = slot_total // 2
        amplitude = held[slot // half_slots, pl.ds(amplitude_rows + slot % half_slots * edge, edge), :]
        factor = weight * (1.0 - amplitude * lax.rsqrt(intensity + 1.0))
        factor = jnp.concatenate([factor] * modes, axis=1)
        residual = far * jnp.concatenate([factor, factor], axis=0)
        halves.append(table_times(spread_both, residual))
    backs = []
    for half in halves:
        parts = [
            [half[part * edge : (part + 1) * edge, m * edge : (m + 1) * edge] for part in range(2)]
            for m in range(modes)
        ]
        half = jnp.concatenate([jnp.concatenate(part, axis=1) for part in parts], axis=0)
        backs.append(times_table(half, turn_high[...], turn_low[...]))
    for slot in slots:
        crop_r, crop_i = crops[slot]
        row0, col0 = corner[slot]
        rows = pl.ds(row0, edge)
        object_r = jnp.zeros((edge, edge), jnp.float32)
        object_i = jnp.zeros((edge, edge), jnp.float32)
        for m in range(modes):
            back_r = backs[slot][m * edge : (m + 1) * edge, :edge]
            back_i = backs[slot][m * edge : (m + 1) * edge, edge:]
            object_r += probe(0, m) * back_r + probe(1, m) * back_i
            object_i += probe(0, m) * back_i - probe(1, m) * back_r
            term_r = crop_r * back_r + crop_i * back_i
            term_i = crop_r * back_i - crop_i * back_r
            if slot == 0:
                probe_sum[0, m] = term_r
                probe_sum[1, m] = term_i
            else:
                probe_sum[0, m] += term_r
                probe_sum[1, m] += term_i
        for part, term in enumerate((object_r, object_i)):
            term = pltpu.roll(term, col0, 1)
            grad_left[part, rows, :] += jnp.where(in_left[slot], term, 0.0)
            grad_right[part, rows, :] += jnp.where(in_left[slot], 0.0, term)
    own_grad[...] = grad_left[:, :edge]
    right_grad[...] = present(has_right, grad_right[:, :edge])
    lower_grads[0] = present(has_below, grad_left[:, edge:])
    lower_grads[1] = present(has_diag, grad_right[:, edge:])
    flat = probe_sum.reshape(2 * modes * edge, edge)
    depth = keep.shape[0]
    for target, half in ((keep, place[0]), (send, 1 - place[0])):
        target[...] = flat[pl.ds(pl.multiple_of(half * depth, depth), depth), :] * scale


def join_kernel(place, own_grad, above, left, *refs):
    (mine, theirs), (out, object_grad, total, semaphores) = refs[:-4], refs[-4:]
    depth = mine.shape[0]
    copies = []
    for half, part in ((place[0], mine), (1 - place[0], theirs)):
        rows = pl.ds(pl.multiple_of(half * depth, depth), depth)
        copies.append(pltpu.make_async_copy(part, out.at[rows, :], semaphores.at[len(copies)]))
    total[...] = own_grad[...] + above[0] + left[...]
    copies.insert(0, pltpu.make_async_copy(total, object_grad, semaphores.at[len(copies)]))
    for copy in copies:
        copy.start()
    for copy in copies:
        copy.wait()


def on_device(object_tiles, probe, amplitudes, offsets, counts):
    modes, edge = probe.shape[1], probe.shape[2]
    slot_total = amplitudes.shape[1]
    n_region, n_pos = lax.axis_size("region"), lax.axis_size("pos")
    total = n_region * n_pos
    axes = ("region", "pos")
    f32 = jnp.float32

    row_index, column_index = lax.axis_index("region"), lax.axis_index("pos")

    def shifted(block, down, across):
        route = [
            (i * n_pos + j, (i + down) % n_region * n_pos + (j + across) % n_pos)
            for i in range(n_region)
            for j in range(n_pos)
        ]
        return lax.ppermute(block, axes, route)

    pieces = n_pos // 2

    def partner(block, mask):
        return lax.ppermute(block, axes, [(i, i ^ mask) for i in range(total)])

    place = jnp.stack(
        [
            column_index & 1,
            column_index >> 1,
            (row_index < n_region - 1).astype(jnp.int32),
            (column_index < n_pos - 1).astype(jnp.int32),
            row_index & 1,
        ]
    )

    def swapped(first, across):
        route = []
        for i in range(n_region):
            a = i + 1 if (i - first) % 2 == 0 else i - 1
            for j in range(n_pos):
                if 0 <= a < n_region:
                    target = a * n_pos + (j + across) % n_pos
                else:
                    target = i * n_pos + ((j + across) % n_pos if across else j ^ 1)
                route.append((i * n_pos + j, target))
        return lax.ppermute(object_tiles, axes, route)

    right = shifted(object_tiles, 0, -1)
    halo = (swapped(0, 0), right, swapped(1, -1), swapped(0, -1), swapped(1, 0))

    lines = 2 * modes * edge
    smem = pl.BlockSpec(memory_space=pltpu.SMEM)
    vmem = pl.BlockSpec(memory_space=pltpu.VMEM)
    held = jnp.concatenate(
        [
            amplitudes.reshape(2, -1, edge),
            jnp.asarray(dft_tables(edge)),
        ],
        axis=1,
    )
    quadrant = jax.ShapeDtypeStruct((2, edge, edge), f32)
    part = jax.ShapeDtypeStruct((lines // 2, edge), f32)
    scale = 1.0 / math.sqrt(total * slot_total)
    own_grad, right_grad, lower_grads, keep, send = pl.pallas_call(
        functools.partial(slots_kernel, scale, modes, slot_total, edge),
        out_shape=(quadrant, quadrant, jax.ShapeDtypeStruct((2, 2, edge, edge), f32), part, part),
        in_specs=[pl.BlockSpec(memory_space=pl.ANY)] * 2 + [smem] + [vmem] * 8,
        out_specs=(vmem,) * 5,
        scratch_shapes=[pltpu.VMEM((4, 2 * edge, 2 * edge), jnp.bfloat16)]
        + [pltpu.VMEM((2, 2 * edge, edge), f32)] * 4
        + [
            pltpu.VMEM((2, modes, edge, edge), f32),
            pltpu.SMEM(offsets.shape, jnp.int32),
            pltpu.SMEM(counts.shape, jnp.int32),
            pltpu.SemaphoreType.DMA((2,)),
        ],
        compiler_params=pltpu.CompilerParams(vmem_limit_bytes=16 * 1024 * 1024),
    )(offsets, counts, place, probe, held, object_tiles, *halo)

    groups = [[i for i in range(total) if i % 2 == parity] for parity in range(2)]

    def swapped_all(block):
        return lax.all_to_all(block, axes, 0, 0, axis_index_groups=groups, tiled=True)

    half = keep + partner(send, 1)
    above = shifted(lower_grads, 1, 0)
    chunk = jnp.sum(swapped_all(half).reshape(total // 2, -1, edge), axis=0)
    chunk, above = lax.optimization_barrier((chunk, above))
    left = shifted(right_grad + above[1], 0, 1)
    spread = jnp.broadcast_to(chunk, (total // 2,) + chunk.shape)
    half = swapped_all(spread.reshape(half.shape))
    half, left = lax.optimization_barrier((half, left))
    gathered = [half, partner(half, 1)]
    probe_grad, object_grad = pl.pallas_call(
        join_kernel,
        out_shape=(jax.ShapeDtypeStruct((lines, edge), f32), quadrant),
        in_specs=[smem] + [vmem] * 5,
        out_specs=(pl.BlockSpec(memory_space=pl.ANY),) * 2,
        scratch_shapes=[pltpu.VMEM((2, edge, edge), f32), pltpu.SemaphoreType.DMA((3,))],
        compiler_params=pltpu.CompilerParams(vmem_limit_bytes=4 * 1024 * 1024),
    )(place, own_grad, above, left, *gathered)
    return (object_grad, probe_grad.reshape(probe.shape))


def solution(mesh):
    return jax.shard_map(
        on_device,
        mesh=mesh,
        in_specs=(
            P(None, "region", "pos"),
            P(),
            P("region", "pos", None, None),
            P("region", None, "pos"),
            P("region", "pos"),
        ),
        out_specs=(P(None, "region", "pos"), P()),
        check_vma=False,
    )
```

```python
import functools
import math

import jax
import jax.numpy as jnp
import numpy as np
from jax import lax
from jax.experimental import pallas as pl
from jax.experimental.pallas import tpu as pltpu
from jax.sharding import PartitionSpec as P


def dft_tables(order):
    index = np.arange(order)
    angle = (index[:, None] * index[None, :] % order) * (2.0 * math.pi / order)
    tables = np.stack([np.cos(angle), np.sin(angle)]) / math.sqrt(order)
    return tables.astype(np.float32)


def split(value):
    high = value.astype(jnp.bfloat16)
    low = (value - high.astype(jnp.float32)).astype(jnp.bfloat16)
    return high, low


def dot(a, b):
    return jnp.dot(a, b, preferred_element_type=jnp.float32)


def times_table(value, table_high, table_low):
    rows = table_high.shape[0]
    sums = []
    for start in range(0, value.shape[0], rows):
        high, low = split(value[start : start + rows])
        both = dot(jnp.concatenate([high, low], axis=0), table_high)
        sums.append(both[:rows] + (both[rows:] + dot(high, table_low)))
    return jnp.concatenate(sums, axis=0)


def table_times(tables, value):
    rows = tables.shape[0] // 2
    sums = []
    for start in range(0, value.shape[1], rows):
        high, low = split(value[:, start : start + rows])
        both = dot(tables, high)
        sums.append(both[:rows] + (both[rows:] + dot(tables[:rows], low)))
    return jnp.concatenate(sums, axis=1)


def slots_kernel(
    scale, modes, slot_total, edge, offsets, counts, place, probes, held, own, below, right, other_diag, diag, other_below,
    own_grad, right_grad, lower_grads, keep, send,
    tables, field_left, field_right, grad_left, grad_right, probe_sum, corners, live, semaphores,
):
    scalars = (
        pltpu.make_async_copy(offsets, corners, semaphores.at[0]),
        pltpu.make_async_copy(counts, live, semaphores.at[1]),
    )
    for copy in scalars:
        copy.start()

    def probe(part, mode):
        return probes[part, mode]

    amplitude_rows = 0
    table_rows = amplitude_rows + slot_total * edge // 2
    cos_high, cos_low = split(held[0, pl.ds(table_rows, edge), :])
    sin_high, sin_low = split(held[1, pl.ds(table_rows, edge), :])
    spread_high, spread_low, turn_high, turn_low = (tables.at[k] for k in range(4))
    for spread, turn, cos_part, sin_part in (
        (spread_high, turn_high, cos_high, sin_high),
        (spread_low, turn_low, cos_low, sin_low),
    ):
        for target, upper, lower in ((spread, -sin_part, sin_part), (turn, sin_part, -sin_part)):
            target[:edge, :edge] = cos_part
            target[:edge, edge:] = upper
            target[edge:, :edge] = lower
            target[edge:, edge:] = cos_part
    turn_both = jnp.concatenate([turn_high[...], turn_low[...]], axis=0)
    spread_both = jnp.concatenate([spread_high[...], spread_low[...]], axis=0)
    has_below, has_right, odd_row = place[2] > 0, place[3] > 0, place[4] > 0
    has_diag = jnp.logical_and(has_below, has_right)

    def present(flag, value):
        return jnp.where(flag, value, jnp.zeros_like(value))

    def arrived(flag, first, second):
        return present(flag, jnp.where(odd_row, second[...], first[...]).astype(jnp.float32))

    field_left[:, :edge] = own[...].astype(jnp.float32)
    field_left[:, edge:] = arrived(has_below, below, other_below)
    field_right[:, :edge] = present(has_right, right[...].astype(jnp.float32))
    field_right[:, edge:] = arrived(has_diag, diag, other_diag)
    grad_left[...] = jnp.zeros_like(grad_left)
    grad_right[...] = jnp.zeros_like(grad_right)
    lane = lax.broadcasted_iota(jnp.int32, (edge, edge), 1)
    for copy in scalars:
        copy.wait()
    per_slot = modes // 2
    blocks = slot_total * per_slot
    crops, halves, fars, factors, backs, objects = {}, {}, {}, {}, {}, {}

    def crop_of(slot):
        if slot not in crops:
            row0, col0 = corners[0, 0, slot], corners[0, 1, slot]
            rows, shift = pl.ds(row0, edge), lax.rem(edge - col0, edge)
            in_left = lane >= col0
            crops[slot] = [
                pltpu.roll(
                    jnp.where(in_left, field_left[part, rows, :], field_right[part, rows, :]), shift, 1
                )
                for part in range(2)
            ]
        return crops[slot]

    def quarters(block):
        parts = [[block[:edge, :edge], block[:edge, edge:]], [block[edge:, :edge], block[edge:, edge:]]]
        return jnp.concatenate(
            [jnp.concatenate([parts[0][k], parts[1][k]], axis=1) for k in range(2)], axis=0
        )

    def modes_of(block):
        return [block % per_slot * 2 + k for k in range(2)]

    def first(block):
        crop_r, crop_i = crop_of(block // per_slot)
        exits = [
            jnp.concatenate(
                [
                    probe(0, m) * crop_r - probe(1, m) * crop_i,
                    probe(0, m) * crop_i + probe(1, m) * crop_r,
                ],
                axis=1,
            )
            for m in modes_of(block)
        ]
        halves[block] = times_table(jnp.concatenate(exits, axis=0), spread_high[...], spread_low[...])

    def second(block):
        fars[block] = table_times(turn_both, quarters(halves.pop(block)))

    def factor_of(slot):
        squares = []
        for block in range(slot * per_slot, (slot + 1) * per_slot):
            square = fars[block] * fars[block]
            square = square[:edge] + square[edge:]
            squares += [square[:, :edge], square[:, edge:]]
        intensity = functools.reduce(jnp.add, squares)
        half_slots = slot_total // 2
        amplitude = held[slot // half_slots, pl.ds(amplitude_rows + slot % half_slots * edge, edge), :]
        weight = (slot < live[0, 0]).astype(jnp.float32)
        factor = weight * (1.0 - amplitude * lax.rsqrt(intensity + 1.0))
        factor = jnp.concatenate([factor, factor], axis=1)
        factors[slot] = jnp.concatenate([factor, factor], axis=0)

    def third(block):
        backs[block] = table_times(spread_both, fars.pop(block) * factors[block // per_slot])

    def fourth(block):
        slot = block // per_slot
        crop_r, crop_i = crop_of(slot)
        back = times_table(quarters(backs.pop(block)), turn_high[...], turn_low[...])
        object_r, object_i = objects.pop(slot, (0.0, 0.0))
        for k, m in enumerate(modes_of(block)):
            back_r = back[k * edge : (k + 1) * edge, :edge]
            back_i = back[k * edge : (k + 1) * edge, edge:]
            object_r += probe(0, m) * back_r + probe(1, m) * back_i
            object_i += probe(0, m) * back_i - probe(1, m) * back_r
            term_r = crop_r * back_r + crop_i * back_i
            term_i = crop_r * back_i - crop_i * back_r
            if slot == 0:
                probe_sum[0, m] = term_r
                probe_sum[1, m] = term_i
            else:
                probe_sum[0, m] += term_r
                probe_sum[1, m] += term_i
        objects[slot] = (object_r, object_i)

    def scatter(slot):
        rows, col0 = pl.ds(corners[0, 0, slot], edge), corners[0, 1, slot]
        in_left = lane >= col0
        for part, term in enumerate(objects.pop(slot)):
            term = pltpu.roll(term, col0, 1)
            grad_left[part, rows, :] += jnp.where(in_left, term, 0.0)
            grad_right[part, rows, :] += jnp.where(in_left, 0.0, term)

    behind = per_slot + 1
    for step in range(blocks + behind + 1):
        if step < blocks:
            first(step)
        if 0 <= step - 1 < blocks:
            second(step - 1)
            if step % per_slot == 0:
                factor_of(step // per_slot - 1)
        if 0 <= step - behind < blocks:
            third(step - behind)
        if 0 <= step - behind - 1 < blocks:
            fourth(step - behind - 1)
            if (step - behind) % per_slot == 0:
                scatter((step - behind) // per_slot - 1)
    own_grad[...] = grad_left[:, :edge]
    right_grad[...] = present(has_right, grad_right[:, :edge])
    lower_grads[0] = present(has_below, grad_left[:, edge:])
    lower_grads[1] = present(has_diag, grad_right[:, edge:])
    flat = probe_sum.reshape(2 * modes * edge, edge)
    pieces, depth = keep.shape[0], keep.shape[1]
    for target, half in ((keep, place[0]), (send, 1 - place[0])):
        for position in range(pieces):
            chunk = half * pieces + jnp.bitwise_xor(place[1], position)
            rows = pl.ds(pl.multiple_of(chunk * depth, depth), depth)
            target[position] = flat[rows, :] * scale


def join_kernel(place, own_grad, above, left, *refs):
    pieces, (out, object_grad, total, semaphores) = refs[:-4], refs[-4:]
    count, depth = len(pieces) // 2, pieces[0].shape[0]
    copies = []
    for index, piece in enumerate(pieces):
        half = place[0] if index < count else 1 - place[0]
        chunk = half * count + jnp.bitwise_xor(place[1], index % count)
        rows = pl.ds(pl.multiple_of(chunk * depth, depth), depth)
        copies.append(pltpu.make_async_copy(piece, out.at[rows, :], semaphores.at[index]))
    total[...] = own_grad[...] + above[0] + left[...]
    copies.insert(0, pltpu.make_async_copy(total, object_grad, semaphores.at[len(pieces)]))
    for copy in copies:
        copy.start()
    for copy in copies:
        copy.wait()


def on_device(object_tiles, probe, amplitudes, offsets, counts):
    modes, edge = probe.shape[1], probe.shape[2]
    slot_total = amplitudes.shape[1]
    n_region, n_pos = lax.axis_size("region"), lax.axis_size("pos")
    total = n_region * n_pos
    axes = ("region", "pos")
    f32 = jnp.float32

    row_index, column_index = lax.axis_index("region"), lax.axis_index("pos")

    def shifted(block, down, across):
        route = [
            (i * n_pos + j, (i + down) % n_region * n_pos + (j + across) % n_pos)
            for i in range(n_region)
            for j in range(n_pos)
        ]
        return lax.ppermute(block, axes, route)

    pieces = n_pos // 2

    def partner(block, mask):
        return lax.ppermute(block, axes, [(i, i ^ mask) for i in range(total)])

    place = jnp.stack(
        [
            column_index & 1,
            column_index >> 1,
            (row_index < n_region - 1).astype(jnp.int32),
            (column_index < n_pos - 1).astype(jnp.int32),
            row_index & 1,
        ]
    )

    def swapped(first, across):
        route = []
        for i in range(n_region):
            a = i + 1 if (i - first) % 2 == 0 else i - 1
            for j in range(n_pos):
                if 0 <= a < n_region:
                    target = a * n_pos + (j + across) % n_pos
                else:
                    target = i * n_pos + ((j + across) % n_pos if across else j ^ 1)
                route.append((i * n_pos + j, target))
        return lax.ppermute(object_tiles, axes, route)

    right = shifted(object_tiles, 0, -1)
    halo = (swapped(0, 0), right, swapped(1, -1), swapped(0, -1), swapped(1, 0))

    lines = 2 * modes * edge
    smem = pl.BlockSpec(memory_space=pltpu.SMEM)
    vmem = pl.BlockSpec(memory_space=pltpu.VMEM)
    held = jnp.concatenate(
        [
            amplitudes.reshape(2, -1, edge),
            jnp.asarray(dft_tables(edge)),
        ],
        axis=1,
    )
    quadrant = jax.ShapeDtypeStruct((2, edge, edge), f32)
    part = jax.ShapeDtypeStruct((pieces, lines // n_pos, edge), f32)
    scale = 1.0 / math.sqrt(total * slot_total)
    own_grad, right_grad, lower_grads, keep, send = pl.pallas_call(
        functools.partial(slots_kernel, scale, modes, slot_total, edge),
        out_shape=(quadrant, quadrant, jax.ShapeDtypeStruct((2, 2, edge, edge), f32), part, part),
        in_specs=[pl.BlockSpec(memory_space=pl.ANY)] * 2 + [smem] + [vmem] * 8,
        out_specs=(vmem,) * 5,
        scratch_shapes=[pltpu.VMEM((4, 2 * edge, 2 * edge), jnp.bfloat16)]
        + [pltpu.VMEM((2, 2 * edge, edge), f32)] * 4
        + [
            pltpu.VMEM((2, modes, edge, edge), f32),
            pltpu.SMEM(offsets.shape, jnp.int32),
            pltpu.SMEM(counts.shape, jnp.int32),
            pltpu.SemaphoreType.DMA((2,)),
        ],
        compiler_params=pltpu.CompilerParams(vmem_limit_bytes=16 * 1024 * 1024),
    )(offsets, counts, place, probe, held, object_tiles, *halo)

    half = keep + partner(send, 1)
    above = shifted(lower_grads, 1, 0)
    got = [partner(half[k], 2 * k) for k in range(1, pieces)]
    got[0], above = lax.optimization_barrier((got[0], above))
    chunk = functools.reduce(jnp.add, got, half[0])
    terms = [chunk] + [partner(chunk, n_pos * k) for k in range(1, n_region)]
    left = shifted(right_grad + above[1], 0, 1)
    while len(terms) > 1:
        terms = [terms[k] + terms[k + 1] for k in range(0, len(terms), 2)]
    chunk = terms[0]
    gathered = [chunk] + [partner(chunk, 2 * k) for k in range(1, pieces)]
    gathered[1], left = lax.optimization_barrier((gathered[1], left))
    gathered += [partner(piece, 1) for piece in gathered]
    probe_grad, object_grad = pl.pallas_call(
        join_kernel,
        out_shape=(jax.ShapeDtypeStruct((lines, edge), f32), quadrant),
        in_specs=[smem] + [vmem] * (3 + n_pos),
        out_specs=(pl.BlockSpec(memory_space=pl.ANY),) * 2,
        scratch_shapes=[pltpu.VMEM((2, edge, edge), f32), pltpu.SemaphoreType.DMA((n_pos + 1,))],
        compiler_params=pltpu.CompilerParams(vmem_limit_bytes=4 * 1024 * 1024),
    )(place, own_grad, above, left, *gathered)
    return (object_grad, probe_grad.reshape(probe.shape))


def solution(mesh):
    return jax.shard_map(
        on_device,
        mesh=mesh,
        in_specs=(
            P(None, "region", "pos"),
            P(),
            P("region", "pos", None, None),
            P("region", None, "pos"),
            P("region", "pos"),
        ),
        out_specs=(P(None, "region", "pos"), P()),
        check_vma=False,
    )
```

```python
import functools
import math

import jax
import jax.numpy as jnp
import numpy as np
from jax import lax
from jax.experimental import pallas as pl
from jax.experimental.pallas import tpu as pltpu
from jax.sharding import PartitionSpec as P


def dft_tables(order):
    index = np.arange(order)
    angle = (index[:, None] * index[None, :] % order) * (2.0 * math.pi / order)
    tables = np.stack([np.cos(angle), np.sin(angle)]) / math.sqrt(order)
    return tables.astype(np.float32)


def split(value):
    high = value.astype(jnp.bfloat16)
    low = (value - high.astype(jnp.float32)).astype(jnp.bfloat16)
    return high, low


def dot(a, b):
    return jnp.dot(a, b, preferred_element_type=jnp.float32)


def times_table(value, table_high, table_low):
    rows = table_high.shape[0]
    sums = []
    for start in range(0, value.shape[0], rows):
        high, low = split(value[start : start + rows])
        both = dot(jnp.concatenate([high, low], axis=0), table_high)
        sums.append(both[:rows] + (both[rows:] + dot(high, table_low)))
    return jnp.concatenate(sums, axis=0)


def table_times(tables, value):
    rows = tables.shape[0] // 2
    sums = []
    for start in range(0, value.shape[1], rows):
        high, low = split(value[:, start : start + rows])
        both = dot(tables, high)
        sums.append(both[:rows] + (both[rows:] + dot(tables[:rows], low)))
    return jnp.concatenate(sums, axis=1)


def slots_kernel(
    scale, modes, slot_total, edge, offsets, counts, place, probes, held, own, below, right, other_diag, diag, other_below,
    own_grad, right_grad, lower_grads, keep, send,
    tables, field_left, field_right, grad_left, grad_right, probe_sum, corners, live, semaphores,
):
    scalars = (
        pltpu.make_async_copy(offsets, corners, semaphores.at[0]),
        pltpu.make_async_copy(counts, live, semaphores.at[1]),
    )
    for copy in scalars:
        copy.start()

    def probe(part, mode):
        return probes[part, mode]

    amplitude_rows = 0
    table_rows = amplitude_rows + slot_total * edge // 2
    cos_high, cos_low = split(held[0, pl.ds(table_rows, edge), :])
    sin_high, sin_low = split(held[1, pl.ds(table_rows, edge), :])
    spread_high, spread_low, turn_high, turn_low = (tables.at[k] for k in range(4))
    for spread, turn, cos_part, sin_part in (
        (spread_high, turn_high, cos_high, sin_high),
        (spread_low, turn_low, cos_low, sin_low),
    ):
        for target, upper, lower in ((spread, -sin_part, sin_part), (turn, sin_part, -sin_part)):
            target[:edge, :edge] = cos_part
            target[:edge, edge:] = upper
            target[edge:, :edge] = lower
            target[edge:, edge:] = cos_part
    turn_both = jnp.concatenate([turn_high[...], turn_low[...]], axis=0)
    spread_both = jnp.concatenate([spread_high[...], spread_low[...]], axis=0)
    has_below, has_right, odd_row = place[2] > 0, place[3] > 0, place[4] > 0
    has_diag = jnp.logical_and(has_below, has_right)

    def present(flag, value):
        return jnp.where(flag, value, jnp.zeros_like(value))

    def arrived(flag, first, second):
        return present(flag, jnp.where(odd_row, second[...], first[...]).astype(jnp.float32))

    field_left[:, :edge] = own[...].astype(jnp.float32)
    field_left[:, edge:] = arrived(has_below, below, other_below)
    field_right[:, :edge] = present(has_right, right[...].astype(jnp.float32))
    field_right[:, edge:] = arrived(has_diag, diag, other_diag)
    grad_left[...] = jnp.zeros_like(grad_left)
    grad_right[...] = jnp.zeros_like(grad_right)
    lane = lax.broadcasted_iota(jnp.int32, (edge, edge), 1)
    for copy in scalars:
        copy.wait()
    slots = range(slot_total)
    corner = [(corners[0, 0, slot], corners[0, 1, slot]) for slot in slots]
    in_left = [lane >= col0 for _, col0 in corner]
    crops, halves = [], []
    for slot in slots:
        row0, col0 = corner[slot]
        rows, shift = pl.ds(row0, edge), lax.rem(edge - col0, edge)
        crop_r, crop_i = (
            pltpu.roll(
                jnp.where(in_left[slot], field_left[part, rows, :], field_right[part, rows, :]), shift, 1
            )
            for part in range(2)
        )
        exits = [
            jnp.concatenate(
                [
                    probe(0, m) * crop_r - probe(1, m) * crop_i,
                    probe(0, m) * crop_i + probe(1, m) * crop_r,
                ],
                axis=1,
            )
            for m in range(modes)
        ]
        crops.append((crop_r, crop_i))
        halves.append(times_table(jnp.concatenate(exits, axis=0), spread_high[...], spread_low[...]))
    fars = []
    for half in halves:
        parts = [
            [half[m * edge : (m + 1) * edge, part * edge : (part + 1) * edge] for m in range(modes)]
            for part in range(2)
        ]
        half = jnp.concatenate([jnp.concatenate(part, axis=1) for part in parts], axis=0)
        fars.append(table_times(turn_both, half))
    halves = []
    for slot in slots:
        far = fars[slot]
        squares = far * far
        squares = squares[:edge] + squares[edge:]
        intensity = functools.reduce(
            jnp.add, [squares[:, m * edge : (m + 1) * edge] for m in range(modes)]
        )
        weight = (slot < live[0, 0]).astype(jnp.float32)
        half_slots = slot_total // 2
        amplitude = held[slot // half_slots, pl.ds(amplitude_rows + slot % half_slots * edge, edge), :]
        factor = weight * (1.0 - amplitude * lax.rsqrt(intensity + 1.0))
        factor = jnp.concatenate([factor] * modes, axis=1)
        residual = far * jnp.concatenate([factor, factor], axis=0)
        halves.append(table_times(spread_both, residual))
    backs = []
    for half in halves:
        parts = [
            [half[part * edge : (part + 1) * edge, m * edge : (m + 1) * edge] for part in range(2)]
            for m in range(modes)
        ]
        half = jnp.concatenate([jnp.concatenate(part, axis=1) for part in parts], axis=0)
        backs.append(times_table(half, turn_high[...], turn_low[...]))
    for slot in slots:
        crop_r, crop_i = crops[slot]
        row0, col0 = corner[slot]
        rows = pl.ds(row0, edge)
        object_r = jnp.zeros((edge, edge), jnp.float32)
        object_i = jnp.zeros((edge, edge), jnp.float32)
        for m in range(modes):
            back_r = backs[slot][m * edge : (m + 1) * edge, :edge]
            back_i = backs[slot][m * edge : (m + 1) * edge, edge:]
            object_r += probe(0, m) * back_r + probe(1, m) * back_i
            object_i += probe(0, m) * back_i - probe(1, m) * back_r
            term_r = crop_r * back_r + crop_i * back_i
            term_i = crop_r * back_i - crop_i * back_r
            if slot == 0:
                probe_sum[0, m] = term_r
                probe_sum[1, m] = term_i
            else:
                probe_sum[0, m] += term_r
                probe_sum[1, m] += term_i
        for part, term in enumerate((object_r, object_i)):
            term = pltpu.roll(term, col0, 1)
            grad_left[part, rows, :] += jnp.where(in_left[slot], term, 0.0)
            grad_right[part, rows, :] += jnp.where(in_left[slot], 0.0, term)
    own_grad[...] = grad_left[:, :edge]
    right_grad[...] = present(has_right, grad_right[:, :edge])
    lower_grads[0] = present(has_below, grad_left[:, edge:])
    lower_grads[1] = present(has_diag, grad_right[:, edge:])
    flat = probe_sum.reshape(2 * modes * edge, edge)
    pieces, depth = keep.shape[0], keep.shape[1]
    for target, half in ((keep, place[0]), (send, 1 - place[0])):
        for position in range(pieces):
            chunk = half * pieces + jnp.bitwise_xor(place[1], position)
            rows = pl.ds(pl.multiple_of(chunk * depth, depth), depth)
            target[position] = flat[rows, :] * scale


def on_device(object_tiles, probe, amplitudes, offsets, counts):
    modes, edge = probe.shape[1], probe.shape[2]
    slot_total = amplitudes.shape[1]
    n_region, n_pos = lax.axis_size("region"), lax.axis_size("pos")
    total = n_region * n_pos
    axes = ("region", "pos")
    f32 = jnp.float32

    row_index, column_index = lax.axis_index("region"), lax.axis_index("pos")

    def shifted(block, down, across):
        route = [
            (i * n_pos + j, (i + down) % n_region * n_pos + (j + across) % n_pos)
            for i in range(n_region)
            for j in range(n_pos)
        ]
        return lax.ppermute(block, axes, route)

    pieces = n_pos // 2

    def partner(block, mask):
        return lax.ppermute(block, axes, [(i, i ^ mask) for i in range(total)])

    place = jnp.stack(
        [
            column_index & 1,
            column_index >> 1,
            (row_index < n_region - 1).astype(jnp.int32),
            (column_index < n_pos - 1).astype(jnp.int32),
            row_index & 1,
        ]
    )

    def swapped(first, across):
        route = []
        for i in range(n_region):
            a = i + 1 if (i - first) % 2 == 0 else i - 1
            for j in range(n_pos):
                if 0 <= a < n_region:
                    target = a * n_pos + (j + across) % n_pos
                else:
                    target = i * n_pos + ((j + across) % n_pos if across else j ^ 1)
                route.append((i * n_pos + j, target))
        return lax.ppermute(object_tiles, axes, route)

    right = shifted(object_tiles, 0, -1)
    halo = (swapped(0, 0), right, swapped(1, -1), swapped(0, -1), swapped(1, 0))

    lines = 2 * modes * edge
    smem = pl.BlockSpec(memory_space=pltpu.SMEM)
    vmem = pl.BlockSpec(memory_space=pltpu.VMEM)
    held = jnp.concatenate(
        [
            amplitudes.reshape(2, -1, edge),
            jnp.asarray(dft_tables(edge)),
        ],
        axis=1,
    )
    quadrant = jax.ShapeDtypeStruct((2, edge, edge), f32)
    part = jax.ShapeDtypeStruct((pieces, lines // n_pos, edge), f32)
    scale = 1.0 / math.sqrt(total * slot_total)
    own_grad, right_grad, lower_grads, keep, send = pl.pallas_call(
        functools.partial(slots_kernel, scale, modes, slot_total, edge),
        out_shape=(quadrant, quadrant, jax.ShapeDtypeStruct((2, 2, edge, edge), f32), part, part),
        in_specs=[pl.BlockSpec(memory_space=pl.ANY)] * 2 + [smem] + [vmem] * 8,
        out_specs=(vmem,) * 5,
        scratch_shapes=[pltpu.VMEM((4, 2 * edge, 2 * edge), jnp.bfloat16)]
        + [pltpu.VMEM((2, 2 * edge, edge), f32)] * 4
        + [
            pltpu.VMEM((2, modes, edge, edge), f32),
            pltpu.SMEM(offsets.shape, jnp.int32),
            pltpu.SMEM(counts.shape, jnp.int32),
            pltpu.SemaphoreType.DMA((2,)),
        ],
        compiler_params=pltpu.CompilerParams(vmem_limit_bytes=16 * 1024 * 1024),
    )(offsets, counts, place, probe, held, object_tiles, *halo)

    half = keep + partner(send, 1)
    above = shifted(lower_grads, 1, 0)
    got = [partner(half[k], 2 * k) for k in range(1, pieces)]
    got[0], above = lax.optimization_barrier((got[0], above))
    chunk = functools.reduce(jnp.add, got, half[0])
    terms = [chunk] + [partner(chunk, n_pos * k) for k in range(1, n_region)]
    left = shifted(right_grad + above[1], 0, 1)
    while len(terms) > 1:
        terms = [terms[k] + terms[k + 1] for k in range(0, len(terms), 2)]
    chunk = terms[0]
    gathered = [chunk] + [partner(chunk, 2 * k) for k in range(1, pieces)]
    gathered[1], left = lax.optimization_barrier((gathered[1], left))
    forwarded = [partner(piece, 1) for piece in gathered]
    object_grad = own_grad + above[0] + left

    def in_order(parts, index):
        while len(parts) > 1:
            swap, index = index % 2 == 1, index // 2
            parts = [
                jnp.where(swap, jnp.concatenate([b, a], axis=0), jnp.concatenate([a, b], axis=0))
                for a, b in zip(parts[::2], parts[1::2])
            ]
            parts = list(lax.optimization_barrier(tuple(parts)))
        return parts[0]

    halves = [in_order(gathered, column_index // 2), in_order(forwarded, column_index // 2)]
    probe_grad = in_order(halves, column_index % 2)
    return (object_grad, probe_grad.reshape(probe.shape))


def solution(mesh):
    return jax.shard_map(
        on_device,
        mesh=mesh,
        in_specs=(
            P(None, "region", "pos"),
            P(),
            P("region", "pos", None, None),
            P("region", None, "pos"),
            P("region", "pos"),
        ),
        out_specs=(P(None, "region", "pos"), P()),
        check_vma=False,
    )
```

```python
import functools
import math

import jax
import jax.numpy as jnp
import numpy as np
from jax import lax
from jax.experimental import pallas as pl
from jax.experimental.pallas import tpu as pltpu
from jax.sharding import PartitionSpec as P


def dft_tables(order):
    index = np.arange(order)
    angle = (index[:, None] * index[None, :] % order) * (2.0 * math.pi / order)
    tables = np.stack([np.cos(angle), np.sin(angle)]) / math.sqrt(order)
    return tables.astype(np.float32)


def split(value):
    high = value.astype(jnp.bfloat16)
    low = (value - high.astype(jnp.float32)).astype(jnp.bfloat16)
    return high, low


def dot(a, b):
    return jnp.dot(a, b, preferred_element_type=jnp.float32)


def times_table(value, table_high, table_low):
    rows = table_high.shape[0]
    sums = []
    for start in range(0, value.shape[0], rows):
        high, low = split(value[start : start + rows])
        both = dot(jnp.concatenate([high, low], axis=0), table_high)
        sums.append(both[:rows] + (both[rows:] + dot(high, table_low)))
    return jnp.concatenate(sums, axis=0)


def table_times(tables, value):
    rows = tables.shape[0] // 2
    sums = []
    for start in range(0, value.shape[1], rows):
        high, low = split(value[:, start : start + rows])
        both = dot(tables, high)
        sums.append(both[:rows] + (both[rows:] + dot(tables[:rows], low)))
    return jnp.concatenate(sums, axis=1)


def slots_kernel(
    scale, modes, slot_total, edge, offsets, counts, place, probes, held, own, below, right, other_diag, diag, other_below,
    own_grad, right_grad, below_grad, diag_grad, keep, send,
    tables, field_left, field_right, grad_left, grad_right, probe_sum, corners, live, semaphores,
):
    scalars = (
        pltpu.make_async_copy(offsets, corners, semaphores.at[0]),
        pltpu.make_async_copy(counts, live, semaphores.at[1]),
    )
    for copy in scalars:
        copy.start()

    def probe(part, mode):
        return probes[part, mode]

    amplitude_rows = 0
    table_rows = amplitude_rows + slot_total * edge // 2
    cos_high, cos_low = split(held[0, pl.ds(table_rows, edge), :])
    sin_high, sin_low = split(held[1, pl.ds(table_rows, edge), :])
    spread_high, spread_low, turn_high, turn_low = (tables.at[k] for k in range(4))
    for spread, turn, cos_part, sin_part in (
        (spread_high, turn_high, cos_high, sin_high),
        (spread_low, turn_low, cos_low, sin_low),
    ):
        for target, upper, lower in ((spread, -sin_part, sin_part), (turn, sin_part, -sin_part)):
            target[:edge, :edge] = cos_part
            target[:edge, edge:] = upper
            target[edge:, :edge] = lower
            target[edge:, edge:] = cos_part
    turn_both = jnp.concatenate([turn_high[...], turn_low[...]], axis=0)
    spread_both = jnp.concatenate([spread_high[...], spread_low[...]], axis=0)
    has_below, has_right, odd_row = place[2] > 0, place[3] > 0, place[4] > 0
    has_diag = jnp.logical_and(has_below, has_right)

    def present(flag, value):
        return jnp.where(flag, value, jnp.zeros_like(value))

    def arrived(flag, first, second):
        return present(flag, jnp.where(odd_row, second[...], first[...]).astype(jnp.float32))

    field_left[:, :edge] = own[...].astype(jnp.float32)
    field_left[:, edge:] = arrived(has_below, below, other_below)
    field_right[:, :edge] = present(has_right, right[...].astype(jnp.float32))
    field_right[:, edge:] = arrived(has_diag, diag, other_diag)
    grad_left[...] = jnp.zeros_like(grad_left)
    grad_right[...] = jnp.zeros_like(grad_right)
    lane = lax.broadcasted_iota(jnp.int32, (edge, edge), 1)
    for copy in scalars:
        copy.wait()
    slots = range(slot_total)
    corner = [(corners[0, 0, slot], corners[0, 1, slot]) for slot in slots]
    in_left = [lane >= col0 for _, col0 in corner]
    crops, halves = [], []
    for slot in slots:
        row0, col0 = corner[slot]
        rows, shift = pl.ds(row0, edge), lax.rem(edge - col0, edge)
        crop_r, crop_i = (
            pltpu.roll(
                jnp.where(in_left[slot], field_left[part, rows, :], field_right[part, rows, :]), shift, 1
            )
            for part in range(2)
        )
        exits = [
            jnp.concatenate(
                [
                    probe(0, m) * crop_r - probe(1, m) * crop_i,
                    probe(0, m) * crop_i + probe(1, m) * crop_r,
                ],
                axis=1,
            )
            for m in range(modes)
        ]
        crops.append((crop_r, crop_i))
        halves.append(times_table(jnp.concatenate(exits, axis=0), spread_high[...], spread_low[...]))
    fars = []
    for half in halves:
        parts = [
            [half[m * edge : (m + 1) * edge, part * edge : (part + 1) * edge] for m in range(modes)]
            for part in range(2)
        ]
        half = jnp.concatenate([jnp.concatenate(part, axis=1) for part in parts], axis=0)
        fars.append(table_times(turn_both, half))
    halves = []
    for slot in slots:
        far = fars[slot]
        squares = far * far
        squares = squares[:edge] + squares[edge:]
        intensity = functools.reduce(
            jnp.add, [squares[:, m * edge : (m + 1) * edge] for m in range(modes)]
        )
        weight = (slot < live[0, 0]).astype(jnp.float32)
        half_slots = slot_total // 2
        amplitude = held[slot // half_slots, pl.ds(amplitude_rows + slot % half_slots * edge, edge), :]
        factor = weight * (1.0 - amplitude * lax.rsqrt(intensity + 1.0))
        factor = jnp.concatenate([factor] * modes, axis=1)
        residual = far * jnp.concatenate([factor, factor], axis=0)
        halves.append(table_times(spread_both, residual))
    backs = []
    for half in halves:
        parts = [
            [half[part * edge : (part + 1) * edge, m * edge : (m + 1) * edge] for part in range(2)]
            for m in range(modes)
        ]
        half = jnp.concatenate([jnp.concatenate(part, axis=1) for part in parts], axis=0)
        backs.append(times_table(half, turn_high[...], turn_low[...]))
    for slot in slots:
        crop_r, crop_i = crops[slot]
        row0, col0 = corner[slot]
        rows = pl.ds(row0, edge)
        object_r = jnp.zeros((edge, edge), jnp.float32)
        object_i = jnp.zeros((edge, edge), jnp.float32)
        for m in range(modes):
            back_r = backs[slot][m * edge : (m + 1) * edge, :edge]
            back_i = backs[slot][m * edge : (m + 1) * edge, edge:]
            object_r += probe(0, m) * back_r + probe(1, m) * back_i
            object_i += probe(0, m) * back_i - probe(1, m) * back_r
            term_r = crop_r * back_r + crop_i * back_i
            term_i = crop_r * back_i - crop_i * back_r
            if slot == 0:
                probe_sum[0, m] = term_r
                probe_sum[1, m] = term_i
            else:
                probe_sum[0, m] += term_r
                probe_sum[1, m] += term_i
        for part, term in enumerate((object_r, object_i)):
            term = pltpu.roll(term, col0, 1)
            grad_left[part, rows, :] += jnp.where(in_left[slot], term, 0.0)
            grad_right[part, rows, :] += jnp.where(in_left[slot], 0.0, term)
    own_grad[...] = grad_left[:, :edge]
    right_grad[...] = present(has_right, grad_right[:, :edge])
    below_grad[...] = present(has_below, grad_left[:, edge:])
    diag_grad[...] = present(has_diag, grad_right[:, edge:])
    flat = probe_sum.reshape(2 * modes * edge, edge)
    pieces, depth = keep.shape[0], keep.shape[1]
    for target, half in ((keep, place[0]), (send, 1 - place[0])):
        for position in range(pieces):
            chunk = half * pieces + jnp.bitwise_xor(place[1], position)
            rows = pl.ds(pl.multiple_of(chunk * depth, depth), depth)
            target[position] = flat[rows, :] * scale


def on_device(object_tiles, probe, amplitudes, offsets, counts):
    modes, edge = probe.shape[1], probe.shape[2]
    slot_total = amplitudes.shape[1]
    n_region, n_pos = lax.axis_size("region"), lax.axis_size("pos")
    total = n_region * n_pos
    axes = ("region", "pos")
    f32 = jnp.float32

    row_index, column_index = lax.axis_index("region"), lax.axis_index("pos")

    def shifted(block, down, across):
        route = [
            (i * n_pos + j, (i + down) % n_region * n_pos + (j + across) % n_pos)
            for i in range(n_region)
            for j in range(n_pos)
        ]
        return lax.ppermute(block, axes, route)

    pieces = n_pos // 2

    def partner(block, mask):
        return lax.ppermute(block, axes, [(i, i ^ mask) for i in range(total)])

    place = jnp.stack(
        [
            column_index & 1,
            column_index >> 1,
            (row_index < n_region - 1).astype(jnp.int32),
            (column_index < n_pos - 1).astype(jnp.int32),
            row_index & 1,
        ]
    )

    def swapped(first, across):
        route = []
        for i in range(n_region):
            a = i + 1 if (i - first) % 2 == 0 else i - 1
            for j in range(n_pos):
                if 0 <= a < n_region:
                    target = a * n_pos + (j + across) % n_pos
                else:
                    target = i * n_pos + ((j + across) % n_pos if across else j ^ 1)
                route.append((i * n_pos + j, target))
        return lax.ppermute(object_tiles, axes, route)

    right = shifted(object_tiles, 0, -1)
    halo = (swapped(0, 0), right, swapped(1, -1), swapped(0, -1), swapped(1, 0))

    lines = 2 * modes * edge
    smem = pl.BlockSpec(memory_space=pltpu.SMEM)
    vmem = pl.BlockSpec(memory_space=pltpu.VMEM)
    held = jnp.concatenate(
        [
            amplitudes.reshape(2, -1, edge),
            jnp.asarray(dft_tables(edge)),
        ],
        axis=1,
    )
    quadrant = jax.ShapeDtypeStruct((2, edge, edge), f32)
    part = jax.ShapeDtypeStruct((pieces, lines // n_pos, edge), f32)
    scale = 1.0 / math.sqrt(total * slot_total)
    own_grad, right_grad, below_grad, diag_grad, keep, send = pl.pallas_call(
        functools.partial(slots_kernel, scale, modes, slot_total, edge),
        out_shape=(quadrant,) * 4 + (part, part),
        in_specs=[pl.BlockSpec(memory_space=pl.ANY)] * 2 + [smem] + [vmem] * 8,
        out_specs=(vmem,) * 6,
        scratch_shapes=[pltpu.VMEM((4, 2 * edge, 2 * edge), jnp.bfloat16)]
        + [pltpu.VMEM((2, 2 * edge, edge), f32)] * 4
        + [
            pltpu.VMEM((2, modes, edge, edge), f32),
            pltpu.SMEM(offsets.shape, jnp.int32),
            pltpu.SMEM(counts.shape, jnp.int32),
            pltpu.SemaphoreType.DMA((2,)),
        ],
        compiler_params=pltpu.CompilerParams(vmem_limit_bytes=16 * 1024 * 1024),
    )(offsets, counts, place, probe, held, object_tiles, *halo)

    half = keep + partner(send, 1)
    right_part = shifted(diag_grad, 1, 0)
    got = [partner(half[k], 2 * k) for k in range(1, pieces)]
    got[0], right_part = lax.optimization_barrier((got[0], right_part))
    left = shifted(right_grad + right_part, 0, 1)
    chunk = functools.reduce(jnp.add, got, half[0])
    chunk, below_grad = lax.optimization_barrier((chunk, below_grad))
    above = shifted(below_grad, 1, 0)
    terms = [chunk] + [partner(chunk, n_pos * k) for k in range(1, n_region)]
    while len(terms) > 1:
        terms = [terms[k] + terms[k + 1] for k in range(0, len(terms), 2)]
    chunk = terms[0]
    gathered = [chunk] + [partner(chunk, 2 * k) for k in range(1, pieces)]
    gathered[1], left, above = lax.optimization_barrier((gathered[1], left, above))
    forwarded = [partner(piece, 1) for piece in gathered]
    object_grad = own_grad + above + left

    def in_order(parts, index):
        while len(parts) > 1:
            swap, index = index % 2 == 1, index // 2
            parts = [
                jnp.where(swap, jnp.concatenate([b, a], axis=0), jnp.concatenate([a, b], axis=0))
                for a, b in zip(parts[::2], parts[1::2])
            ]
            parts = list(lax.optimization_barrier(tuple(parts)))
        return parts[0]

    halves = [in_order(gathered, column_index // 2), in_order(forwarded, column_index // 2)]
    probe_grad = in_order(halves, column_index % 2)
    return (object_grad, probe_grad.reshape(probe.shape))


def solution(mesh):
    return jax.shard_map(
        on_device,
        mesh=mesh,
        in_specs=(
            P(None, "region", "pos"),
            P(),
            P("region", "pos", None, None),
            P("region", None, "pos"),
            P("region", "pos"),
        ),
        out_specs=(P(None, "region", "pos"), P()),
        check_vma=False,
    )
```

```python
import functools
import math

import jax
import jax.numpy as jnp
import numpy as np
from jax import lax
from jax.experimental import pallas as pl
from jax.experimental.pallas import tpu as pltpu
from jax.sharding import PartitionSpec as P


def dft_tables(order):
    index = np.arange(order)
    angle = (index[:, None] * index[None, :] % order) * (2.0 * math.pi / order)
    tables = np.stack([np.cos(angle), np.sin(angle)]) / math.sqrt(order)
    return tables.astype(np.float32)


def split(value):
    high = value.astype(jnp.bfloat16)
    low = (value - high.astype(jnp.float32)).astype(jnp.bfloat16)
    return high, low


def dot(a, b):
    return jnp.dot(a, b, preferred_element_type=jnp.float32)


def times_table(value, table_high, table_low):
    rows = table_high.shape[0]
    sums = []
    for start in range(0, value.shape[0], rows):
        high, low = split(value[start : start + rows])
        both = dot(jnp.concatenate([high, low], axis=0), table_high)
        sums.append(both[:rows] + (both[rows:] + dot(high, table_low)))
    return jnp.concatenate(sums, axis=0)


def table_times(tables, value):
    rows = tables.shape[0] // 2
    sums = []
    for start in range(0, value.shape[1], rows):
        high, low = split(value[:, start : start + rows])
        both = dot(tables, high)
        sums.append(both[:rows] + (both[rows:] + dot(tables[:rows], low)))
    return jnp.concatenate(sums, axis=1)


def slots_kernel(
    scale, modes, slot_total, edge, offsets, counts, place, probes, held, own, below, right, other_diag, diag, other_below,
    own_grad, right_grad, lower_grads, keep, send,
    tables, field_left, field_right, grad_left, grad_right, probe_sum, corners, live, semaphores,
):
    scalars = (
        pltpu.make_async_copy(offsets, corners, semaphores.at[0]),
        pltpu.make_async_copy(counts, live, semaphores.at[1]),
    )
    for copy in scalars:
        copy.start()

    def probe(part, mode):
        return probes[part, mode]

    amplitude_rows = 0
    table_rows = amplitude_rows + slot_total * edge // 2
    cos_high, cos_low = split(held[0, pl.ds(table_rows, edge), :])
    sin_high, sin_low = split(held[1, pl.ds(table_rows, edge), :])
    spread_high, spread_low, turn_high, turn_low = (tables.at[k] for k in range(4))
    for spread, turn, cos_part, sin_part in (
        (spread_high, turn_high, cos_high, sin_high),
        (spread_low, turn_low, cos_low, sin_low),
    ):
        for target, upper, lower in ((spread, -sin_part, sin_part), (turn, sin_part, -sin_part)):
            target[:edge, :edge] = cos_part
            target[:edge, edge:] = upper
            target[edge:, :edge] = lower
            target[edge:, edge:] = cos_part
    turn_both = jnp.concatenate([turn_high[...], turn_low[...]], axis=0)
    spread_both = jnp.concatenate([spread_high[...], spread_low[...]], axis=0)
    has_below, has_right, odd_row = place[2] > 0, place[3] > 0, place[4] > 0
    has_diag = jnp.logical_and(has_below, has_right)

    def present(flag, value):
        return jnp.where(flag, value, jnp.zeros_like(value))

    def arrived(flag, first, second):
        return present(flag, jnp.where(odd_row, second[...], first[...]).astype(jnp.float32))

    field_left[:, :edge] = own[...].astype(jnp.float32)
    field_left[:, edge:] = arrived(has_below, below, other_below)
    field_right[:, :edge] = present(has_right, right[...].astype(jnp.float32))
    field_right[:, edge:] = arrived(has_diag, diag, other_diag)
    grad_left[...] = jnp.zeros_like(grad_left)
    grad_right[...] = jnp.zeros_like(grad_right)
    lane = lax.broadcasted_iota(jnp.int32, (edge, edge), 1)
    for copy in scalars:
        copy.wait()
    slots = range(slot_total)
    corner = [(corners[0, 0, slot], corners[0, 1, slot]) for slot in slots]
    in_left = [lane >= col0 for _, col0 in corner]
    crops, halves = [], []
    for slot in slots:
        row0, col0 = corner[slot]
        rows, shift = pl.ds(row0, edge), lax.rem(edge - col0, edge)
        crop_r, crop_i = (
            pltpu.roll(
                jnp.where(in_left[slot], field_left[part, rows, :], field_right[part, rows, :]), shift, 1
            )
            for part in range(2)
        )
        exits = [
            jnp.concatenate(
                [
                    probe(0, m) * crop_r - probe(1, m) * crop_i,
                    probe(0, m) * crop_i + probe(1, m) * crop_r,
                ],
                axis=1,
            )
            for m in range(modes)
        ]
        crops.append((crop_r, crop_i))
        halves.append(times_table(jnp.concatenate(exits, axis=0), spread_high[...], spread_low[...]))
    fars = []
    for half in halves:
        parts = [
            [half[m * edge : (m + 1) * edge, part * edge : (part + 1) * edge] for m in range(modes)]
            for part in range(2)
        ]
        half = jnp.concatenate([jnp.concatenate(part, axis=1) for part in parts], axis=0)
        fars.append(table_times(turn_both, half))
    halves = []
    for slot in slots:
        far = fars[slot]
        squares = far * far
        squares = squares[:edge] + squares[edge:]
        intensity = functools.reduce(
            jnp.add, [squares[:, m * edge : (m + 1) * edge] for m in range(modes)]
        )
        weight = (slot < live[0, 0]).astype(jnp.float32)
        half_slots = slot_total // 2
        amplitude = held[slot // half_slots, pl.ds(amplitude_rows + slot % half_slots * edge, edge), :]
        factor = weight * (1.0 - amplitude * lax.rsqrt(intensity + 1.0))
        factor = jnp.concatenate([factor] * modes, axis=1)
        residual = far * jnp.concatenate([factor, factor], axis=0)
        halves.append(table_times(spread_both, residual))
    backs = []
    for half in halves:
        parts = [
            [half[part * edge : (part + 1) * edge, m * edge : (m + 1) * edge] for part in range(2)]
            for m in range(modes)
        ]
        half = jnp.concatenate([jnp.concatenate(part, axis=1) for part in parts], axis=0)
        backs.append(times_table(half, turn_high[...], turn_low[...]))
    for slot in slots:
        crop_r, crop_i = crops[slot]
        row0, col0 = corner[slot]
        rows = pl.ds(row0, edge)
        object_r = jnp.zeros((edge, edge), jnp.float32)
        object_i = jnp.zeros((edge, edge), jnp.float32)
        for m in range(modes):
            back_r = backs[slot][m * edge : (m + 1) * edge, :edge]
            back_i = backs[slot][m * edge : (m + 1) * edge, edge:]
            object_r += probe(0, m) * back_r + probe(1, m) * back_i
            object_i += probe(0, m) * back_i - probe(1, m) * back_r
            term_r = crop_r * back_r + crop_i * back_i
            term_i = crop_r * back_i - crop_i * back_r
            if slot == 0:
                probe_sum[0, m] = term_r
                probe_sum[1, m] = term_i
            else:
                probe_sum[0, m] += term_r
                probe_sum[1, m] += term_i
        for part, term in enumerate((object_r, object_i)):
            term = pltpu.roll(term, col0, 1)
            grad_left[part, rows, :] += jnp.where(in_left[slot], term, 0.0)
            grad_right[part, rows, :] += jnp.where(in_left[slot], 0.0, term)
    own_grad[...] = grad_left[:, :edge]
    right_grad[...] = present(has_right, grad_right[:, :edge])
    lower_grads[0] = present(has_below, grad_left[:, edge:])
    lower_grads[1] = present(has_diag, grad_right[:, edge:])
    flat = probe_sum.reshape(2 * modes * edge, edge)
    pieces, depth = keep.shape[0], keep.shape[1]
    for target, half in ((keep, place[0]), (send, 1 - place[0])):
        for position in range(pieces):
            chunk = half * pieces + jnp.bitwise_xor(place[1], position)
            rows = pl.ds(pl.multiple_of(chunk * depth, depth), depth)
            target[position] = flat[rows, :] * scale


def on_device(object_tiles, probe, amplitudes, offsets, counts):
    modes, edge = probe.shape[1], probe.shape[2]
    slot_total = amplitudes.shape[1]
    n_region, n_pos = lax.axis_size("region"), lax.axis_size("pos")
    total = n_region * n_pos
    axes = ("region", "pos")
    f32 = jnp.float32

    row_index, column_index = lax.axis_index("region"), lax.axis_index("pos")

    def shifted(block, down, across):
        route = [
            (i * n_pos + j, (i + down) % n_region * n_pos + (j + across) % n_pos)
            for i in range(n_region)
            for j in range(n_pos)
        ]
        return lax.ppermute(block, axes, route)

    pieces = n_pos // 2

    def partner(block, mask):
        return lax.ppermute(block, axes, [(i, i ^ mask) for i in range(total)])

    place = jnp.stack(
        [
            column_index & 1,
            column_index >> 1,
            (row_index < n_region - 1).astype(jnp.int32),
            (column_index < n_pos - 1).astype(jnp.int32),
            row_index & 1,
        ]
    )

    def swapped(first, across):
        route = []
        for i in range(n_region):
            a = i + 1 if (i - first) % 2 == 0 else i - 1
            for j in range(n_pos):
                if 0 <= a < n_region:
                    target = a * n_pos + (j + across) % n_pos
                else:
                    target = i * n_pos + ((j + across) % n_pos if across else j ^ 1)
                route.append((i * n_pos + j, target))
        return lax.ppermute(object_tiles, axes, route)

    right = shifted(object_tiles, 0, -1)
    halo = (swapped(0, 0), right, swapped(1, -1), swapped(0, -1), swapped(1, 0))

    lines = 2 * modes * edge
    smem = pl.BlockSpec(memory_space=pltpu.SMEM)
    vmem = pl.BlockSpec(memory_space=pltpu.VMEM)
    held = jnp.concatenate(
        [
            amplitudes.reshape(2, -1, edge),
            jnp.asarray(dft_tables(edge)),
        ],
        axis=1,
    )
    quadrant = jax.ShapeDtypeStruct((2, edge, edge), f32)
    part = jax.ShapeDtypeStruct((pieces, lines // n_pos, edge), f32)
    scale = 1.0 / math.sqrt(total * slot_total)
    own_grad, right_grad, lower_grads, keep, send = pl.pallas_call(
        functools.partial(slots_kernel, scale, modes, slot_total, edge),
        out_shape=(quadrant, quadrant, jax.ShapeDtypeStruct((2, 2, edge, edge), f32), part, part),
        in_specs=[pl.BlockSpec(memory_space=pl.ANY)] * 2 + [smem] + [vmem] * 8,
        out_specs=(vmem,) * 5,
        scratch_shapes=[pltpu.VMEM((4, 2 * edge, 2 * edge), jnp.bfloat16)]
        + [pltpu.VMEM((2, 2 * edge, edge), f32)] * 4
        + [
            pltpu.VMEM((2, modes, edge, edge), f32),
            pltpu.SMEM(offsets.shape, jnp.int32),
            pltpu.SMEM(counts.shape, jnp.int32),
            pltpu.SemaphoreType.DMA((2,)),
        ],
        compiler_params=pltpu.CompilerParams(vmem_limit_bytes=16 * 1024 * 1024),
    )(offsets, counts, place, probe, held, object_tiles, *halo)

    half = keep + partner(send, 1)
    above = shifted(lower_grads, 1, 0)
    got = [partner(half[k], 2 * k) for k in range(1, pieces)]
    got[-1], above = lax.optimization_barrier((got[-1], above))
    chunk = functools.reduce(jnp.add, got, half[0])
    terms = [partner(chunk, n_pos * k) for k in range(n_region - 1, 0, -1)] + [chunk]
    left = shifted(right_grad + above[1], 0, 1)
    while len(terms) > 1:
        terms = [terms[k] + terms[k + 1] for k in range(0, len(terms), 2)]
    chunk = terms[0]
    gathered = [chunk] + [partner(chunk, 2 * k) for k in range(1, pieces)]
    gathered[-1], left = lax.optimization_barrier((gathered[-1], left))
    forwarded = [partner(piece, 1) for piece in gathered]
    object_grad = own_grad + above[0] + left

    def in_order(parts, index):
        while len(parts) > 1:
            swap, index = index % 2 == 1, index // 2
            parts = [
                jnp.where(swap, jnp.concatenate([b, a], axis=0), jnp.concatenate([a, b], axis=0))
                for a, b in zip(parts[::2], parts[1::2])
            ]
            parts = list(lax.optimization_barrier(tuple(parts)))
        return parts[0]

    halves = [in_order(gathered, column_index // 2), in_order(forwarded, column_index // 2)]
    probe_grad = in_order(halves, column_index % 2)
    return (object_grad, probe_grad.reshape(probe.shape))


def solution(mesh):
    return jax.shard_map(
        on_device,
        mesh=mesh,
        in_specs=(
            P(None, "region", "pos"),
            P(),
            P("region", "pos", None, None),
            P("region", None, "pos"),
            P("region", "pos"),
        ),
        out_specs=(P(None, "region", "pos"), P()),
        check_vma=False,
    )
```

```python
import functools
import math

import jax
import jax.numpy as jnp
import numpy as np
from jax import lax
from jax.experimental import pallas as pl
from jax.experimental.pallas import tpu as pltpu
from jax.sharding import PartitionSpec as P


def dft_tables(order):
    index = np.arange(order)
    angle = (index[:, None] * index[None, :] % order) * (2.0 * math.pi / order)
    tables = np.stack([np.cos(angle), np.sin(angle)]) / math.sqrt(order)
    return tables.astype(np.float32)


def split(value):
    high = value.astype(jnp.bfloat16)
    low = (value - high.astype(jnp.float32)).astype(jnp.bfloat16)
    return high, low


def dot(a, b):
    return jnp.dot(a, b, preferred_element_type=jnp.float32)


def times_table(value, table_high, table_low):
    rows = table_high.shape[0]
    sums = []
    for start in range(0, value.shape[0], rows):
        high, low = split(value[start : start + rows])
        both = dot(jnp.concatenate([high, low], axis=0), table_high)
        sums.append(both[:rows] + (both[rows:] + dot(high, table_low)))
    return jnp.concatenate(sums, axis=0)


def table_times(tables, value):
    rows = tables.shape[0] // 2
    sums = []
    for start in range(0, value.shape[1], rows):
        high, low = split(value[:, start : start + rows])
        both = dot(tables, high)
        sums.append(both[:rows] + (both[rows:] + dot(tables[:rows], low)))
    return jnp.concatenate(sums, axis=1)


def slots_kernel(
    scale, modes, slot_total, edge, offsets, counts, place, probes, held, own, below, right, other_diag, diag, other_below,
    own_grad, right_grad, lower_grads, keep, send,
    tables, field_left, field_right, grad_left, grad_right, probe_sum, corners, live, semaphores,
):
    scalars = (
        pltpu.make_async_copy(offsets, corners, semaphores.at[0]),
        pltpu.make_async_copy(counts, live, semaphores.at[1]),
    )
    for copy in scalars:
        copy.start()

    def probe(part, mode):
        return probes[part, mode]

    amplitude_rows = 0
    table_rows = amplitude_rows + slot_total * edge // 2
    cos_high, cos_low = split(held[0, pl.ds(table_rows, edge), :])
    sin_high, sin_low = split(held[1, pl.ds(table_rows, edge), :])
    spread_high, spread_low, turn_high, turn_low = (tables.at[k] for k in range(4))
    for spread, turn, cos_part, sin_part in (
        (spread_high, turn_high, cos_high, sin_high),
        (spread_low, turn_low, cos_low, sin_low),
    ):
        for target, upper, lower in ((spread, -sin_part, sin_part), (turn, sin_part, -sin_part)):
            target[:edge, :edge] = cos_part
            target[:edge, edge:] = upper
            target[edge:, :edge] = lower
            target[edge:, edge:] = cos_part
    turn_both = jnp.concatenate([turn_high[...], turn_low[...]], axis=0)
    spread_both = jnp.concatenate([spread_high[...], spread_low[...]], axis=0)
    has_below, has_right, odd_row = place[2] > 0, place[3] > 0, place[4] > 0
    has_diag = jnp.logical_and(has_below, has_right)

    def present(flag, value):
        return jnp.where(flag, value, jnp.zeros_like(value))

    def arrived(flag, first, second):
        return present(flag, jnp.where(odd_row, second[...], first[...]).astype(jnp.float32))

    field_left[:, :edge] = own[...].astype(jnp.float32)
    field_left[:, edge:] = arrived(has_below, below, other_below)
    field_right[:, :edge] = present(has_right, right[...].astype(jnp.float32))
    field_right[:, edge:] = arrived(has_diag, diag, other_diag)
    grad_left[...] = jnp.zeros_like(grad_left)
    grad_right[...] = jnp.zeros_like(grad_right)
    lane = lax.broadcasted_iota(jnp.int32, (edge, edge), 1)
    for copy in scalars:
        copy.wait()
    slots = range(slot_total)
    corner = [(corners[0, 0, slot], corners[0, 1, slot]) for slot in slots]
    in_left = [lane >= col0 for _, col0 in corner]
    crops, halves = [], []
    for slot in slots:
        row0, col0 = corner[slot]
        rows, shift = pl.ds(row0, edge), lax.rem(edge - col0, edge)
        crop_r, crop_i = (
            pltpu.roll(
                jnp.where(in_left[slot], field_left[part, rows, :], field_right[part, rows, :]), shift, 1
            )
            for part in range(2)
        )
        exits = [
            jnp.concatenate(
                [
                    probe(0, m) * crop_r - probe(1, m) * crop_i,
                    probe(0, m) * crop_i + probe(1, m) * crop_r,
                ],
                axis=1,
            )
            for m in range(modes)
        ]
        crops.append((crop_r, crop_i))
        halves.append(times_table(jnp.concatenate(exits, axis=0), spread_high[...], spread_low[...]))
    fars = []
    for half in halves:
        parts = [
            [half[m * edge : (m + 1) * edge, part * edge : (part + 1) * edge] for m in range(modes)]
            for part in range(2)
        ]
        half = jnp.concatenate([jnp.concatenate(part, axis=1) for part in parts], axis=0)
        fars.append(table_times(turn_both, half))
    halves = []
    for slot in slots:
        far = fars[slot]
        squares = far * far
        squares = squares[:edge] + squares[edge:]
        intensity = functools.reduce(
            jnp.add, [squares[:, m * edge : (m + 1) * edge] for m in range(modes)]
        )
        weight = (slot < live[0, 0]).astype(jnp.float32)
        half_slots = slot_total // 2
        amplitude = held[slot // half_slots, pl.ds(amplitude_rows + slot % half_slots * edge, edge), :]
        factor = weight * (1.0 - amplitude * lax.rsqrt(intensity + 1.0))
        factor = jnp.concatenate([factor] * modes, axis=1)
        residual = far * jnp.concatenate([factor, factor], axis=0)
        halves.append(table_times(spread_both, residual))
    backs = []
    for half in halves:
        parts = [
            [half[part * edge : (part + 1) * edge, m * edge : (m + 1) * edge] for part in range(2)]
            for m in range(modes)
        ]
        half = jnp.concatenate([jnp.concatenate(part, axis=1) for part in parts], axis=0)
        backs.append(times_table(half, turn_high[...], turn_low[...]))
    for slot in slots:
        crop_r, crop_i = crops[slot]
        row0, col0 = corner[slot]
        rows = pl.ds(row0, edge)
        object_r = jnp.zeros((edge, edge), jnp.float32)
        object_i = jnp.zeros((edge, edge), jnp.float32)
        for m in range(modes):
            back_r = backs[slot][m * edge : (m + 1) * edge, :edge]
            back_i = backs[slot][m * edge : (m + 1) * edge, edge:]
            object_r += probe(0, m) * back_r + probe(1, m) * back_i
            object_i += probe(0, m) * back_i - probe(1, m) * back_r
            term_r = crop_r * back_r + crop_i * back_i
            term_i = crop_r * back_i - crop_i * back_r
            if slot == 0:
                probe_sum[0, m] = term_r
                probe_sum[1, m] = term_i
            else:
                probe_sum[0, m] += term_r
                probe_sum[1, m] += term_i
        for part, term in enumerate((object_r, object_i)):
            term = pltpu.roll(term, col0, 1)
            grad_left[part, rows, :] += jnp.where(in_left[slot], term, 0.0)
            grad_right[part, rows, :] += jnp.where(in_left[slot], 0.0, term)
    own_grad[...] = grad_left[:, :edge]
    right_grad[...] = present(has_right, grad_right[:, :edge])
    lower_grads[0] = present(has_below, grad_left[:, edge:])
    lower_grads[1] = present(has_diag, grad_right[:, edge:])
    flat = probe_sum.reshape(2 * modes * edge, edge)
    pieces, depth = keep.shape[0], keep.shape[1]
    for target, half in ((keep, place[0]), (send, 1 - place[0])):
        for position in range(pieces):
            chunk = half * pieces + jnp.bitwise_xor(place[1], position)
            rows = pl.ds(pl.multiple_of(chunk * depth, depth), depth)
            target[position] = flat[rows, :] * scale


def on_device(object_tiles, probe, amplitudes, offsets, counts):
    modes, edge = probe.shape[1], probe.shape[2]
    slot_total = amplitudes.shape[1]
    n_region, n_pos = lax.axis_size("region"), lax.axis_size("pos")
    total = n_region * n_pos
    axes = ("region", "pos")
    f32 = jnp.float32

    row_index, column_index = lax.axis_index("region"), lax.axis_index("pos")

    def shifted(block, down, across):
        route = [
            (i * n_pos + j, (i + down) % n_region * n_pos + (j + across) % n_pos)
            for i in range(n_region)
            for j in range(n_pos)
        ]
        return lax.ppermute(block, axes, route)

    pieces = n_pos // 2

    def partner(block, mask):
        return lax.ppermute(block, axes, [(i, i ^ mask) for i in range(total)])

    place = jnp.stack(
        [
            column_index & 1,
            column_index >> 1,
            (row_index < n_region - 1).astype(jnp.int32),
            (column_index < n_pos - 1).astype(jnp.int32),
            row_index & 1,
        ]
    )

    def swapped(first, across):
        route = []
        for i in range(n_region):
            a = i + 1 if (i - first) % 2 == 0 else i - 1
            for j in range(n_pos):
                if 0 <= a < n_region:
                    target = a * n_pos + (j + across) % n_pos
                else:
                    target = i * n_pos + ((j + across) % n_pos if across else j ^ 1)
                route.append((i * n_pos + j, target))
        return lax.ppermute(object_tiles, axes, route)

    right = shifted(object_tiles, 0, -1)
    halo = (swapped(0, 0), right, swapped(1, -1), swapped(0, -1), swapped(1, 0))

    lines = 2 * modes * edge
    smem = pl.BlockSpec(memory_space=pltpu.SMEM)
    vmem = pl.BlockSpec(memory_space=pltpu.VMEM)
    held = jnp.concatenate(
        [
            amplitudes.reshape(2, -1, edge),
            jnp.asarray(dft_tables(edge)),
        ],
        axis=1,
    )
    quadrant = jax.ShapeDtypeStruct((2, edge, edge), f32)
    part = jax.ShapeDtypeStruct((pieces, lines // n_pos, edge), f32)
    scale = 1.0 / math.sqrt(total * slot_total)
    own_grad, right_grad, lower_grads, keep, send = pl.pallas_call(
        functools.partial(slots_kernel, scale, modes, slot_total, edge),
        out_shape=(quadrant, quadrant, jax.ShapeDtypeStruct((2, 2, edge, edge), f32), part, part),
        in_specs=[pl.BlockSpec(memory_space=pl.ANY)] * 2 + [smem] + [vmem] * 8,
        out_specs=(vmem,) * 5,
        scratch_shapes=[pltpu.VMEM((4, 2 * edge, 2 * edge), jnp.bfloat16)]
        + [pltpu.VMEM((2, 2 * edge, edge), f32)] * 4
        + [
            pltpu.VMEM((2, modes, edge, edge), f32),
            pltpu.SMEM(offsets.shape, jnp.int32),
            pltpu.SMEM(counts.shape, jnp.int32),
            pltpu.SemaphoreType.DMA((2,)),
        ],
        compiler_params=pltpu.CompilerParams(vmem_limit_bytes=16 * 1024 * 1024),
    )(offsets, counts, place, probe, held, object_tiles, *halo)

    half = keep + partner(send, 1)
    above = shifted(lower_grads, 1, 0)
    got = [partner(half[k], 2 * k) for k in range(1, pieces)]
    got[-1], above = lax.optimization_barrier((got[-1], above))
    chunk = functools.reduce(jnp.add, got, half[0])
    terms = [chunk] + [partner(chunk, n_pos * k) for k in range(1, n_region)]
    left = shifted(right_grad + above[1], 0, 1)
    while len(terms) > 1:
        terms = [terms[k] + terms[k + 1] for k in range(0, len(terms), 2)]
    chunk = terms[0]
    gathered = [chunk] + [partner(chunk, 2 * k) for k in range(1, pieces)]
    gathered[-1], left = lax.optimization_barrier((gathered[-1], left))
    forwarded = [partner(piece, 1) for piece in gathered]
    object_grad = own_grad + above[0] + left

    def in_order(parts, index):
        while len(parts) > 1:
            swap, index = index % 2 == 1, index // 2
            parts = [
                jnp.where(swap, jnp.concatenate([b, a], axis=0), jnp.concatenate([a, b], axis=0))
                for a, b in zip(parts[::2], parts[1::2])
            ]
            parts = list(lax.optimization_barrier(tuple(parts)))
        return parts[0]

    halves = [in_order(gathered, column_index // 2), in_order(forwarded, column_index // 2)]
    probe_grad = in_order(halves, column_index % 2)
    return (object_grad, probe_grad.reshape(probe.shape))


def solution(mesh):
    return jax.shard_map(
        on_device,
        mesh=mesh,
        in_specs=(
            P(None, "region", "pos"),
            P(),
            P("region", "pos", None, None),
            P("region", None, "pos"),
            P("region", "pos"),
        ),
        out_specs=(P(None, "region", "pos"), P()),
        check_vma=False,
    )
```
